32 devices in a mesh: batch: 8 (over y, x, core), seq: 4 (over z).
Axes of the slice: x: 2, y: 2, z: 4, core: 2. Of those that a mesh axis runs over, the one named last changes fastest.
Arguments:
- hidden: bfloat16 [32, 512, 768], P('batch', 'seq'), may hold values from -6 to 6
- groups: int32 [32, 512], P('batch'), may hold values from 0 to 7, never falling along the last dimension, each value on 1 to 128 neighbouring positions
- answer_flags: int32 [32, 512], P('batch', 'seq'), may hold values 0 or 1
- lengths: int32 [32], P('batch'), may hold values from 256 to 512, as said below
- answer_embed: bfloat16 [2, 768], replicated, may hold values from -3 to 3
- query_weight: bfloat16 [768, 768], replicated, may hold values from -0.21875 to 0.21875
- query_bias: bfloat16 [768], replicated, may hold values from -3 to 3
- key_weight: bfloat16 [768, 768], replicated, may hold values from -0.21875 to 0.21875
- value_weight: bfloat16 [768, 768], replicated, may hold values from -0.21875 to 0.21875
- value_bias: bfloat16 [768], replicated, may hold values from -3 to 3
- output_weight: bfloat16 [768, 768], replicated, may hold values from -1.75 to 1.75
- output_bias: bfloat16 [768], replicated, may hold values from -2 to 2
- first_gain: bfloat16 [768], replicated, may hold values from 0.099609375 to 1.8984375
- first_shift: bfloat16 [768], replicated, may hold values from -2 to 2
- inner_weight: bfloat16 [768, 3072], replicated, may hold values from -0.21875 to 0.21875
- inner_bias: bfloat16 [3072], replicated, may hold values from -3 to 3
- outer_weight: bfloat16 [3072, 768], replicated, may hold values from -0.109375 to 0.109375
- outer_bias: bfloat16 [768], replicated, may hold values from -2 to 2
- second_gain: bfloat16 [768], replicated, may hold values from 0.099609375 to 1.8984375
- second_shift: bfloat16 [768], replicated, may hold values from -2 to 2
- cotangent: bfloat16 [32, 512, 768], P('batch', 'seq'), may hold values from -6 to 6
Outputs:
- output: bfloat16 [32, 512, 768], P('batch', 'seq')
- input_gradient: bfloat16 [32, 512, 768], P('batch', 'seq')
- answer_embed_gradient: float32 [2, 768], P(None, ('batch', 'seq'))
- query_weight_gradient: float32 [768, 768], P(('batch', 'seq'))
- query_bias_gradient: float32 [768], P(('batch', 'seq'))
- key_weight_gradient: float32 [768, 768], P(('batch', 'seq'))
- value_weight_gradient: float32 [768, 768], P(('batch', 'seq'))
- value_bias_gradient: float32 [768], P(('batch', 'seq'))
- output_weight_gradient: float32 [768, 768], P(('batch', 'seq'))
- output_bias_gradient: float32 [768], P(('batch', 'seq'))
- first_gain_gradient: float32 [768], P(('batch', 'seq'))
- first_shift_gradient: float32 [768], P(('batch', 'seq'))
- inner_weight_gradient: float32 [768, 3072], P(('batch', 'seq'))
- inner_bias_gradient: float32 [3072], P(('batch', 'seq'))
- outer_weight_gradient: float32 [3072, 768], P(('batch', 'seq'))
- outer_bias_gradient: float32 [768], P(('batch', 'seq'))
- second_gain_gradient: float32 [768], P(('batch', 'seq'))
- second_shift_gradient: float32 [768], P(('batch', 'seq'))
The draws below stay inside these ranges and needn't reach their ends.
Inputs may be any that keep to these rules, and one draw needn't show every extreme that they name: `lengths`: in every aligned block of 2 items one item has length 512. `groups`: never falling along an item, starting at 0.
All inputs are finite; a program needn't handle non-finite values. No bound on the sum of `answer_flags` on one device may be relied on, other than what follows from the above.
Results may differ from the reference program's by a relative error of at most 0.018.
Values may be sent and summed in bfloat16 or wider, within the bound.
No kernel may reach another device: no remote copies, remote signals or barrier semaphores. Data moves between devices by JAX's collectives and lax.ppermute only.
A program may use at most 256 MiB of HBM per device.

```python
import math
import jax
import jax.numpy as jnp
import numpy as np
from jax import lax

D = 768
HEAD_DIM = 64
FF = 3072
LENGTH = 512
ITEMS_DEV = 2
ITEMS = 32


def draw_lengths(key, part):
    key = jax.random.fold_in(key, 11)
    base = jax.random.randint(key, (ITEMS,), LENGTH // 2, LENGTH + 1)
    chosen = jax.random.randint(jax.random.fold_in(key, 5), (ITEMS // ITEMS_DEV,), 0, ITEMS_DEV)
    place = jnp.arange(ITEMS, dtype=jnp.int32)
    full = place % ITEMS_DEV == jnp.repeat(chosen, ITEMS_DEV, total_repeat_length=ITEMS)
    return jnp.where(full, LENGTH, base).astype(jnp.int32)


def plant(drawn, key, low, high):
    shape = drawn.shape
    spot = [jax.random.randint(jax.random.fold_in(key, axis), (), 0, shape[axis]) for axis in range(len(shape))]
    drawn = drawn.at[tuple(spot)].set(low)
    longest = shape.index(max(shape))
    spot[longest] = (spot[longest] + 1) % shape[longest]
    return drawn.at[tuple(spot)].set(high)


def block_scale(key, shape, shards, least, largest):
    loudness, own = 1.0, jax.random.fold_in(key, 6)
    for axis_at, shards_of in shards:
        heights = jnp.exp(jax.random.uniform(jax.random.fold_in(own, axis_at), (shards_of,), jnp.float32, least / len(shards), largest / len(shards)))
        loudness = loudness * jnp.repeat(heights, shape[axis_at] // shards_of).reshape([-1 if axis == axis_at else 1 for axis in range(len(shape))])
    return loudness


def split_up(amount, total, reach, slope):
    weights = [(1 << 20) // math.isqrt(standing ** slope) + 1 for standing in range(2, amount + 1)]
    spare, counts = total - reach - (amount - 1), [1] * (amount - 1)
    while spare > 0:
        free = [i for i in range(amount - 1) if counts[i] < reach]
        pool, budget = sum([weights[i] for i in free]), spare
        for i in free:
            addition = min(reach - counts[i], max(1, budget * weights[i] // pool), spare)
            counts[i] = counts[i] + addition
            spare = spare - addition
    return np.array([reach] + counts)


def uneven(own_key, count, total, reach, skew):
    if count == 2:
        one = jax.random.randint(own_key, (), max(1, total - reach), min(reach, total - 1) + 1)
        return jnp.stack([one, total - one])
    tallies = jnp.asarray(split_up(count, total, reach, skew), jnp.int32)
    twos = (count - 1) // 2
    source_of, receiver = tallies[1:1 + 2 * twos:2], tallies[2:2 + 2 * twos:2]
    room = jnp.minimum(source_of - 1, reach - receiver)
    passed = jax.random.randint(jax.random.fold_in(own_key, 1), (twos,), 0, 1 << 20) % (room + 1)
    tallies = tallies.at[1:1 + 2 * twos:2].set(source_of - passed).at[2:2 + 2 * twos:2].set(receiver + passed)
    return tallies[jax.random.permutation(jax.random.fold_in(own_key, 2), count)]


def scatter_about(own_key, shape, scale, reach, pieces=(), held_as=jnp.bfloat16):
    drawn = scale * jax.random.normal(own_key, shape, jnp.float32)
    if pieces:
        drawn = drawn * block_scale(own_key, shape, pieces, -0.22, 0.18)
    return jnp.clip(drawn, -reach, reach).astype(held_as)


def setup_inputs(seed: int = 0) -> dict:
    key_of = jax.random.split(jax.random.key(seed), 22)
    hidden = scatter_about(key_of[0], (ITEMS, LENGTH, D), 1.0, 6.0, ((0, 8), (1, 4)))
    groups = jax.vmap(lambda own: jnp.searchsorted(jnp.cumsum(uneven(own, 8, LENGTH, LENGTH // 4, 0)), jnp.arange(LENGTH), side="right"))(jax.random.split(key_of[1], ITEMS)).reshape((ITEMS, LENGTH)).astype(jnp.int32)
    answer_flags = plant((jax.random.randint(key_of[2], (ITEMS, LENGTH), 0, 4) < 1).astype(jnp.int32), jax.random.fold_in(key_of[2], 1), 0, 1)
    lengths = draw_lengths(jax.random.fold_in(key_of[21], 71), 0)
    answer_embed = scatter_about(key_of[4], (2, D), 0.5, 3.0)
    query_weight = scatter_about(key_of[5], (D, D), D ** -0.5, 0.21875)
    query_bias = scatter_about(key_of[6], (D,), 0.5, 3.0)
    key_weight = scatter_about(key_of[7], (D, D), D ** -0.5, 0.21875)
    value_weight = scatter_about(key_of[8], (D, D), D ** -0.5, 0.21875)
    value_bias = scatter_about(key_of[9], (D,), 0.5, 3.0)
    output_weight = scatter_about(key_of[10], (D, D), (D * 8 // LENGTH) ** -0.5, 1.75)
    output_bias = scatter_about(key_of[11], (D,), 0.3, 2.0)
    first_gain = jnp.clip(1.0 + 0.18 * jax.random.normal(key_of[12], (D,), jnp.float32), 0.099609375, 1.8984375).astype(jnp.bfloat16)
    first_shift = scatter_about(key_of[13], (D,), 0.3, 2.0)
    inner_weight = scatter_about(key_of[14], (D, FF), D ** -0.5, 0.21875)
    inner_bias = scatter_about(key_of[15], (FF,), 0.5, 3.0)
    outer_weight = scatter_about(key_of[16], (FF, D), FF ** -0.5, 0.109375)
    outer_bias = scatter_about(key_of[17], (D,), 0.3, 2.0)
    second_gain = jnp.clip(1.0 + 0.18 * jax.random.normal(key_of[18], (D,), jnp.float32), 0.099609375, 1.8984375).astype(jnp.bfloat16)
    second_shift = scatter_about(key_of[19], (D,), 0.3, 2.0)
    cotangent = scatter_about(key_of[20], (ITEMS, LENGTH, D), 1.0, 6.0, ((0, 8), (1, 4)))
    return {"hidden": hidden, "groups": groups, "answer_flags": answer_flags, "lengths": lengths, "answer_embed": answer_embed, "query_weight": query_weight, "query_bias": query_bias, "key_weight": key_weight, "value_weight": value_weight, "value_bias": value_bias, "output_weight": output_weight, "output_bias": output_bias, "first_gain": first_gain, "first_shift": first_shift, "inner_weight": inner_weight, "inner_bias": inner_bias, "outer_weight": outer_weight, "outer_bias": outer_bias, "second_gain": second_gain, "second_shift": second_shift, "cotangent": cotangent}


norm_epsilon = 1e-12
masked_score = -1000000000.0

@jax.custom_vjp
def low(v):
    return lax.optimization_barrier(v.astype(jnp.bfloat16)).astype(jnp.float32)

@jax.custom_vjp
def low_back(v):
    return v

def low_keep(v):
    return (low(v), None)

def low_pass(kept, grad):
    return (grad,)

def back_keep(v):
    return (v, None)

def back_low(kept, grad):
    return (low(grad),)
low.defvjp(low_keep, low_pass)
low_back.defvjp(back_keep, back_low)

def normalize(values, gain, shift):
    centre = values - lax.optimization_barrier(jnp.mean(values, -1, keepdims=True))
    spread = lax.optimization_barrier(jnp.mean(centre * centre, -1, keepdims=True))
    return centre * lax.rsqrt(spread + norm_epsilon) * gain + shift

def smooth_gate(values):
    return 0.5 * values * (1.0 + jax.scipy.special.erf(values * 0.7071067811865476))

def matmul(left, right):
    return jnp.dot(left, right, precision=lax.Precision.HIGHEST)

def layer_forward(flags, allowed, inputs, answer_embed, query_weight, query_bias, key_weight, value_weight, value_bias, output_weight, output_bias, first_gain, first_shift, inner_weight, inner_bias, outer_weight, outer_bias, second_gain, second_shift):
    item_count, length, model_width = inputs.shape
    head_count = model_width // HEAD_DIM
    score_scale = 1.0 / jnp.sqrt(jnp.float32(HEAD_DIM)).astype(inputs.dtype)
    entry = inputs + jnp.where(flags[:, :, None] == 1, answer_embed[1], answer_embed[0])
    acts = low(entry)
    queries = low(low_back(matmul(acts, query_weight) + query_bias))
    keys = low(low_back(matmul(acts, key_weight)))
    values = low(low_back(matmul(acts, value_weight) + value_bias))
    query_heads = queries.reshape(item_count, length, head_count, HEAD_DIM)
    key_heads = keys.reshape(item_count, length, head_count, HEAD_DIM)
    value_heads = values.reshape(item_count, length, head_count, HEAD_DIM)
    raw = low_back(jnp.einsum('iqhd,ikhd->ihqk', query_heads, key_heads, precision=lax.Precision.HIGHEST) * score_scale)
    scores = jnp.where(allowed[:, None], raw, masked_score)
    row_peak = lax.optimization_barrier(jnp.max(scores, -1, keepdims=True))
    exponent = jnp.exp(scores - row_peak)
    attention = exponent / lax.optimization_barrier(jnp.sum(exponent, -1, keepdims=True))
    context = jnp.einsum('ihqk,ikhd->iqhd', low(attention), value_heads, precision=lax.Precision.HIGHEST)
    context = low(low_back(context.reshape(item_count, length, model_width)))
    mixed = low_back(matmul(context, output_weight) + output_bias)
    settled = normalize(entry + mixed, first_gain, first_shift)
    inner = low_back(matmul(low(settled), inner_weight) + inner_bias)
    active = low(smooth_gate(inner))
    branch = low_back(matmul(active, outer_weight) + outer_bias)
    return normalize(settled + branch, second_gain, second_shift)

def reference(hidden, groups, answer_flags, lengths, answer_embed, query_weight, query_bias, key_weight, value_weight, value_bias, output_weight, output_bias, first_gain, first_shift, inner_weight, inner_bias, outer_weight, outer_bias, second_gain, second_shift, cotangent):
    params = tuple((p.astype(jnp.float32) for p in (answer_embed, query_weight, query_bias, key_weight, value_weight, value_bias, output_weight, output_bias, first_gain, first_shift, inner_weight, inner_bias, outer_weight, outer_bias, second_gain, second_shift)))

    def split(array):
        return array.reshape((-1, ITEMS_DEV) + array.shape[1:])
    positions = jnp.arange(LENGTH, dtype=jnp.int32)

    def one_group(totals, block):
        inputs, group_ids, flags, item_lengths, outer_grad = block
        allowed = (positions[None, None, :] < item_lengths[:, None, None]) & (group_ids[:, None, :] <= group_ids[:, :, None])

        def forward_fn(inputs_f, *weights):
            return layer_forward(flags, allowed, inputs_f, *weights)
        result, back_fn = jax.vjp(forward_fn, inputs.astype(jnp.float32), *params)
        gradients = back_fn(outer_grad.astype(jnp.float32))
        totals = tuple((a + b for a, b in zip(totals, gradients[1:])))
        return (totals, (result.astype(jnp.bfloat16), gradients[0].astype(jnp.bfloat16)))
    start_totals = tuple((jnp.zeros(p.shape, jnp.float32) for p in params))
    totals, (outputs, input_grads) = lax.scan(one_group, start_totals, (split(hidden), split(groups), split(answer_flags), split(lengths), split(cotangent)))
    return (outputs.reshape(hidden.shape), input_grads.reshape(hidden.shape), totals[0], totals[1], totals[2], totals[3], totals[4], totals[5], totals[6], totals[7], totals[8], totals[9], totals[10], totals[11], totals[12], totals[13], totals[14], totals[15])
```

```python
import functools
import math

import jax
import jax.numpy as jnp
from jax import lax
from jax.experimental import pallas as pl
from jax.experimental.pallas import tpu as pltpu
from jax.sharding import PartitionSpec as P

HEAD_DIM = 64
LANES = 128
EPSILON = 1e-12
BF16 = jnp.bfloat16
F32 = jnp.float32

CONTRACT_LAST = (((1,), (1,)), ((), ()))
CONTRACT_FIRST = (((0,), (0,)), ((), ()))


def dot(a, b, dims=(((1,), (0,)), ((), ()))):
    return lax.dot_general(a, b, dims, preferred_element_type=F32)


def attention_forward_kernel(length, group_column, group_row, q_ref, k_ref, v_ref, o_ref, p_ref, bias):
    rows, keys = bias.shape

    @pl.when(pl.program_id(0) == 0)
    def _():
        place = lax.broadcasted_iota(jnp.int32, (1, keys), 1)
        row = jnp.where(place < length[0], group_row[...], 1 << 20)
        bias[...] = jnp.where(row <= group_column[...], 0.0, -1e30)

    lane = lax.broadcasted_iota(jnp.int32, (rows, LANES), 1)
    k, v = k_ref[...], v_ref[...]
    parts = []
    for head in range(LANES // HEAD_DIM):
        mine = (lane // HEAD_DIM) == head
        q = jnp.where(mine, q_ref[...].astype(F32) * (1.0 / math.sqrt(HEAD_DIM)), 0.0).astype(BF16)
        s = dot(q, k, CONTRACT_LAST) + bias[...]
        e = jnp.exp(s - jnp.max(s, -1, keepdims=True))
        p = (e * (1.0 / jnp.sum(e, -1, keepdims=True))).astype(BF16)
        p_ref[head] = p
        parts.append(jnp.where(mine, dot(p, v), 0.0))
    o_ref[...] = sum(parts).astype(BF16)


def attention_backward_kernel(p_ref, q_ref, k_ref, v_ref, o_ref, do_ref, dq_ref, dk_ref, dv_ref):
    rows = q_ref.shape[0]
    scale = 1.0 / math.sqrt(HEAD_DIM)
    lane = lax.broadcasted_iota(jnp.int32, (rows, LANES), 1)
    q, k, v, do = q_ref[...], k_ref[...], v_ref[...], do_ref[...]
    weighed = do.astype(F32) * o_ref[...].astype(F32)
    dq, dk, dv = [], [], []
    for head in range(LANES // HEAD_DIM):
        mine = (lane // HEAD_DIM) == head
        p = p_ref[head]
        do_head = jnp.where(mine, do, jnp.zeros_like(do))
        row_dot = jnp.sum(jnp.where(mine, weighed, 0.0), -1, keepdims=True)
        ds = (p.astype(F32) * (dot(do_head, v, CONTRACT_LAST) - row_dot)).astype(BF16)
        dq.append(jnp.where(mine, dot(ds, k), 0.0))
        dk.append(jnp.where(mine, dot(ds, q, CONTRACT_FIRST), 0.0))
        dv.append(jnp.where(mine, dot(p, do, CONTRACT_FIRST), 0.0))
    dq_ref[...] = (sum(dq) * scale).astype(BF16)
    dk_ref[...] = (sum(dk) * scale).astype(BF16)
    dv_ref[...] = sum(dv).astype(BF16)


def attention_forward(queries, keys, values, group_ids, length):
    rows, width = queries.shape
    pairs, heads = width // LANES, LANES // HEAD_DIM
    whole = lambda shape: pl.BlockSpec(shape, lambda i: (0, 0))
    column = pl.BlockSpec((rows, LANES), lambda i: (0, i))
    return pl.pallas_call(
        attention_forward_kernel,
        grid=(pairs,),
        out_shape=(
            jax.ShapeDtypeStruct((rows, width), BF16),
            jax.ShapeDtypeStruct((pairs * heads, rows, rows), BF16),
        ),
        in_specs=[
            pl.BlockSpec(memory_space=pltpu.SMEM),
            whole((rows, 1)),
            whole((1, rows)),
            column,
            column,
            column,
        ],
        out_specs=(column, pl.BlockSpec((heads, rows, rows), lambda i: (i, 0, 0))),
        scratch_shapes=[pltpu.VMEM((rows, rows), F32)],
        compiler_params=pltpu.CompilerParams(vmem_limit_bytes=40 << 20),
        cost_estimate=pl.CostEstimate(
            flops=16 * rows * rows * width, bytes_accessed=8 * rows * width, transcendentals=rows * rows * pairs * heads
        ),
        name="attention_forward",
    )(length, group_ids[:, None], group_ids[None, :], queries, keys, values)


def attention_backward(attention, queries, keys, values, context, d_context):
    rows, width = queries.shape
    pairs, heads = width // LANES, LANES // HEAD_DIM
    column = pl.BlockSpec((rows, LANES), lambda i: (0, i))
    grad = jax.ShapeDtypeStruct((rows, width), BF16)
    return pl.pallas_call(
        attention_backward_kernel,
        grid=(pairs,),
        out_shape=(grad, grad, grad),
        in_specs=[pl.BlockSpec((heads, rows, rows), lambda i: (i, 0, 0))] + [column] * 5,
        out_specs=(column, column, column),
        compiler_params=pltpu.CompilerParams(vmem_limit_bytes=40 << 20),
        cost_estimate=pl.CostEstimate(
            flops=32 * rows * rows * width, bytes_accessed=24 * rows * width, transcendentals=0
        ),
        name="attention_backward",
    )(attention, queries, keys, values, context, d_context)


def norm_forward(values, gain, shift):
    centre = values - jnp.mean(values, -1, keepdims=True)
    inverse = lax.rsqrt(jnp.mean(centre * centre, -1, keepdims=True) + EPSILON)
    hat = centre * inverse
    return hat * gain + shift, hat, inverse


def norm_backward(cotangent, hat, inverse, gain):
    g = cotangent * gain
    return inverse * (
        g - jnp.mean(g, -1, keepdims=True) - hat * jnp.mean(g * hat, -1, keepdims=True)
    )


def gate_parts(u):
    half_square = -0.5 * u * u
    bell = jnp.exp(half_square)
    share = 0.5 * (1.0 + lax.erf(u * 0.7071067811865476))
    return u * share, share + u * bell * 0.3989422804014327


def swap_pairs(array, axis, mask):
    size = lax.axis_size(axis)
    return lax.ppermute(array, axis, [(i, i ^ mask) for i in range(size)])


def pick(array, index, dim):
    return lax.dynamic_index_in_dim(array, index, dim, keepdims=False)


def items_for_rows(blocks):
    size = lax.axis_size("seq")
    me = lax.axis_index("seq")
    items, rows, width = blocks.shape
    whole = jnp.zeros((items, rows, width), blocks.dtype)
    for mask in range(size):
        block = pick(blocks, me ^ mask, 0)
        if mask:
            block = swap_pairs(block, "seq", mask)
        whole = lax.dynamic_update_index_in_dim(whole, block, me ^ mask, 0)
    return whole.reshape(items * rows, width)


def rows_for_items(whole, items):
    return items_for_rows(whole.reshape(items, whole.shape[0] // items, whole.shape[1])).reshape(
        items, whole.shape[0] // items, whole.shape[1]
    )


def total(parts):
    result = parts[0].astype(F32)
    for part in parts[1:]:
        result = result + part.astype(F32)
    return result


def halve(parts, dim, axis, bit):
    mine = (lax.axis_index(axis) >> bit) & 1
    sent = total([pick(part, 1 - mine, dim) for part in parts]).astype(BF16)
    got = swap_pairs(sent, axis, 1 << bit)
    return [pick(part, mine, dim) for part in parts] + [got]


def scatter(gradient):
    batch, seq = lax.axis_size("batch"), lax.axis_size("seq")
    rows, columns = gradient.shape
    batch_bits, seq_bits = batch.bit_length() - 1, seq.bit_length() - 1
    each = rows // (batch * seq)
    shape = (2,) * (batch_bits + seq_bits) + (each, columns)
    parts = [gradient.astype(BF16).reshape(shape)]
    parts = halve(parts, batch_bits - 1, "batch", 0)
    ways = []
    for way in range(2):
        half = [
            lax.slice_in_dim(part, way * (columns // 2), (way + 1) * (columns // 2), axis=part.ndim - 1)
            for part in parts
        ]
        bits = list(range(1, batch_bits))
        if way:
            bits = bits[::-1]
        left = list(range(batch_bits - 1, 0, -1))
        for bit in bits:
            dim = left.index(bit)
            half = halve(half, dim, "batch", bit)
            left.remove(bit)
        ways.append(half)
    parts = [jnp.concatenate([a, b], -1) for a, b in zip(*ways)]
    for bit in range(seq_bits):
        parts = halve(parts, seq_bits - 1 - bit, "seq", bit)
    return total(parts)


def per_device(
    hidden,
    groups,
    answer_flags,
    lengths,
    answer_embed,
    query_weight,
    query_bias,
    key_weight,
    value_weight,
    value_bias,
    output_weight,
    output_bias,
    first_gain,
    first_shift,
    inner_weight,
    inner_bias,
    outer_weight,
    outer_bias,
    second_gain,
    second_shift,
    cotangent,
):
    items, block_rows, width = hidden.shape
    length = items * block_rows
    me = lax.axis_index("seq")
    flags = pick(lax.all_gather(answer_flags, "seq", axis=1, tiled=True), me, 0)
    group_ids = pick(groups, me, 0)
    item_length = lax.dynamic_slice_in_dim(lengths, me, 1)

    embed = answer_embed.astype(F32)
    entry_rows = hidden.astype(F32) + jnp.where(answer_flags[:, :, None] == 1, embed[1], embed[0])
    acts = items_for_rows(entry_rows.astype(BF16))
    cotangent_item = items_for_rows(cotangent)

    queries = (dot(acts, query_weight) + query_bias.astype(F32)).astype(BF16)
    keys = dot(acts, key_weight).astype(BF16)
    values = (dot(acts, value_weight) + value_bias.astype(F32)).astype(BF16)
    context, attention = attention_forward(queries, keys, values, group_ids, item_length)
    first_sum = acts.astype(F32) + dot(context, output_weight) + output_bias.astype(F32)
    gain_one, gain_two = first_gain.astype(F32), second_gain.astype(F32)
    settled, first_hat, first_inverse = norm_forward(first_sum, gain_one, first_shift.astype(F32))
    settled_low = settled.astype(BF16)
    inner = dot(settled_low, inner_weight) + inner_bias.astype(F32)
    active, slope = gate_parts(inner)
    active, slope = active.astype(BF16), slope.astype(BF16)
    second_sum = settled + dot(active, outer_weight) + outer_bias.astype(F32)
    output, second_hat, second_inverse = norm_forward(second_sum, gain_two, second_shift.astype(F32))
    output = rows_for_items(output.astype(BF16), items)

    upper = cotangent_item.astype(F32)
    d_second = norm_backward(upper, second_hat, second_inverse, gain_two)
    second_gain_gradient = jnp.sum(upper * second_hat, 0)
    second_shift_gradient = jnp.sum(upper, 0)
    branch_low = d_second.astype(BF16)
    outer_bias_gradient = jnp.sum(branch_low.astype(F32), 0)
    outer_weight_gradient = scatter(dot(active, branch_low, CONTRACT_FIRST))
    d_inner = (dot(branch_low, outer_weight, CONTRACT_LAST) * slope.astype(F32)).astype(BF16)
    inner_bias_gradient = jnp.sum(d_inner.astype(F32), 0)
    inner_weight_gradient = scatter(dot(settled_low, d_inner, CONTRACT_FIRST))
    d_settled = d_second + dot(d_inner, inner_weight, CONTRACT_LAST)
    d_first = norm_backward(d_settled, first_hat, first_inverse, gain_one)
    first_gain_gradient = jnp.sum(d_settled * first_hat, 0)
    first_shift_gradient = jnp.sum(d_settled, 0)
    mixed_low = d_first.astype(BF16)
    output_bias_gradient = jnp.sum(mixed_low.astype(F32), 0)
    output_weight_gradient = dot(context, mixed_low, CONTRACT_FIRST)
    d_context = dot(mixed_low, output_weight, CONTRACT_LAST).astype(BF16)
    d_queries, d_keys, d_values = attention_backward(
        attention, queries, keys, values, context, d_context
    )
    d_entry = (
        d_first
        + dot(d_queries, query_weight, CONTRACT_LAST)
        + dot(d_keys, key_weight, CONTRACT_LAST)
        + dot(d_values, value_weight, CONTRACT_LAST)
    )
    input_gradient = rows_for_items(d_entry.astype(BF16), items)
    query_weight_gradient = dot(acts, d_queries, CONTRACT_FIRST)
    key_weight_gradient = dot(acts, d_keys, CONTRACT_FIRST)
    value_weight_gradient = dot(acts, d_values, CONTRACT_FIRST)
    narrow = scatter(
        jnp.concatenate(
            [
                output_weight_gradient.astype(BF16),
                query_weight_gradient.astype(BF16),
                key_weight_gradient.astype(BF16),
                value_weight_gradient.astype(BF16),
            ],
            1,
        )
    )
    output_weight_gradient, query_weight_gradient, key_weight_gradient, value_weight_gradient = jnp.split(
        narrow, 4, 1
    )
    query_bias_gradient = jnp.sum(d_queries.astype(F32), 0)
    value_bias_gradient = jnp.sum(d_values.astype(F32), 0)
    flagged = (flags == 1)[:, None]
    vectors = jnp.concatenate(
        [
            jnp.sum(jnp.where(flagged, 0.0, d_entry), 0)[None],
            jnp.sum(jnp.where(flagged, d_entry, 0.0), 0)[None],
            query_bias_gradient[None],
            value_bias_gradient[None],
            output_bias_gradient[None],
            first_gain_gradient[None],
            first_shift_gradient[None],
            outer_bias_gradient[None],
            second_gain_gradient[None],
            second_shift_gradient[None],
            inner_bias_gradient.reshape(-1, width),
        ],
        0,
    )
    vectors = lax.psum(vectors, ("batch", "seq"))
    pieces = lax.axis_size("batch") * lax.axis_size("seq")
    place = lax.axis_index("batch") * lax.axis_size("seq") + me
    size = width // pieces
    piece = lax.dynamic_slice_in_dim(vectors[:10], place * size, size, 1)
    inner_bias_gradient = lax.dynamic_slice_in_dim(
        vectors[10:].reshape(-1), place * size * 4, size * 4, 0
    )
    return (
        output,
        input_gradient,
        piece[:2],
        query_weight_gradient,
        piece[2],
        key_weight_gradient,
        value_weight_gradient,
        piece[3],
        output_weight_gradient,
        piece[4],
        piece[5],
        piece[6],
        inner_weight_gradient,
        inner_bias_gradient,
        outer_weight_gradient,
        piece[7],
        piece[8],
        piece[9],
    )


def solution(mesh):
    both = ("batch", "seq")
    in_specs = (
        (P("batch", "seq", None), P("batch", None), P("batch", "seq"), P("batch"))
        + (P(),) * 16
        + (P("batch", "seq", None),)
    )
    matrix, vector = P(both, None), P(both)
    out_specs = (
        P("batch", "seq", None),
        P("batch", "seq", None),
        P(None, both),
        matrix,
        vector,
        matrix,
        matrix,
        vector,
        matrix,
        vector,
        vector,
        vector,
        matrix,
        vector,
        matrix,
        vector,
        vector,
        vector,
    )
    return jax.shard_map(
        per_device, mesh=mesh, in_specs=in_specs, out_specs=out_specs, check_vma=False
    )
```

```python
import functools
import math

import jax
import jax.numpy as jnp
from jax import lax
from jax.experimental import pallas as pl
from jax.experimental.pallas import tpu as pltpu
from jax.sharding import PartitionSpec as P

HEAD_DIM = 64
LANES = 128
EPSILON = 1e-12
BF16 = jnp.bfloat16
F32 = jnp.float32

CONTRACT_LAST = (((1,), (1,)), ((), ()))
CONTRACT_FIRST = (((0,), (0,)), ((), ()))


def dot(a, b, dims=(((1,), (0,)), ((), ()))):
    return lax.dot_general(a, b, dims, preferred_element_type=F32)


def attention_forward_kernel(length, group_column, group_row, q_ref, k_ref, v_ref, o_ref, p_ref, bias):
    rows, keys = bias.shape

    @pl.when(pl.program_id(0) == 0)
    def _():
        place = lax.broadcasted_iota(jnp.int32, (1, keys), 1)
        row = jnp.where(place < length[0], group_row[...], 1 << 20)
        bias[...] = jnp.where(row <= group_column[...], 0.0, -1e30)

    lane = lax.broadcasted_iota(jnp.int32, (rows, LANES), 1)
    k, v = k_ref[...], v_ref[...]
    parts = []
    for head in range(LANES // HEAD_DIM):
        mine = (lane // HEAD_DIM) == head
        q = jnp.where(mine, q_ref[...].astype(F32) * (1.0 / math.sqrt(HEAD_DIM)), 0.0).astype(BF16)
        s = dot(q, k, CONTRACT_LAST) + bias[...]
        e = jnp.exp(s - jnp.max(s, -1, keepdims=True))
        p = (e * (1.0 / jnp.sum(e, -1, keepdims=True))).astype(BF16)
        p_ref[head] = p
        parts.append(jnp.where(mine, dot(p, v), 0.0))
    o_ref[...] = sum(parts).astype(BF16)


def attention_backward_kernel(p_ref, q_ref, k_ref, v_ref, o_ref, do_ref, dq_ref, dk_ref, dv_ref):
    rows = q_ref.shape[0]
    scale = 1.0 / math.sqrt(HEAD_DIM)
    lane = lax.broadcasted_iota(jnp.int32, (rows, LANES), 1)
    q, k, v, do = q_ref[...], k_ref[...], v_ref[...], do_ref[...]
    weighed = do.astype(F32) * o_ref[...].astype(F32)
    dq, dk, dv = [], [], []
    for head in range(LANES // HEAD_DIM):
        mine = (lane // HEAD_DIM) == head
        p = p_ref[head]
        do_head = jnp.where(mine, do, jnp.zeros_like(do))
        row_dot = jnp.sum(jnp.where(mine, weighed, 0.0), -1, keepdims=True)
        ds = (p.astype(F32) * (dot(do_head, v, CONTRACT_LAST) - row_dot)).astype(BF16)
        dq.append(jnp.where(mine, dot(ds, k), 0.0))
        dk.append(jnp.where(mine, dot(ds, q, CONTRACT_FIRST), 0.0))
        dv.append(jnp.where(mine, dot(p, do, CONTRACT_FIRST), 0.0))
    dq_ref[...] = (sum(dq) * scale).astype(BF16)
    dk_ref[...] = (sum(dk) * scale).astype(BF16)
    dv_ref[...] = sum(dv).astype(BF16)


def attention_forward(queries, keys, values, group_ids, length):
    rows, width = queries.shape
    pairs, heads = width // LANES, LANES // HEAD_DIM
    whole = lambda shape: pl.BlockSpec(shape, lambda i: (0, 0))
    column = pl.BlockSpec((rows, LANES), lambda i: (0, i))
    return pl.pallas_call(
        attention_forward_kernel,
        grid=(pairs,),
        out_shape=(
            jax.ShapeDtypeStruct((rows, width), BF16),
            jax.ShapeDtypeStruct((pairs * heads, rows, rows), BF16),
        ),
        in_specs=[
            pl.BlockSpec(memory_space=pltpu.SMEM),
            whole((rows, 1)),
            whole((1, rows)),
            column,
            column,
            column,
        ],
        out_specs=(column, pl.BlockSpec((heads, rows, rows), lambda i: (i, 0, 0))),
        scratch_shapes=[pltpu.VMEM((rows, rows), F32)],
        compiler_params=pltpu.CompilerParams(vmem_limit_bytes=40 << 20),
        cost_estimate=pl.CostEstimate(
            flops=16 * rows * rows * width, bytes_accessed=8 * rows * width, transcendentals=rows * rows * pairs * heads
        ),
        name="attention_forward",
    )(length, group_ids[:, None], group_ids[None, :], queries, keys, values)


def attention_backward(attention, queries, keys, values, context, d_context):
    rows, width = queries.shape
    pairs, heads = width // LANES, LANES // HEAD_DIM
    column = pl.BlockSpec((rows, LANES), lambda i: (0, i))
    grad = jax.ShapeDtypeStruct((rows, width), BF16)
    return pl.pallas_call(
        attention_backward_kernel,
        grid=(pairs,),
        out_shape=(grad, grad, grad),
        in_specs=[pl.BlockSpec((heads, rows, rows), lambda i: (i, 0, 0))] + [column] * 5,
        out_specs=(column, column, column),
        compiler_params=pltpu.CompilerParams(vmem_limit_bytes=40 << 20),
        cost_estimate=pl.CostEstimate(
            flops=32 * rows * rows * width, bytes_accessed=24 * rows * width, transcendentals=0
        ),
        name="attention_backward",
    )(attention, queries, keys, values, context, d_context)


def norm_forward(values, gain, shift):
    centre = values - jnp.mean(values, -1, keepdims=True)
    inverse = lax.rsqrt(jnp.mean(centre * centre, -1, keepdims=True) + EPSILON)
    hat = centre * inverse
    return hat * gain + shift, hat, inverse


def norm_backward(cotangent, hat, inverse, gain):
    g = cotangent * gain
    return inverse * (
        g - jnp.mean(g, -1, keepdims=True) - hat * jnp.mean(g * hat, -1, keepdims=True)
    )


def gate_parts(u):
    half_square = -0.5 * u * u
    bell = jnp.exp(half_square)
    share = 0.5 * (1.0 + lax.erf(u * 0.7071067811865476))
    return u * share, share + u * bell * 0.3989422804014327


def swap_pairs(array, axis, mask):
    size = lax.axis_size(axis)
    return lax.ppermute(array, axis, [(i, i ^ mask) for i in range(size)])


def pick(array, index, dim):
    return lax.dynamic_index_in_dim(array, index, dim, keepdims=False)


def spec(shape, index):
    return pl.BlockSpec(shape, index)


def whole_spec(shape):
    zeros = (0,) * len(shape)
    return pl.BlockSpec(shape, lambda *_: zeros)


def prefetch_call(kernel, name, grid, in_specs, out_specs, out_shape, limit, flops, moved, scratch=(), extra=0):
    return pl.pallas_call(
        kernel,
        grid_spec=pltpu.PrefetchScalarGridSpec(
            num_scalar_prefetch=1,
            grid=grid,
            in_specs=in_specs + [pl.BlockSpec(memory_space=pl.ANY)] * extra,
            out_specs=out_specs,
            scratch_shapes=list(scratch),
        ),
        out_shape=out_shape,
        compiler_params=pltpu.CompilerParams(vmem_limit_bytes=limit << 20),
        cost_estimate=pl.CostEstimate(flops=flops, bytes_accessed=moved, transcendentals=0),
        name=name,
    )


def entry_kernel(count, place, hidden, flags, embed, *outs):
    rows = hidden.shape[1]
    row = lax.broadcasted_iota(jnp.int32, (rows, rows), 0)
    column = lax.broadcasted_iota(jnp.int32, (rows, rows), 1)
    first, second = embed[0:1].astype(F32), embed[1:2].astype(F32)
    for mask in range(count):
        item = place[0] ^ mask
        flag = flags[pl.ds(item, 1), :].astype(F32)
        upright = jnp.sum(jnp.where(row == column, flag, 0.0), 1, keepdims=True)
        added = jnp.where(upright == 1.0, second, first)
        outs[mask][...] = (hidden[item].astype(F32) + added).astype(BF16)


def entry_blocks(place, hidden, flags, embed):
    count, rows, width = hidden.shape
    return prefetch_call(
        functools.partial(entry_kernel, count),
        "entry_blocks",
        (1,),
        [whole_spec(hidden.shape), whole_spec(flags.shape), whole_spec(embed.shape)],
        (whole_spec((rows, width)),) * count,
        (jax.ShapeDtypeStruct((rows, width), BF16),) * count,
        16,
        hidden.size * 4,
        hidden.size * 4,
    )(place, hidden, flags, embed)


def flagged_kernel(count, place, cotangent, flags, *outs):
    rows = cotangent.shape[1]
    for mask in range(count):
        item = place[0] ^ mask
        outs[mask][pl.ds(0, rows), :] = cotangent[item]
        outs[mask][pl.ds(rows, 16), :] = jnp.zeros((16, cotangent.shape[2]), BF16)
        flag = jnp.broadcast_to(flags[pl.ds(item, 1), :].astype(F32), (16, rows))
        outs[mask][pl.ds(rows, 16), pl.ds(0, rows)] = flag.astype(BF16)


def flagged_blocks(place, cotangent, flags):
    count, rows, width = cotangent.shape
    return prefetch_call(
        functools.partial(flagged_kernel, count),
        "flagged_blocks",
        (1,),
        [whole_spec(cotangent.shape), whole_spec(flags.shape)],
        (whole_spec((rows + 16, width)),) * count,
        (jax.ShapeDtypeStruct((rows + 16, width), BF16),) * count,
        16,
        cotangent.size,
        cotangent.size * 4,
    )(place, cotangent, flags)


def split_kernel(count, place, array, *outs):
    for mask in range(count):
        outs[mask][...] = array[place[0] ^ mask]


def split_blocks(place, array, count):
    rows, width = array.shape[0] // count, array.shape[1]
    array = array.reshape(count, rows, width)
    return prefetch_call(
        functools.partial(split_kernel, count),
        "split_blocks",
        (1,),
        [whole_spec(array.shape)],
        (whole_spec((rows, width)),) * count,
        (jax.ShapeDtypeStruct((rows, width), BF16),) * count,
        16,
        array.size,
        array.size * 4,
    )(place, array)


def join_kernel(count, place, *refs):
    out = refs[count]
    rows = out.shape[1]
    for mask in range(count):
        out[place[0] ^ mask] = refs[mask][pl.ds(0, rows), :]


def join_blocks(place, blocks, rows):
    count, width = len(blocks), blocks[0].shape[1]
    return prefetch_call(
        functools.partial(join_kernel, count),
        "join_blocks",
        (1,),
        [whole_spec(b.shape) for b in blocks],
        whole_spec((count, rows, width)),
        jax.ShapeDtypeStruct((count, rows, width), BF16),
        16,
        count * rows * width,
        count * rows * width * 4,
    )(place, *blocks)


def exchange(blocks):
    order = sorted(range(1, len(blocks)), key=lambda mask: mask < 2)
    got = {mask: swap_pairs(blocks[mask], "seq", mask) for mask in order}
    return [blocks[0]] + [got[mask] for mask in range(1, len(blocks))]


def total(parts):
    result = parts[0].astype(F32)
    for part in parts[1:]:
        result = result + part.astype(F32)
    return result


def halve(parts, dim, axis, bit, dtype=BF16):
    mine = (lax.axis_index(axis) >> bit) & 1
    sent = total([pick(part, 1 - mine, dim) for part in parts]).astype(dtype)
    got = swap_pairs(sent, axis, 1 << bit)
    return [pick(part, mine, dim) for part in parts] + [got]


def scatter(gradient):
    batch, seq = lax.axis_size("batch"), lax.axis_size("seq")
    rows, columns = gradient.shape
    batch_bits, seq_bits = batch.bit_length() - 1, seq.bit_length() - 1
    each = rows // (batch * seq)
    shape = (2,) * (batch_bits + seq_bits) + (each, columns)
    parts = [gradient.astype(BF16).reshape(shape)]
    parts = halve(parts, batch_bits - 1, "batch", 0)
    ways = []
    for way in range(2):
        half = [
            lax.slice_in_dim(part, way * (columns // 2), (way + 1) * (columns // 2), axis=part.ndim - 1)
            for part in parts
        ]
        bits = list(range(1, batch_bits))
        if way:
            bits = bits[::-1]
        left = list(range(batch_bits - 1, 0, -1))
        for bit in bits:
            dim = left.index(bit)
            half = halve(half, dim, "batch", bit)
            left.remove(bit)
        ways.append(half)
    parts = [jnp.concatenate([a, b], -1) for a, b in zip(*ways)]
    for bit in range(seq_bits):
        parts = halve(parts, seq_bits - 1 - bit, "seq", bit)
    return total(parts)


GROUPS, SHARES, PIECE, SIDE = 4, 4, 96, 768


def tall_gradient_kernel(place, left, right, out):
    out[0] = dot(left[...], right[...], CONTRACT_FIRST).reshape(out.shape[1:]).astype(BF16)


def tall_gradient(place, left, right, keep):
    tokens, high = left.shape
    rows = high // GROUPS // 2
    shape = (GROUPS, SHARES, PIECE, SIDE)
    return prefetch_call(
        tall_gradient_kernel,
        "tall_gradient",
        (GROUPS,),
        [
            spec((tokens, rows), lambda i, place: (0, 2 * i + (place[1] if keep else 1 - place[1]))),
            whole_spec(right.shape),
        ],
        spec((1,) + shape[1:], lambda i, place: (i, 0, 0, 0)),
        jax.ShapeDtypeStruct(shape, BF16),
        24,
        tokens * high * SIDE,
        tokens * high + GROUPS * SHARES * PIECE * SIDE * 2,
    )(place, left, right)


def stack_pieces(place, totals, send, keep):
    each = SIDE // (GROUPS * SHARES * 2)
    for out, core in ((send, 1 - place[1]), (keep, place[1])):
        for group in range(GROUPS):
            for share in range(SHARES):
                start = pl.multiple_of((2 * group + core) * (SHARES * each) + share * each, 8)
                piece = jnp.concatenate([t[pl.ds(start, each), :] for t in totals], 0)
                out[group, share] = piece.astype(BF16)


def wide_gradient_kernel(place, left, right, send, keep, first, second):
    side = first.shape[1]
    first[...] = dot(left[...], right[:, :side], CONTRACT_FIRST)
    second[...] = dot(left[...], right[:, side:], CONTRACT_FIRST)
    stack_pieces(place, (first, second), send, keep)


def wide_gradient(place, left, right):
    tokens = left.shape[0]
    shape = (GROUPS, SHARES, PIECE, SIDE)
    part = spec((GROUPS, SHARES, PIECE // 2, SIDE), lambda i, place: (0, 0, i, 0))
    return prefetch_call(
        wide_gradient_kernel,
        "wide_gradient",
        (2,),
        [whole_spec(left.shape), spec((tokens, 2 * SIDE), lambda i, place: (0, i))],
        (part, part),
        (jax.ShapeDtypeStruct(shape, BF16),) * 2,
        40,
        tokens * SIDE * SIDE * 8,
        tokens * SIDE * 10 + GROUPS * SHARES * PIECE * SIDE * 4,
        [pltpu.VMEM((SIDE, SIDE), F32)] * 2,
    )(place, left, right)


def square_gradients_kernel(place, context, acts, mixed, d_queries, d_keys, d_values, send, keep, first, second):
    each = 2 * (SIDE // (GROUPS * SHARES * 2))
    first[...] = dot(context[...], mixed[...], CONTRACT_FIRST)
    second[...] = dot(acts[...], d_queries[...], CONTRACT_FIRST)
    top = pl.ds(0, each)
    stack_pieces(place, (first, second), send.at[:, :, top], keep.at[:, :, top])
    first[...] = dot(acts[...], d_keys[...], CONTRACT_FIRST)
    second[...] = dot(acts[...], d_values[...], CONTRACT_FIRST)
    rest = pl.ds(each, each)
    stack_pieces(place, (first, second), send.at[:, :, rest], keep.at[:, :, rest])


def square_gradients(place, *arrays):
    tokens = arrays[0].shape[0]
    shape = (GROUPS, SHARES, PIECE, SIDE)
    return prefetch_call(
        square_gradients_kernel,
        "square_gradients",
        (1,),
        [whole_spec(a.shape) for a in arrays],
        (whole_spec(shape),) * 2,
        (jax.ShapeDtypeStruct(shape, BF16),) * 2,
        40,
        tokens * SIDE * SIDE * 8,
        tokens * SIDE * 12 + GROUPS * SHARES * PIECE * SIDE * 4,
        [pltpu.VMEM((SIDE, SIDE), F32)] * 2,
    )(place, *arrays)


def add(*parts):
    result = parts[0].astype(F32)
    for part in parts[1:]:
        result = result + part.astype(F32)
    return result


def first_sums_kernel(place, keep_a, got_a, keep_b, got_b, send_a, send_b):
    send_a[...] = add(keep_a[...], got_a[...]).astype(BF16)
    send_b[...] = add(keep_b[...], got_b[...]).astype(BF16)


def first_sums(place, keep, got):
    block = (1, SHARES, PIECE, SIDE // 2)
    to_x = spec(block, lambda i, place: (2 * i + 1 - place[2], 0, 0, 0))
    to_y = spec(block, lambda i, place: (2 * (1 - place[3]) + i, 0, 0, 1))
    out = spec(block, lambda i, place: (i, 0, 0, 0))
    shape = jax.ShapeDtypeStruct((2,) + block[1:], BF16)
    return prefetch_call(
        first_sums_kernel,
        "first_sums",
        (2,),
        [to_x, to_x, to_y, to_y],
        (out, out),
        (shape, shape),
        12,
        4 * SHARES * PIECE * SIDE,
        6 * SHARES * PIECE * SIDE * 2,
    )(place, keep, got, keep, got)


def second_sums_kernel(place, keep_a, got_a, x_a, keep_b, got_b, y_b, send_a, send_b):
    send_a[...] = add(keep_a[0], got_a[0], x_a[0]).astype(BF16)
    send_b[...] = add(keep_b[0], got_b[0], y_b[0]).astype(BF16)


def second_sums(place, keep, got, from_x, from_y):
    block = (1, SHARES, PIECE, SIDE // 2)
    to_y = spec(block, lambda i, place: (2 * (1 - place[3]) + place[2], 0, 0, 0))
    to_x = spec(block, lambda i, place: (2 * place[3] + 1 - place[2], 0, 0, 1))
    other_y = spec(block, lambda i, place: (1 - place[3], 0, 0, 0))
    other_x = spec(block, lambda i, place: (1 - place[2], 0, 0, 0))
    shape = jax.ShapeDtypeStruct(block[1:], BF16)
    return prefetch_call(
        second_sums_kernel,
        "second_sums",
        (1,),
        [to_y, to_y, other_y, to_x, to_x, other_x],
        (whole_spec(block[1:]),) * 2,
        (shape, shape),
        12,
        2 * SHARES * PIECE * SIDE,
        4 * SHARES * PIECE * SIDE * 2,
    )(place, keep, got, from_x, keep, got, from_y)


def third_sums_kernel(place, keep, got, x_a, y_b, y_a, x_b, send, kept):
    side = SIDE // 2
    bit = place[0] & 1
    for out, low in ((send, 1 - bit), (kept, bit)):
        for high in range(SHARES // 2):
            share = 2 * high + low
            a = add(keep[0, share, :, :side], got[0, share, :, :side], x_a[0, share], y_a[share])
            b = add(keep[0, share, :, side:], got[0, share, :, side:], y_b[0, share], x_b[share])
            out[high] = jnp.concatenate([a, b], 1).astype(out.dtype)


def third_sums(place, keep, got, from_x, from_y, then_y, then_x):
    full = spec((1, SHARES, PIECE, SIDE), lambda i, place: (2 * place[3] + place[2], 0, 0, 0))
    half = (1, SHARES, PIECE, SIDE // 2)
    out = (SHARES // 2, PIECE, SIDE)
    return prefetch_call(
        third_sums_kernel,
        "third_sums",
        (1,),
        [
            full,
            full,
            spec(half, lambda i, place: (place[3], 0, 0, 0)),
            spec(half, lambda i, place: (place[2], 0, 0, 0)),
            whole_spec(half[1:]),
            whole_spec(half[1:]),
        ],
        (whole_spec(out),) * 2,
        (jax.ShapeDtypeStruct(out, BF16), jax.ShapeDtypeStruct(out, F32)),
        16,
        4 * SHARES * PIECE * SIDE,
        6 * SHARES * PIECE * SIDE * 2,
    )(place, keep, got, from_x, from_y, then_y, then_x)


def fourth_sums_kernel(place, kept, got, send):
    other = 1 - (place[0] >> 1)
    send[...] = add(kept[other], got[other]).astype(BF16)


def fourth_sums(place, kept, got):
    return prefetch_call(
        fourth_sums_kernel,
        "fourth_sums",
        (1,),
        [whole_spec(kept.shape), whole_spec(got.shape)],
        whole_spec(kept.shape[1:]),
        jax.ShapeDtypeStruct(kept.shape[1:], BF16),
        12,
        PIECE * SIDE,
        PIECE * SIDE * 8,
    )(place, kept, got)


def last_sums_kernel(form, place, kept, got, last, *outs):
    mine = place[0] >> 1
    result = add(kept[mine], got[mine], last[...])
    each = PIECE // 4
    if form == "tall":
        outs[0][...] = result
    else:
        for i in range(4):
            rows = result[i * each : (i + 1) * each]
            if form == "wide":
                outs[0][:, i * SIDE : (i + 1) * SIDE] = rows
            else:
                outs[i][...] = rows


def last_sums(place, kept, got, last, form):
    each = PIECE // 4
    shapes = {"tall": [(PIECE, SIDE)], "wide": [(each, 4 * SIDE)], "square": [(each, SIDE)] * 4}[form]
    return prefetch_call(
        functools.partial(last_sums_kernel, form),
        "last_sums",
        (1,),
        [whole_spec(kept.shape), whole_spec(got.shape), whole_spec(last.shape)],
        tuple(whole_spec(s) for s in shapes),
        tuple(jax.ShapeDtypeStruct(s, F32) for s in shapes),
        12,
        PIECE * SIDE * 2,
        PIECE * SIDE * 14,
    )(place, kept, got, last)


def scatter_pieces(place, send, keep, form):
    got = swap_pairs(send, "batch", 1)
    to_x, to_y = first_sums(place, keep, got)
    from_x, from_y = swap_pairs(to_x, "batch", 2), swap_pairs(to_y, "batch", 4)
    to_y, to_x = second_sums(place, keep, got, from_x, from_y)
    then_y, then_x = swap_pairs(to_y, "batch", 4), swap_pairs(to_x, "batch", 2)
    send, kept = third_sums(place, keep, got, from_x, from_y, then_y, then_x)
    got = swap_pairs(send, "seq", 1)
    last = swap_pairs(fourth_sums(place, kept, got), "seq", 2)
    return last_sums(place, kept, got, last, form)


def scatter_vectors(vectors):
    batch, seq = lax.axis_size("batch"), lax.axis_size("seq")
    count, width = vectors.shape
    each = width // (batch * seq)
    blocks = jnp.swapaxes(vectors.reshape(count, batch * seq, each), 0, 1)
    blocks = blocks.reshape(batch * seq, count * each)
    spare = -(count * each) % LANES
    blocks = jnp.pad(blocks, ((0, 0), (0, spare)))
    batch_bits, seq_bits = batch.bit_length() - 1, seq.bit_length() - 1
    parts = [blocks.reshape((2,) * (batch_bits + seq_bits) + (1, count * each + spare))]
    for bit in range(batch_bits):
        parts = [total(halve(parts, batch_bits - 1 - bit, "batch", bit, F32))]
    for bit in range(seq_bits):
        parts = [total(halve(parts, seq_bits - 1 - bit, "seq", bit, F32))]
    return parts[0].reshape(-1)[: count * each].reshape(count, each)


def per_device(
    hidden,
    groups,
    answer_flags,
    lengths,
    answer_embed,
    query_weight,
    query_bias,
    key_weight,
    value_weight,
    value_bias,
    output_weight,
    output_bias,
    first_gain,
    first_shift,
    inner_weight,
    inner_bias,
    outer_weight,
    outer_bias,
    second_gain,
    second_shift,
    cotangent,
):
    items, block_rows, width = hidden.shape
    batch, seq = lax.axis_size("batch"), lax.axis_size("seq")
    me, group = lax.axis_index("seq"), lax.axis_index("batch")
    place = jnp.stack([me, group & 1, (group >> 1) & 1, (group >> 2) & 1]).astype(jnp.int32)
    high = inner_weight.shape[1]
    even = (batch, seq, width, high) == (8, SHARES, SIDE, 4 * SIDE)
    group_ids = pick(groups, me, 0)
    item_length = lax.dynamic_slice_in_dim(lengths, me, 1)

    got = exchange(entry_blocks(place, hidden, answer_flags, answer_embed))
    later = exchange(flagged_blocks(place, cotangent, answer_flags))
    acts = join_blocks(place, got, block_rows).reshape(items * block_rows, width)
    cotangent_item = join_blocks(place, later, block_rows).reshape(items * block_rows, width)
    flags = [block[block_rows, :block_rows] for block in later]
    flag_rows = jnp.zeros((items, block_rows), F32)
    for mask in range(items):
        flag_rows = lax.dynamic_update_index_in_dim(flag_rows, flags[mask].astype(F32), me ^ mask, 0)
    flags = flag_rows.reshape(1, items * block_rows)

    queries = (dot(acts, query_weight) + query_bias.astype(F32)).astype(BF16)
    keys = dot(acts, key_weight).astype(BF16)
    values = (dot(acts, value_weight) + value_bias.astype(F32)).astype(BF16)
    context, attention = attention_forward(queries, keys, values, group_ids, item_length)
    first_sum = acts.astype(F32) + dot(context, output_weight) + output_bias.astype(F32)
    gain_one, gain_two = first_gain.astype(F32), second_gain.astype(F32)
    settled, first_hat, first_inverse = norm_forward(first_sum, gain_one, first_shift.astype(F32))
    settled_low = settled.astype(BF16)
    inner = dot(settled_low, inner_weight) + inner_bias.astype(F32)
    active, slope = gate_parts(inner)
    active, slope = active.astype(BF16), slope.astype(BF16)
    second_sum = settled + dot(active, outer_weight) + outer_bias.astype(F32)
    output, second_hat, second_inverse = norm_forward(second_sum, gain_two, second_shift.astype(F32))

    upper = cotangent_item.astype(F32)
    d_second = norm_backward(upper, second_hat, second_inverse, gain_two)
    second_gain_gradient = jnp.sum(upper * second_hat, 0)
    second_shift_gradient = jnp.sum(upper, 0)
    branch_low = d_second.astype(BF16)
    outer_bias_gradient = jnp.sum(branch_low.astype(F32), 0)
    if even:
        send = tall_gradient(place, active, branch_low, False)
        keep = tall_gradient(place, active, branch_low, True)
        (outer_weight_gradient,) = scatter_pieces(place, send, keep, "tall")
    else:
        outer_weight_gradient = scatter(dot(active, branch_low, CONTRACT_FIRST))
    output = exchange(split_blocks(place, output.astype(BF16), items))
    output = join_blocks(place, output, block_rows)
    d_inner = (dot(branch_low, outer_weight, CONTRACT_LAST) * slope.astype(F32)).astype(BF16)
    inner_bias_gradient = jnp.sum(d_inner.astype(F32), 0)
    if even:
        send, keep = wide_gradient(place, settled_low, d_inner)
        (inner_weight_gradient,) = scatter_pieces(place, send, keep, "wide")
    else:
        inner_weight_gradient = scatter(dot(settled_low, d_inner, CONTRACT_FIRST))
    d_settled = d_second + dot(d_inner, inner_weight, CONTRACT_LAST)
    d_first = norm_backward(d_settled, first_hat, first_inverse, gain_one)
    first_gain_gradient = jnp.sum(d_settled * first_hat, 0)
    first_shift_gradient = jnp.sum(d_settled, 0)
    mixed_low = d_first.astype(BF16)
    output_bias_gradient = jnp.sum(mixed_low.astype(F32), 0)
    d_context = dot(mixed_low, output_weight, CONTRACT_LAST).astype(BF16)
    d_queries, d_keys, d_values = attention_backward(
        attention, queries, keys, values, context, d_context
    )
    d_entry = (
        d_first
        + dot(d_queries, query_weight, CONTRACT_LAST)
        + dot(d_keys, key_weight, CONTRACT_LAST)
        + dot(d_values, value_weight, CONTRACT_LAST)
    )
    input_gradient = exchange(split_blocks(place, d_entry.astype(BF16), items))
    input_gradient = join_blocks(place, input_gradient, block_rows)
    if even:
        send, keep = square_gradients(place, context, acts, mixed_low, d_queries, d_keys, d_values)
        narrow = scatter_pieces(place, send, keep, "square")
    else:
        narrow = jnp.concatenate(
            [
                dot(left, right, CONTRACT_FIRST).astype(BF16)
                for left, right in (
                    (context, mixed_low),
                    (acts, d_queries),
                    (acts, d_keys),
                    (acts, d_values),
                )
            ],
            1,
        )
        narrow = jnp.split(scatter(narrow), 4, 1)
    output_weight_gradient, query_weight_gradient, key_weight_gradient, value_weight_gradient = narrow
    by_flag = dot(jnp.concatenate([1.0 - flags, flags], 0), d_entry)
    pieces = scatter_vectors(
        jnp.concatenate(
            [
                by_flag,
                jnp.sum(d_queries.astype(F32), 0)[None],
                jnp.sum(d_values.astype(F32), 0)[None],
                output_bias_gradient[None],
                first_gain_gradient[None],
                first_shift_gradient[None],
                outer_bias_gradient[None],
                second_gain_gradient[None],
                second_shift_gradient[None],
                jnp.swapaxes(inner_bias_gradient.reshape(width, -1), 0, 1),
            ],
            0,
        )
    )
    return (
        output,
        input_gradient,
        pieces[:2],
        query_weight_gradient,
        pieces[2],
        key_weight_gradient,
        value_weight_gradient,
        pieces[3],
        output_weight_gradient,
        pieces[4],
        pieces[5],
        pieces[6],
        inner_weight_gradient,
        jnp.swapaxes(pieces[10:], 0, 1).reshape(-1),
        outer_weight_gradient,
        pieces[7],
        pieces[8],
        pieces[9],
    )


def solution(mesh):
    both = ("batch", "seq")
    in_specs = (
        (P("batch", "seq", None), P("batch", None), P("batch", "seq"), P("batch"))
        + (P(),) * 16
        + (P("batch", "seq", None),)
    )
    matrix, vector = P(both, None), P(both)
    out_specs = (
        P("batch", "seq", None),
        P("batch", "seq", None),
        P(None, both),
        matrix,
        vector,
        matrix,
        matrix,
        vector,
        matrix,
        vector,
        vector,
        vector,
        matrix,
        vector,
        matrix,
        vector,
        vector,
        vector,
    )
    return jax.shard_map(
        per_device, mesh=mesh, in_specs=in_specs, out_specs=out_specs, check_vma=False
    )
```

```python
import functools
import math

import jax
import jax.numpy as jnp
from jax import lax
from jax.experimental import pallas as pl
from jax.experimental.pallas import tpu as pltpu
from jax.sharding import PartitionSpec as P

HEAD_DIM = 64
LANES = 128
EPSILON = 1e-12
BF16 = jnp.bfloat16
F32 = jnp.float32

CONTRACT_LAST = (((1,), (1,)), ((), ()))
CONTRACT_FIRST = (((0,), (0,)), ((), ()))
GROUPS, SHARES, PIECE, SIDE = 4, 4, 96, 768


def dot(a, b, dims=(((1,), (0,)), ((), ()))):
    return lax.dot_general(a, b, dims, preferred_element_type=F32)


def low(*shape):
    return jax.ShapeDtypeStruct(shape, BF16)


def full(*shape):
    return jax.ShapeDtypeStruct(shape, F32)


def call(kernel, name, scalars, arrays, outs, limit=16, scratch=(), after=(), flops=1 << 33):
    count = len(scalars) + len(arrays)

    def body(*refs):
        kernel(*refs[:count], *refs[count + len(after) :])

    vmem = pl.BlockSpec(memory_space=pltpu.VMEM)
    single = not isinstance(outs, tuple)
    return pl.pallas_call(
        body,
        in_specs=[pl.BlockSpec(memory_space=pltpu.SMEM)] * len(scalars)
        + [vmem] * len(arrays)
        + [pl.BlockSpec(memory_space=pl.ANY)] * len(after),
        out_specs=vmem if single else (vmem,) * len(outs),
        out_shape=outs,
        scratch_shapes=list(scratch),
        compiler_params=pltpu.CompilerParams(vmem_limit_bytes=limit << 20),
        cost_estimate=pl.CostEstimate(flops=flops, bytes_accessed=1 << 20, transcendentals=0),
        name=name,
    )(*scalars, *arrays, *after)


def line(ref):
    return ref[...].astype(F32)[None]


def block_rows_of(place, mask, each):
    return pl.ds(pl.multiple_of((place[0] ^ mask) * each, each), each)


def entry_kernel(count, place, hidden, flags, embed, *outs):
    rows = hidden.shape[1]
    row = lax.broadcasted_iota(jnp.int32, (rows, rows), 0)
    column = lax.broadcasted_iota(jnp.int32, (rows, rows), 1)
    first, second = embed[0:1].astype(F32), embed[1:2].astype(F32)
    for mask in range(count):
        item = place[0] ^ mask
        flag = flags[pl.ds(item, 1), :].astype(F32)
        upright = jnp.sum(jnp.where(row == column, flag, 0.0), 1, keepdims=True)
        added = jnp.where(upright == 1.0, second, first)
        outs[mask][...] = (hidden[item].astype(F32) + added).astype(BF16)


def entry_blocks(place, hidden, flags, embed):
    count, rows, width = hidden.shape
    return call(
        functools.partial(entry_kernel, count),
        "entry_blocks",
        (place,),
        (hidden, flags, embed),
        (low(rows, width),) * count,
    )


def flagged_kernel(count, place, cotangent, flags, *outs):
    rows = cotangent.shape[1]
    for mask in range(count):
        item = place[0] ^ mask
        outs[mask][pl.ds(0, rows), :] = cotangent[item]
        outs[mask][pl.ds(rows, 16), :] = jnp.zeros((16, cotangent.shape[2]), BF16)
        flag = jnp.broadcast_to(flags[pl.ds(item, 1), :].astype(F32), (16, rows))
        outs[mask][pl.ds(rows, 16), pl.ds(0, rows)] = flag.astype(BF16)


def flagged_blocks(place, cotangent, flags, after):
    count, rows, width = cotangent.shape
    return call(
        functools.partial(flagged_kernel, count),
        "flagged_blocks",
        (place,),
        (cotangent, flags),
        (low(rows + 16, width),) * count,
        after=after,
    )


def join_kernel(count, place, *refs):
    for mask in range(count):
        refs[count][place[0] ^ mask] = refs[mask][...]


def join_blocks(place, blocks):
    return call(
        functools.partial(join_kernel, len(blocks)),
        "join_blocks",
        (place,),
        blocks,
        low(len(blocks), *blocks[0].shape),
    )


def swap_pairs(array, axis, mask):
    size = lax.axis_size(axis)
    return lax.ppermute(array, axis, [(i, i ^ mask) for i in range(size)])


def pick(array, index, dim):
    return lax.dynamic_index_in_dim(array, index, dim, keepdims=False)


def exchange(blocks):
    order = sorted(range(1, len(blocks)), key=lambda mask: mask < 2)
    got = {mask: swap_pairs(blocks[mask], "seq", mask) for mask in order}
    return [blocks[0]] + [got[mask] for mask in range(1, len(blocks))]


def total(parts):
    result = parts[0].astype(F32)
    for part in parts[1:]:
        result = result + part.astype(F32)
    return result


def halve(parts, dim, axis, bit, dtype=BF16):
    mine = (lax.axis_index(axis) >> bit) & 1
    sent = total([pick(part, 1 - mine, dim) for part in parts]).astype(dtype)
    got = swap_pairs(sent, axis, 1 << bit)
    return [pick(part, mine, dim) for part in parts] + [got]


def scatter(gradient):
    batch, seq = lax.axis_size("batch"), lax.axis_size("seq")
    rows, columns = gradient.shape
    batch_bits, seq_bits = batch.bit_length() - 1, seq.bit_length() - 1
    each = rows // (batch * seq)
    shape = (2,) * (batch_bits + seq_bits) + (each, columns)
    parts = [gradient.astype(BF16).reshape(shape)]
    parts = halve(parts, batch_bits - 1, "batch", 0)
    ways = []
    for way in range(2):
        half = [
            lax.slice_in_dim(part, way * (columns // 2), (way + 1) * (columns // 2), axis=part.ndim - 1)
            for part in parts
        ]
        bits = list(range(1, batch_bits))
        if way:
            bits = bits[::-1]
        left = list(range(batch_bits - 1, 0, -1))
        for bit in bits:
            dim = left.index(bit)
            half = halve(half, dim, "batch", bit)
            left.remove(bit)
        ways.append(half)
    parts = [jnp.concatenate([a, b], -1) for a, b in zip(*ways)]
    for bit in range(seq_bits):
        parts = halve(parts, seq_bits - 1 - bit, "seq", bit)
    return total(parts)


def norm_parts(values):
    centre = values - jnp.mean(values, -1, keepdims=True)
    inverse = lax.rsqrt(jnp.mean(centre * centre, -1, keepdims=True) + EPSILON)
    return centre * inverse, inverse


def norm_back(upper, hat, inverse, gain):
    g = upper * gain
    return inverse * (
        g - jnp.mean(g, -1, keepdims=True) - hat * jnp.mean(g * hat, -1, keepdims=True)
    )


def gate_parts(u):
    share = 0.5 + 0.5 * lax.erf(u * 0.7071067811865476)
    return u * share, share + u * (jnp.exp(-0.5 * u * u) * 0.3989422804014327)


def attend_kernel(count, place, lengths, groups, *refs):
    blocks = refs[:count]
    query_weight, query_bias, key_weight, value_weight, value_bias = refs[count : count + 5]
    acts, q_ref, k_ref, v_ref, o_ref, e_ref, inverse_ref, bias = refs[count + 5 :]
    rows, width = acts.shape
    each = rows // count
    for mask in range(count):
        acts[block_rows_of(place, mask, each), :] = blocks[mask][...]
    ids = groups[pl.ds(place[0], 1), :].astype(F32)
    key_place = lax.broadcasted_iota(jnp.int32, (1, rows), 1)
    key_ids = jnp.where(key_place < lengths[place[0]], ids, 1e9)
    upright = jnp.transpose(jnp.broadcast_to(ids, (8, rows)))[:, :1]
    bias[...] = jnp.where(key_ids <= upright, 0.0, -1e30)
    lane = lax.broadcasted_iota(jnp.int32, (rows, LANES), 1) // HEAD_DIM
    tile = 2 * LANES
    for start in range(0, width, tile):
        part = slice(start, start + tile)
        x = acts[...]
        q = (dot(x, query_weight[:, part]) + line(query_bias)[:, part]).astype(BF16)
        k = dot(x, key_weight[:, part]).astype(BF16)
        v = (dot(x, value_weight[:, part]) + line(value_bias)[:, part]).astype(BF16)
        q_ref[:, part] = q
        k_ref[:, part] = k
        v_ref[:, part] = v
        q = q * jnp.asarray(1.0 / math.sqrt(HEAD_DIM), BF16)
        for pair in range(tile // LANES):
            at = slice(pair * LANES, (pair + 1) * LANES)
            q2, k2, v2 = q[:, at], k[:, at], v[:, at]
            sums = []
            for head in range(2):
                mine = lane == head
                s = dot(jnp.where(mine, q2, jnp.zeros_like(q2)), k2, CONTRACT_LAST) + bias[...]
                e = jnp.exp(s - jnp.max(s, -1, keepdims=True)).astype(BF16)
                e_ref[(start + pair * LANES) // HEAD_DIM + head] = e
                sums.append(dot(e, jnp.where(mine, v2, jnp.ones_like(v2))))
            top = jnp.where(lane == 0, sums[0], sums[1])
            under = pltpu.roll(jnp.where(lane == 0, sums[1], sums[0]), HEAD_DIM, 1)
            inverse = 1.0 / under
            at = slice(start + pair * LANES, start + (pair + 1) * LANES)
            inverse_ref[:, at] = inverse
            o_ref[:, at] = (top * inverse).astype(BF16)


def attend(place, lengths, groups, blocks, weights):
    each, width = blocks[0].shape
    rows = len(blocks) * each
    wide = low(rows, width)
    return call(
        functools.partial(attend_kernel, len(blocks)),
        "attend",
        (place, lengths),
        (groups, *blocks, *weights),
        (wide, wide, wide, wide, wide, low(width // HEAD_DIM, rows, rows), full(rows, width)),
        scratch=[pltpu.VMEM((rows, rows), F32)],
    )


def attend_back_kernel(e_ref, q_ref, k_ref, v_ref, o_ref, inverse_ref, do_ref, dq_ref, dk_ref, dv_ref):
    rows, width = q_ref.shape
    scale = 1.0 / math.sqrt(HEAD_DIM)
    lane = lax.broadcasted_iota(jnp.int32, (rows, LANES), 1) // HEAD_DIM
    for pair in range(width // LANES):
        at = slice(pair * LANES, (pair + 1) * LANES)
        q, k, v = q_ref[:, at], k_ref[:, at], v_ref[:, at]
        do = do_ref[:, at].astype(F32) * inverse_ref[:, at]
        weighed = do * o_ref[:, at].astype(F32)
        do = do.astype(BF16)
        q_up, do_up = jnp.transpose(q), jnp.transpose(do)
        dq, dk, dv = [], [], []
        for head in range(2):
            mine = lane == head
            part = slice(head * HEAD_DIM, (head + 1) * HEAD_DIM)
            row_dot = jnp.sum(jnp.where(mine, weighed, 0.0), -1, keepdims=True)
            e = e_ref[2 * pair + head]
            d = dot(jnp.where(mine, do, jnp.zeros_like(do)), v, CONTRACT_LAST) - row_dot
            ds = (e.astype(F32) * d).astype(BF16)
            dq.append(dot(ds, k))
            dk.append(dot(q_up[part], ds))
            dv.append(dot(do_up[part], e))
        dq_ref[:, at] = (jnp.where(lane == 0, dq[0], dq[1]) * scale).astype(BF16)
        dk_ref[:, at] = (jnp.transpose(jnp.concatenate(dk, 0)) * scale).astype(BF16)
        dv_ref[:, at] = jnp.transpose(jnp.concatenate(dv, 0)).astype(BF16)


def attend_back(arrays, after):
    wide = low(*arrays[1].shape)
    return call(
        attend_back_kernel, "attend_back", (), arrays, (wide, wide, wide), after=after
    )


def feed_kernel(count, place, *refs):
    (acts, context, output_weight, output_bias, first_gain, first_shift, inner_weight, inner_bias) = refs[:8]
    outer_weight, outer_bias, second_gain, second_shift = refs[8:12]
    settled_low, hat_ref, inverse_ref, active_ref, slope_ref, hat_two, inverse_two = refs[12:19]
    outs = refs[19 : 19 + count]
    acc = refs[19 + count]
    rows, high = active_ref.shape
    hat, inverse = norm_parts(
        acts[...].astype(F32) + dot(context[...], output_weight[...]) + line(output_bias)
    )
    hat_ref[...] = hat.astype(BF16)
    inverse_ref[...] = jnp.broadcast_to(inverse, inverse_ref.shape)
    settled = hat * line(first_gain) + line(first_shift)
    settled_low[...] = settled.astype(BF16)
    acc[...] = settled + line(outer_bias)
    tile = 4 * LANES
    for start in range(0, high, tile):
        part = slice(start, start + tile)
        inner = dot(settled_low[...], inner_weight[:, part]) + line(inner_bias)[:, part]
        active, slope = gate_parts(inner)
        active_ref[:, part] = active.astype(BF16)
        slope_ref[:, part] = slope.astype(BF16)
    acc[...] += dot(active_ref[...], outer_weight[...])
    each = rows // count
    gain, shift = line(second_gain), line(second_shift)
    for mask in range(count):
        own = block_rows_of(place, mask, each)
        hat, inverse = norm_parts(acc[own, :])
        outs[mask][...] = (hat * gain + shift).astype(BF16)
        hat_two[own, :] = hat
        inverse_two[own, :] = jnp.broadcast_to(inverse, (each, LANES))


def feed(place, acts, context, weights, count):
    rows, width = acts.shape
    high = weights[4].shape[1]
    wide = low(rows, width)
    return call(
        functools.partial(feed_kernel, count),
        "feed",
        (place,),
        (acts, context, *weights),
        (
            wide,
            wide,
            full(rows, LANES),
            low(rows, high),
            low(rows, high),
            full(rows, width),
            full(rows, LANES),
        )
        + (low(rows // count, width),) * count,
        scratch=[pltpu.VMEM((rows, width), F32)],
    )


def turn_kernel(count, place, hat_two, inverse_two, second_gain, *refs):
    cotangents = refs[:count]
    d_second, branch, sums = refs[count:]
    each = hat_two.shape[0] // count
    gain = line(second_gain)
    totals = [0.0, 0.0, 0.0]
    for mask in range(count):
        own = block_rows_of(place, mask, each)
        hat = hat_two[own, :]
        upper = cotangents[mask][pl.ds(0, each), :].astype(F32)
        d = norm_back(upper, hat, inverse_two[own, :1], gain)
        d_low = d.astype(BF16)
        d_second[own, :] = d
        branch[own, :] = d_low
        for i, term in enumerate((d_low.astype(F32), upper * hat, upper)):
            totals[i] = totals[i] + jnp.sum(term, 0, keepdims=True)
    for i in range(3):
        sums[i : i + 1, :] = totals[i]


def turn(place, hat_two, inverse_two, second_gain, cotangents):
    rows, width = hat_two.shape
    return call(
        functools.partial(turn_kernel, len(cotangents)),
        "turn",
        (place,),
        (hat_two, inverse_two, second_gain, *cotangents),
        (full(rows, width), low(rows, width), full(8, width)),
    )


def feed_back_kernel(
    branch,
    outer_weight,
    slope,
    inner_weight,
    d_second,
    hat_ref,
    inverse_ref,
    first_gain,
    output_weight,
    turn_sums,
    d_inner_ref,
    d_first_ref,
    mixed,
    d_context,
    sums,
    acc,
):
    rows, high = slope.shape
    width = acc.shape[1]
    tile = 4 * LANES
    for start in range(0, high, tile):
        part = slice(start, start + tile)
        d_active = dot(branch[...], outer_weight[part, :], CONTRACT_LAST)
        d_inner = (d_active * slope[:, part].astype(F32)).astype(BF16)
        d_inner_ref[:, part] = d_inner
        partial = jnp.sum(d_inner.astype(F32), 0, keepdims=True)
        for lane in range(start, start + tile, LANES):
            row = 6 + lane // width
            sums[row : row + 1, lane % width : lane % width + LANES] = partial[:, lane - start : lane - start + LANES]
    acc[...] = d_second[...] + dot(d_inner_ref[...], inner_weight[...], CONTRACT_LAST)
    parts = 4
    totals = [0.0, 0.0, 0.0]
    gain = line(first_gain)
    for part in range(parts):
        own = slice(part * (rows // parts), (part + 1) * (rows // parts))
        upper = acc[own, :]
        hat = hat_ref[own, :].astype(F32)
        d = norm_back(upper, hat, inverse_ref[own, :1], gain)
        d_low = d.astype(BF16)
        d_first_ref[own, :] = d
        mixed[own, :] = d_low
        for i, term in enumerate((d_low.astype(F32), upper * hat, upper)):
            totals[i] = totals[i] + jnp.sum(term, 0, keepdims=True)
    for i in range(3):
        sums[i : i + 1, :] = totals[i]
    sums[3:6, :] = turn_sums[0:3, :]
    d_context[...] = dot(mixed[...], output_weight[...], CONTRACT_LAST).astype(BF16)


def feed_back(arrays, after):
    rows, width = arrays[0].shape
    high = arrays[2].shape[1]
    wide = low(rows, width)
    return call(
        feed_back_kernel,
        "feed_back",
        (),
        arrays,
        (low(rows, high), full(rows, width), wide, wide, full(16, width)),
        scratch=[pltpu.VMEM((rows, width), F32)],
        after=after,
    )


def entry_back_kernel(count, place, d_first, dq, dk, dv, wq, wk, wv, early_sums, *refs):
    flagged, outs, sums, acc = refs[:count], refs[count : 2 * count], refs[2 * count], refs[2 * count + 1]
    each = dq.shape[0] // count
    acc[...] = (
        d_first[...]
        + dot(dq[...], wq[...], CONTRACT_LAST)
        + dot(dk[...], wk[...], CONTRACT_LAST)
        + dot(dv[...], wv[...], CONTRACT_LAST)
    )
    by_flag = [0.0, 0.0]
    for mask in range(count):
        d = acc[block_rows_of(place, mask, each), :].astype(BF16)
        outs[mask][...] = d
        flag = flagged[mask][pl.ds(each, 16), pl.ds(0, each)]
        by_flag[0] = by_flag[0] + dot(1 - flag, d)
        by_flag[1] = by_flag[1] + dot(flag, d)
    sums[0:10, :] = early_sums[0:10, :]
    sums[10:11, :] = by_flag[0][:1]
    sums[11:12, :] = by_flag[1][:1]
    sums[12:13, :] = jnp.sum(dq[...].astype(F32), 0, keepdims=True)
    sums[13:14, :] = jnp.sum(dv[...].astype(F32), 0, keepdims=True)
    sums[14:16, :] = jnp.zeros((2, sums.shape[1]), F32)


def entry_back(place, arrays, flagged, after):
    rows, width = arrays[1].shape
    count = len(flagged)
    return call(
        functools.partial(entry_back_kernel, count),
        "entry_back",
        (place,),
        (*arrays, *flagged),
        (low(rows // count, width),) * count + (full(16, width),),
        scratch=[pltpu.VMEM((rows, width), F32)],
        after=after,
    )


def tall_gradient_kernel(keep, place, left, right, out):
    rows = left.shape[1] // GROUPS // 2
    core = place[1] if keep else 1 - place[1]
    for group in range(GROUPS):
        part = pl.ds(pl.multiple_of((2 * group + core) * rows, LANES), rows)
        piece = dot(left[:, part], right[...], CONTRACT_FIRST)
        out[group] = piece.reshape(out.shape[1:]).astype(BF16)


def tall_gradient(place, left, right, keep, after=()):
    return call(
        functools.partial(tall_gradient_kernel, keep),
        "tall_gradient",
        (place,),
        (left, right),
        low(GROUPS, SHARES, PIECE, SIDE),
        after=after,
    )


def stack_pieces(place, totals, send, keep, start):
    each = SIDE // (GROUPS * SHARES * 2)
    for out, core in ((send, 1 - place[1]), (keep, place[1])):
        for group in range(GROUPS):
            for share in range(SHARES):
                row = pl.multiple_of((2 * group + core) * (SHARES * each) + share * each, 8)
                piece = jnp.concatenate([t[pl.ds(row, each), :] for t in totals], 0)
                out[group, share, start : start + piece.shape[0], :] = piece.astype(BF16)


def wide_gradient_kernel(place, left, right, send, keep, first, second):
    for half in range(2):
        start = 2 * half * SIDE
        first[...] = dot(left[...], right[:, start : start + SIDE], CONTRACT_FIRST)
        second[...] = dot(left[...], right[:, start + SIDE : start + 2 * SIDE], CONTRACT_FIRST)
        stack_pieces(place, (first, second), send, keep, half * PIECE // 2)


def wide_gradient(place, left, right):
    piece = low(GROUPS, SHARES, PIECE, SIDE)
    return call(
        wide_gradient_kernel,
        "wide_gradient",
        (place,),
        (left, right),
        (piece, piece),
        scratch=[pltpu.VMEM((SIDE, SIDE), F32)] * 2,
    )


def square_gradients_kernel(place, context, acts, mixed, dq, dk, dv, send, keep, first, second):
    first[...] = dot(context[...], mixed[...], CONTRACT_FIRST)
    second[...] = dot(acts[...], dq[...], CONTRACT_FIRST)
    stack_pieces(place, (first, second), send, keep, 0)
    first[...] = dot(acts[...], dk[...], CONTRACT_FIRST)
    second[...] = dot(acts[...], dv[...], CONTRACT_FIRST)
    stack_pieces(place, (first, second), send, keep, PIECE // 2)


def square_gradients(place, arrays, after):
    piece = low(GROUPS, SHARES, PIECE, SIDE)
    return call(
        square_gradients_kernel,
        "square_gradients",
        (place,),
        arrays,
        (piece, piece),
        scratch=[pltpu.VMEM((SIDE, SIDE), F32)] * 2,
        after=after,
    )


def first_sums_kernel(place, keep, got, send_a, send_b):
    side = SIDE // 2
    for i in range(2):
        a, b = 2 * i + 1 - place[2], 2 * (1 - place[3]) + i
        send_a[i] = total([keep[a, :, :, :side], got[a, :, :, :side]]).astype(BF16)
        send_b[i] = total([keep[b, :, :, side:], got[b, :, :, side:]]).astype(BF16)


def first_sums(place, keep, got, after=()):
    half = low(2, SHARES, PIECE, SIDE // 2)
    return call(first_sums_kernel, "first_sums", (place,), (keep, got), (half, half), after=after)


def second_sums_kernel(place, keep, got, from_x, from_y, send_a, send_b):
    side = SIDE // 2
    x, y = place[2], place[3]
    a, b = 2 * (1 - y) + x, 2 * y + 1 - x
    send_a[...] = total([keep[a, :, :, :side], got[a, :, :, :side], from_x[1 - y]]).astype(BF16)
    send_b[...] = total([keep[b, :, :, side:], got[b, :, :, side:], from_y[1 - x]]).astype(BF16)


def second_sums(place, keep, got, from_x, from_y, after=()):
    quarter = low(SHARES, PIECE, SIDE // 2)
    return call(
        second_sums_kernel,
        "second_sums",
        (place,),
        (keep, got, from_x, from_y),
        (quarter, quarter),
        after=after,
    )


def third_sums_kernel(place, keep, got, from_x, from_y, then_y, then_x, send, kept):
    side = SIDE // 2
    x, y, bit = place[2], place[3], place[0] & 1
    own = 2 * y + x
    for out, share_bit in ((send, 1 - bit), (kept, bit)):
        for high in range(SHARES // 2):
            share = 2 * high + share_bit
            out[high, :, :side] = total(
                [keep[own, share, :, :side], got[own, share, :, :side], from_x[y, share], then_y[share]]
            ).astype(out.dtype)
            out[high, :, side:] = total(
                [keep[own, share, :, side:], got[own, share, :, side:], from_y[x, share], then_x[share]]
            ).astype(out.dtype)


def third_sums(place, arrays, after=()):
    out = (SHARES // 2, PIECE, SIDE)
    return call(third_sums_kernel, "third_sums", (place,), arrays, (low(*out), full(*out)), after=after)


def fourth_sums_kernel(place, kept, got, send):
    other = 1 - (place[0] >> 1)
    send[...] = total([kept[other], got[other]]).astype(BF16)


def last_sums_kernel(form, place, kept, got, last, *outs):
    mine = place[0] >> 1
    result = total([kept[mine], got[mine], last[...]])
    each = PIECE // 4
    if form == "tall":
        outs[0][...] = result
    else:
        for i in range(4):
            rows = result[i * each : (i + 1) * each]
            if form == "wide":
                outs[0][:, i * SIDE : (i + 1) * SIDE] = rows
            else:
                outs[i][...] = rows


def last_sums(place, kept, got, last, form):
    each = PIECE // 4
    shapes = {"tall": [(PIECE, SIDE)], "wide": [(each, 4 * SIDE)], "square": [(each, SIDE)] * 4}[form]
    return call(
        functools.partial(last_sums_kernel, form),
        "last_sums",
        (place,),
        (kept, got, last),
        tuple(full(*s) for s in shapes),
    )


class Halving:
    def __init__(self, place, send, keep):
        self.place, self.keep = place, keep
        self.got = swap_pairs(send, "batch", 1)

    def first(self, after=()):
        self.to = first_sums(self.place, self.keep, self.got, after)
        self.from_x, self.from_y = swap_pairs(self.to[0], "batch", 2), swap_pairs(self.to[1], "batch", 4)

    def second(self, after=()):
        self.then = second_sums(self.place, self.keep, self.got, self.from_x, self.from_y, after)
        self.then_y, self.then_x = swap_pairs(self.then[0], "batch", 4), swap_pairs(self.then[1], "batch", 2)

    def third(self, after=()):
        self.send, self.kept = third_sums(
            self.place,
            (self.keep, self.got, self.from_x, self.from_y, self.then_y, self.then_x),
            after,
        )
        self.pair = swap_pairs(self.send, "seq", 1)

    def fourth(self, after=()):
        self.sent = call(
            fourth_sums_kernel,
            "fourth_sums",
            (self.place,),
            (self.kept, self.pair),
            low(PIECE, SIDE),
            after=after,
        )
        self.others = swap_pairs(self.sent, "seq", 2)

    def last(self, form):
        return last_sums(self.place, self.kept, self.pair, self.others, form)


def add_everywhere(array):
    for axis in ("batch", "seq"):
        for bit in range(lax.axis_size(axis).bit_length() - 1):
            array = array + swap_pairs(array, axis, 1 << bit)
    return array


def per_device(
    hidden,
    groups,
    answer_flags,
    lengths,
    answer_embed,
    query_weight,
    query_bias,
    key_weight,
    value_weight,
    value_bias,
    output_weight,
    output_bias,
    first_gain,
    first_shift,
    inner_weight,
    inner_bias,
    outer_weight,
    outer_bias,
    second_gain,
    second_shift,
    cotangent,
):
    items, block_rows, width = hidden.shape
    batch, seq = lax.axis_size("batch"), lax.axis_size("seq")
    me, group = lax.axis_index("seq"), lax.axis_index("batch")
    place = jnp.stack([me, group & 1, (group >> 1) & 1, (group >> 2) & 1]).astype(jnp.int32)
    high = inner_weight.shape[1]
    even = (batch, seq, width, high) == (8, SHARES, SIDE, 4 * SIDE)

    blocks = entry_blocks(place, hidden, answer_flags, answer_embed)
    got = exchange(blocks)
    flagged = exchange(flagged_blocks(place, cotangent, answer_flags, got[1:]))
    acts, queries, keys, values, context, exponents, inverse_sums = attend(
        place, lengths, groups, got, (query_weight, query_bias, key_weight, value_weight, value_bias)
    )
    settled, hat, inverse, active, slope, hat_two, inverse_two, *output = feed(
        place,
        acts,
        context,
        (
            output_weight,
            output_bias,
            first_gain,
            first_shift,
            inner_weight,
            inner_bias,
            outer_weight,
            outer_bias,
            second_gain,
            second_shift,
        ),
        items,
    )
    d_second, branch, sums = turn(place, hat_two, inverse_two, second_gain, flagged)
    if even:
        send = tall_gradient(place, active, branch, False)
        keep = tall_gradient(place, active, branch, True, (send,))
        outer = Halving(place, send, keep)
        outer.first()
        after = (outer.to[0],)
    else:
        outer_weight_gradient = scatter(dot(active, branch, CONTRACT_FIRST))
        after = ()
    output = join_blocks(place, exchange(output))
    d_inner, d_first, mixed, d_context, sums = feed_back(
        (
            branch,
            outer_weight,
            slope,
            inner_weight,
            d_second,
            hat,
            inverse,
            first_gain,
            output_weight,
            sums,
        ),
        after,
    )
    if even:
        send, keep = wide_gradient(place, settled, d_inner)
        inner = Halving(place, send, keep)
        after = (send, output)
    else:
        inner_weight_gradient = scatter(dot(settled, d_inner, CONTRACT_FIRST))
    d_queries, d_keys, d_values = attend_back(
        (exponents, queries, keys, values, context, inverse_sums, d_context), after
    )
    if even:
        outer.second((d_queries,))
        inner.first((d_queries,))
        send, keep = square_gradients(
            place,
            (context, acts, mixed, d_queries, d_keys, d_values),
            (outer.then[0], inner.to[0]),
        )
        narrow = Halving(place, send, keep)
        after = (send,)
    *input_gradient, sums = entry_back(
        place,
        (d_first, d_queries, d_keys, d_values, query_weight, key_weight, value_weight, sums),
        flagged,
        after,
    )
    back = exchange(input_gradient)
    if even:
        narrow.first((input_gradient[0],))
        outer.third((narrow.to[0],))
        inner.second((outer.send,))
        outer.fourth((inner.then[0],))
        inner.third((outer.sent,))
        narrow.second((inner.send,))
        inner.fourth((narrow.then[0],))
        narrow.third((inner.sent,))
        narrow.fourth()
        (outer_weight_gradient,) = outer.last("tall")
        (inner_weight_gradient,) = inner.last("wide")
        narrow = narrow.last("square")
    else:
        narrow = jnp.concatenate(
            [
                dot(left, right, CONTRACT_FIRST).astype(BF16)
                for left, right in (
                    (context, mixed),
                    (acts, d_queries),
                    (acts, d_keys),
                    (acts, d_values),
                )
            ],
            1,
        )
        narrow = jnp.split(scatter(narrow), 4, 1)
    output_weight_gradient, query_weight_gradient, key_weight_gradient, value_weight_gradient = narrow
    sums = add_everywhere(sums)
    index = group * seq + me
    each = width // (batch * seq)
    pieces = lax.dynamic_slice_in_dim(sums, index * each, each, 1)
    inner_bias_gradient = lax.dynamic_slice_in_dim(
        sums[6:10].reshape(-1), index * 4 * each, 4 * each, 0
    )
    input_gradient = join_blocks(place, back)
    return (
        output,
        input_gradient,
        pieces[10:12],
        query_weight_gradient,
        pieces[12],
        key_weight_gradient,
        value_weight_gradient,
        pieces[13],
        output_weight_gradient,
        pieces[0],
        pieces[1],
        pieces[2],
        inner_weight_gradient,
        inner_bias_gradient,
        outer_weight_gradient,
        pieces[3],
        pieces[4],
        pieces[5],
    )


def solution(mesh):
    both = ("batch", "seq")
    in_specs = (
        (P("batch", "seq", None), P("batch", None), P("batch", "seq"), P("batch"))
        + (P(),) * 16
        + (P("batch", "seq", None),)
    )
    matrix, vector = P(both, None), P(both)
    out_specs = (
        P("batch", "seq", None),
        P("batch", "seq", None),
        P(None, both),
        matrix,
        vector,
        matrix,
        matrix,
        vector,
        matrix,
        vector,
        vector,
        vector,
        matrix,
        vector,
        matrix,
        vector,
        vector,
        vector,
    )
    return jax.shard_map(
        per_device, mesh=mesh, in_specs=in_specs, out_specs=out_specs, check_vma=False
    )
```

```python
import functools
import math

import jax
import jax.numpy as jnp
from jax import lax
from jax.experimental import pallas as pl
from jax.experimental.pallas import tpu as pltpu
from jax.sharding import PartitionSpec as P

HEAD_DIM = 64
LANES = 128
EPSILON = 1e-12
BF16 = jnp.bfloat16
F32 = jnp.float32

CONTRACT_LAST = (((1,), (1,)), ((), ()))
CONTRACT_FIRST = (((0,), (0,)), ((), ()))
GROUPS, SHARES, PIECE, SIDE = 4, 4, 96, 768
MICROSECOND = 1150000000


def dot(a, b, dims=(((1,), (0,)), ((), ()))):
    return lax.dot_general(a, b, dims, preferred_element_type=F32)


def low(*shape):
    return jax.ShapeDtypeStruct(shape, BF16)


def full(*shape):
    return jax.ShapeDtypeStruct(shape, F32)


def call(kernel, name, scalars, arrays, outs, limit=16, scratch=(), after=(), cost=4.0):
    count = len(scalars) + len(arrays)

    def body(*refs):
        kernel(*refs[:count], *refs[count + len(after) :])

    single = not isinstance(outs, tuple)
    vmem = pl.BlockSpec(memory_space=pltpu.VMEM)
    return pl.pallas_call(
        body,
        in_specs=[pl.BlockSpec(memory_space=pltpu.SMEM)] * len(scalars)
        + [vmem] * len(arrays)
        + [pl.BlockSpec(memory_space=pl.ANY)] * len(after),
        out_specs=vmem if single else (vmem,) * len(outs),
        out_shape=outs,
        scratch_shapes=list(scratch),
        compiler_params=pltpu.CompilerParams(vmem_limit_bytes=limit << 20),
        cost_estimate=pl.CostEstimate(flops=int(cost * MICROSECOND), bytes_accessed=1 << 16, transcendentals=0),
        name=name,
    )(*scalars, *arrays, *after)


def line(ref):
    return ref[...].astype(F32)[None]


def block_rows_of(place, mask, each):
    return pl.ds(pl.multiple_of((place[0] ^ mask) * each, each), each)


def entry_kernel(count, place, hidden, flags, embed, *outs):
    rows = hidden.shape[1]
    row = lax.broadcasted_iota(jnp.int32, (rows, rows), 0)
    column = lax.broadcasted_iota(jnp.int32, (rows, rows), 1)
    first, second = embed[0:1].astype(F32), embed[1:2].astype(F32)
    for mask in range(count):
        item = place[0] ^ mask
        flag = flags[pl.ds(item, 1), :].astype(F32)
        upright = jnp.sum(jnp.where(row == column, flag, 0.0), 1, keepdims=True)
        added = jnp.where(upright == 1.0, second, first)
        outs[mask][...] = (hidden[item].astype(F32) + added).astype(BF16)


def entry_blocks(place, hidden, flags, embed):
    count, rows, width = hidden.shape
    return call(
        functools.partial(entry_kernel, count),
        "entry_blocks",
        (place,),
        (hidden, flags, embed),
        (low(rows, width),) * count,
    )


def flagged_kernel(count, place, cotangent, flags, *outs):
    rows = cotangent.shape[1]
    for mask in range(count):
        item = place[0] ^ mask
        outs[mask][pl.ds(0, rows), :] = cotangent[item]
        outs[mask][pl.ds(rows, 16), :] = jnp.zeros((16, cotangent.shape[2]), BF16)
        flag = jnp.broadcast_to(flags[pl.ds(item, 1), :].astype(F32), (16, rows))
        outs[mask][pl.ds(rows, 16), pl.ds(0, rows)] = flag.astype(BF16)


def flagged_blocks(place, cotangent, flags, after):
    count, rows, width = cotangent.shape
    return call(
        functools.partial(flagged_kernel, count),
        "flagged_blocks",
        (place,),
        (cotangent, flags),
        (low(rows + 16, width),) * count,
        after=after,
    )


def join_kernel(count, place, *refs):
    for mask in range(count):
        refs[count][place[0] ^ mask] = refs[mask][...]


def join_blocks(place, blocks, after=()):
    return call(
        functools.partial(join_kernel, len(blocks)),
        "join_blocks",
        (place,),
        blocks,
        low(len(blocks), *blocks[0].shape),
        after=after,
        cost=0.5,
    )


def swap_pairs(array, axis, mask):
    size = lax.axis_size(axis)
    return lax.ppermute(array, axis, [(i, i ^ mask) for i in range(size)])


def pick(array, index, dim):
    return lax.dynamic_index_in_dim(array, index, dim, keepdims=False)


def exchange(blocks):
    order = sorted(range(1, len(blocks)), key=lambda mask: mask < 2)
    got = {mask: swap_pairs(blocks[mask], "seq", mask) for mask in order}
    return [blocks[0]] + [got[mask] for mask in range(1, len(blocks))]


def total(parts):
    result = parts[0].astype(F32)
    for part in parts[1:]:
        result = result + part.astype(F32)
    return result


def halve(parts, dim, axis, bit, dtype=BF16):
    mine = (lax.axis_index(axis) >> bit) & 1
    sent = total([pick(part, 1 - mine, dim) for part in parts]).astype(dtype)
    got = swap_pairs(sent, axis, 1 << bit)
    return [pick(part, mine, dim) for part in parts] + [got]


def scatter(gradient):
    batch, seq = lax.axis_size("batch"), lax.axis_size("seq")
    rows, columns = gradient.shape
    batch_bits, seq_bits = batch.bit_length() - 1, seq.bit_length() - 1
    each = rows // (batch * seq)
    shape = (2,) * (batch_bits + seq_bits) + (each, columns)
    parts = [gradient.astype(BF16).reshape(shape)]
    parts = halve(parts, batch_bits - 1, "batch", 0)
    ways = []
    for way in range(2):
        half = [
            lax.slice_in_dim(part, way * (columns // 2), (way + 1) * (columns // 2), axis=part.ndim - 1)
            for part in parts
        ]
        bits = list(range(1, batch_bits))
        if way:
            bits = bits[::-1]
        left = list(range(batch_bits - 1, 0, -1))
        for bit in bits:
            dim = left.index(bit)
            half = halve(half, dim, "batch", bit)
            left.remove(bit)
        ways.append(half)
    parts = [jnp.concatenate([a, b], -1) for a, b in zip(*ways)]
    for bit in range(seq_bits):
        parts = halve(parts, seq_bits - 1 - bit, "seq", bit)
    return total(parts)


def norm_parts(values):
    centre = values - jnp.mean(values, -1, keepdims=True)
    inverse = lax.rsqrt(jnp.mean(centre * centre, -1, keepdims=True) + EPSILON)
    return centre * inverse, inverse


def norm_back(upper, hat, inverse, gain):
    g = upper * gain
    return inverse * (
        g - jnp.mean(g, -1, keepdims=True) - hat * jnp.mean(g * hat, -1, keepdims=True)
    )


def gate_parts(u):
    share = 0.5 + 0.5 * lax.erf(u * 0.7071067811865476)
    return u * share, share + u * (jnp.exp(-0.5 * u * u) * 0.3989422804014327)


def attend_kernel(count, place, lengths, groups, *refs):
    blocks = refs[:count]
    query_weight, query_bias, key_weight, value_weight, value_bias = refs[count : count + 5]
    acts, q_ref, k_ref, v_ref, o_ref, e_ref, inverse_ref, bias = refs[count + 5 :]
    rows, width = acts.shape
    each = rows // count
    for mask in range(count):
        acts[block_rows_of(place, mask, each), :] = blocks[mask][...]
    ids = groups[pl.ds(place[0], 1), :].astype(F32)
    key_place = lax.broadcasted_iota(jnp.int32, (1, rows), 1)
    key_ids = jnp.where(key_place < lengths[place[0]], ids, 1e9)
    upright = jnp.transpose(jnp.broadcast_to(ids, (8, rows)))[:, :1]
    bias[...] = jnp.where(key_ids <= upright, 0.0, -1e30)
    lane = lax.broadcasted_iota(jnp.int32, (rows, LANES), 1) // HEAD_DIM
    tile = 2 * LANES
    for start in range(0, width, tile):
        part = slice(start, start + tile)
        x = acts[...]
        q = (dot(x, query_weight[:, part]) + line(query_bias)[:, part]).astype(BF16)
        k = dot(x, key_weight[:, part]).astype(BF16)
        v = (dot(x, value_weight[:, part]) + line(value_bias)[:, part]).astype(BF16)
        q_ref[:, part] = q
        k_ref[:, part] = k
        v_ref[:, part] = v
        q = q * jnp.asarray(1.0 / math.sqrt(HEAD_DIM), BF16)
        for pair in range(tile // LANES):
            at = slice(pair * LANES, (pair + 1) * LANES)
            q2, k2, v2 = q[:, at], k[:, at], v[:, at]
            sums = []
            for head in range(2):
                mine = lane == head
                s = dot(jnp.where(mine, q2, jnp.zeros_like(q2)), k2, CONTRACT_LAST) + bias[...]
                e = jnp.exp(s - jnp.max(s, -1, keepdims=True)).astype(BF16)
                e_ref[(start + pair * LANES) // HEAD_DIM + head] = e
                sums.append(dot(e, jnp.where(mine, v2, jnp.ones_like(v2))))
            top = jnp.where(lane == 0, sums[0], sums[1])
            under = pltpu.roll(jnp.where(lane == 0, sums[1], sums[0]), HEAD_DIM, 1)
            inverse = 1.0 / under
            at = slice(start + pair * LANES, start + (pair + 1) * LANES)
            inverse_ref[:, at] = inverse
            o_ref[:, at] = (top * inverse).astype(BF16)


def attend(place, lengths, groups, blocks, weights):
    each, width = blocks[0].shape
    rows = len(blocks) * each
    wide = low(rows, width)
    return call(
        functools.partial(attend_kernel, len(blocks)),
        "attend",
        (place, lengths),
        (groups, *blocks, *weights),
        (wide, wide, wide, wide, wide, low(width // HEAD_DIM, rows, rows), full(rows, width)),
        scratch=[pltpu.VMEM((rows, rows), F32)],
    )


def attend_back_kernel(e_ref, q_ref, k_ref, v_ref, o_ref, inverse_ref, do_ref, dq_ref, dk_ref, dv_ref):
    rows, width = q_ref.shape
    scale = 1.0 / math.sqrt(HEAD_DIM)
    lane = lax.broadcasted_iota(jnp.int32, (rows, LANES), 1) // HEAD_DIM
    for pair in range(width // LANES):
        at = slice(pair * LANES, (pair + 1) * LANES)
        q, k, v = q_ref[:, at], k_ref[:, at], v_ref[:, at]
        do = do_ref[:, at].astype(F32) * inverse_ref[:, at]
        weighed = do * o_ref[:, at].astype(F32)
        do = do.astype(BF16)
        q_up, do_up = jnp.transpose(q), jnp.transpose(do)
        dq, dk, dv = [], [], []
        for head in range(2):
            mine = lane == head
            part = slice(head * HEAD_DIM, (head + 1) * HEAD_DIM)
            row_dot = jnp.sum(jnp.where(mine, weighed, 0.0), -1, keepdims=True)
            e = e_ref[2 * pair + head]
            d = dot(jnp.where(mine, do, jnp.zeros_like(do)), v, CONTRACT_LAST) - row_dot
            ds = (e.astype(F32) * d).astype(BF16)
            dq.append(dot(ds, k))
            dk.append(dot(q_up[part], ds))
            dv.append(dot(do_up[part], e))
        dq_ref[:, at] = (jnp.where(lane == 0, dq[0], dq[1]) * scale).astype(BF16)
        dk_ref[:, at] = (jnp.transpose(jnp.concatenate(dk, 0)) * scale).astype(BF16)
        dv_ref[:, at] = jnp.transpose(jnp.concatenate(dv, 0)).astype(BF16)


def attend_back(arrays, after):
    wide = low(*arrays[1].shape)
    return call(
        attend_back_kernel, "attend_back", (), arrays, (wide, wide, wide), after=after, cost=30.0
    )


def feed_kernel(count, place, *refs):
    (acts, context, output_weight, output_bias, first_gain, first_shift, inner_weight, inner_bias) = refs[:8]
    outer_weight, outer_bias, second_gain, second_shift = refs[8:12]
    settled_low, hat_ref, inverse_ref, active_ref, slope_ref, hat_two, inverse_two = refs[12:19]
    outs = refs[19 : 19 + count]
    acc = refs[19 + count]
    rows, high = active_ref.shape
    hat, inverse = norm_parts(
        acts[...].astype(F32) + dot(context[...], output_weight[...]) + line(output_bias)
    )
    hat_ref[...] = hat.astype(BF16)
    inverse_ref[...] = jnp.broadcast_to(inverse, inverse_ref.shape)
    settled = hat * line(first_gain) + line(first_shift)
    settled_low[...] = settled.astype(BF16)
    acc[...] = settled + line(outer_bias)
    tile = 4 * LANES
    for start in range(0, high, tile):
        part = slice(start, start + tile)
        inner = dot(settled_low[...], inner_weight[:, part]) + line(inner_bias)[:, part]
        active, slope = gate_parts(inner)
        active_ref[:, part] = active.astype(BF16)
        slope_ref[:, part] = slope.astype(BF16)
    acc[...] += dot(active_ref[...], outer_weight[...])
    each = rows // count
    gain, shift = line(second_gain), line(second_shift)
    for mask in range(count):
        own = block_rows_of(place, mask, each)
        hat, inverse = norm_parts(acc[own, :])
        outs[mask][...] = (hat * gain + shift).astype(BF16)
        hat_two[own, :] = hat
        inverse_two[own, :] = jnp.broadcast_to(inverse, (each, LANES))


def feed(place, acts, context, weights, count):
    rows, width = acts.shape
    high = weights[4].shape[1]
    wide = low(rows, width)
    return call(
        functools.partial(feed_kernel, count),
        "feed",
        (place,),
        (acts, context, *weights),
        (
            wide,
            wide,
            full(rows, LANES),
            low(rows, high),
            low(rows, high),
            full(rows, width),
            full(rows, LANES),
        )
        + (low(rows // count, width),) * count,
        scratch=[pltpu.VMEM((rows, width), F32)],
    )


def turn_kernel(count, place, hat_two, inverse_two, second_gain, *refs):
    cotangents = refs[:count]
    d_second, branch, sums = refs[count:]
    each = hat_two.shape[0] // count
    gain = line(second_gain)
    totals = [0.0, 0.0, 0.0]
    for mask in range(count):
        own = block_rows_of(place, mask, each)
        hat = hat_two[own, :]
        upper = cotangents[mask][pl.ds(0, each), :].astype(F32)
        d = norm_back(upper, hat, inverse_two[own, :1], gain)
        d_low = d.astype(BF16)
        d_second[own, :] = d
        branch[own, :] = d_low
        for i, term in enumerate((d_low.astype(F32), upper * hat, upper)):
            totals[i] = totals[i] + jnp.sum(term, 0, keepdims=True)
    for i in range(3):
        sums[i : i + 1, :] = totals[i]


def turn(place, hat_two, inverse_two, second_gain, cotangents):
    rows, width = hat_two.shape
    return call(
        functools.partial(turn_kernel, len(cotangents)),
        "turn",
        (place,),
        (hat_two, inverse_two, second_gain, *cotangents),
        (full(rows, width), low(rows, width), full(8, width)),
    )


def feed_back_kernel(
    branch,
    outer_weight,
    slope,
    inner_weight,
    d_second,
    hat_ref,
    inverse_ref,
    first_gain,
    output_weight,
    turn_sums,
    d_inner_ref,
    d_first_ref,
    mixed,
    d_context,
    sums,
    acc,
):
    rows, high = slope.shape
    width = acc.shape[1]
    tile = 4 * LANES
    for start in range(0, high, tile):
        part = slice(start, start + tile)
        d_active = dot(branch[...], outer_weight[part, :], CONTRACT_LAST)
        d_inner = (d_active * slope[:, part].astype(F32)).astype(BF16)
        d_inner_ref[:, part] = d_inner
        partial = jnp.sum(d_inner.astype(F32), 0, keepdims=True)
        for lane in range(start, start + tile, LANES):
            row = 6 + lane // width
            sums[row : row + 1, lane % width : lane % width + LANES] = partial[:, lane - start : lane - start + LANES]
    acc[...] = d_second[...] + dot(d_inner_ref[...], inner_weight[...], CONTRACT_LAST)
    parts = 4
    totals = [0.0, 0.0, 0.0]
    gain = line(first_gain)
    for part in range(parts):
        own = slice(part * (rows // parts), (part + 1) * (rows // parts))
        upper = acc[own, :]
        hat = hat_ref[own, :].astype(F32)
        d = norm_back(upper, hat, inverse_ref[own, :1], gain)
        d_low = d.astype(BF16)
        d_first_ref[own, :] = d
        mixed[own, :] = d_low
        for i, term in enumerate((d_low.astype(F32), upper * hat, upper)):
            totals[i] = totals[i] + jnp.sum(term, 0, keepdims=True)
    for i in range(3):
        sums[i : i + 1, :] = totals[i]
    sums[3:6, :] = turn_sums[0:3, :]
    d_context[...] = dot(mixed[...], output_weight[...], CONTRACT_LAST).astype(BF16)


def feed_back(arrays, after):
    rows, width = arrays[0].shape
    high = arrays[2].shape[1]
    wide = low(rows, width)
    return call(
        feed_back_kernel,
        "feed_back",
        (),
        arrays,
        (low(rows, high), full(rows, width), wide, wide, full(16, width)),
        scratch=[pltpu.VMEM((rows, width), F32)],
        after=after,
    )


def entry_back_kernel(count, place, d_first, dq, dk, dv, wq, wk, wv, early_sums, *refs):
    flagged, outs, sums, acc = refs[:count], refs[count : 2 * count], refs[2 * count], refs[2 * count + 1]
    rows, width = dq.shape
    each = rows // count
    acc[...] = (
        d_first[...]
        + dot(dq[...], wq[...], CONTRACT_LAST)
        + dot(dk[...], wk[...], CONTRACT_LAST)
        + dot(dv[...], wv[...], CONTRACT_LAST)
    )
    by_flag = [0.0, 0.0]
    for mask in range(count):
        d = acc[block_rows_of(place, mask, each), :].astype(BF16)
        outs[mask][...] = d
        flag = flagged[mask][pl.ds(each, 16), pl.ds(0, each)]
        by_flag[0] = by_flag[0] + dot(1 - flag, d)
        by_flag[1] = by_flag[1] + dot(flag, d)
    pieces = sums.shape[0]
    piece = width // pieces
    first = early_sums[0:8, :]
    vectors = [by_flag[0][:1], by_flag[1][:1]]
    vectors += [jnp.sum(d[...].astype(F32), 0, keepdims=True) for d in (dq, dv)]
    second = jnp.concatenate(vectors, 0)
    sums[...] = jnp.zeros(sums.shape, F32)
    for i in range(pieces):
        part = slice(i * piece, (i + 1) * piece)
        row, lane = divmod(i * 4 * piece, width)
        sums[i, 0:6, 0:piece] = first[0:6, part]
        sums[i, 0:4, LANES : LANES + piece] = second[:, part]
        sums[i, 0:1, 2 * LANES : 2 * LANES + 4 * piece] = early_sums[6 + row : 7 + row, lane : lane + 4 * piece]


def entry_back(place, arrays, flagged, pieces, after):
    rows, width = arrays[1].shape
    count = len(flagged)
    return call(
        functools.partial(entry_back_kernel, count),
        "entry_back",
        (place,),
        (*arrays, *flagged),
        (low(rows // count, width),) * count + (full(pieces, 8, SIDE // 2),),
        scratch=[pltpu.VMEM((rows, width), F32)],
        after=after,
    )


def parts_of(place):
    x, y = place[2], place[3]
    far, beside, behind, own = 2 * (1 - y) + 1 - x, 2 * y + 1 - x, 2 * (1 - y) + x, 2 * y + x
    return ((far, 0), (beside, 0), (far, 1), (behind, 1), (behind, 0), (beside, 1), (own, 0), (own, 1))


def tall_gradient_kernel(keep, place, left, right, out):
    rows = left.shape[1] // GROUPS // 2
    core = place[1] if keep else 1 - place[1]
    parts = parts_of(place)
    half = SIDE // 2
    for group, homes in ((0, (0, 2)), (1, (1, 5)), (3, (4, 3)), (6, (6, 7))):
        columns = pl.ds(pl.multiple_of((2 * parts[group][0] + core) * rows, LANES), rows)
        product = dot(left[:, columns], right[...], CONTRACT_FIRST).reshape(SHARES, PIECE, SIDE)
        for side, home in enumerate(homes):
            out[home] = product[:, :, side * half : (side + 1) * half].astype(BF16)


def tall_gradient(place, left, right, keep, after=(), cost=2.0):
    return call(
        functools.partial(tall_gradient_kernel, keep),
        "tall_gradient",
        (place,),
        (left, right),
        low(8, SHARES, PIECE, SIDE // 2),
        after=after,
        cost=cost,
    )


def stack_pieces(place, totals, send, keep, start):
    each = SIDE // (GROUPS * SHARES * 2)
    half = SIDE // 2
    for out, core in ((send, 1 - place[1]), (keep, place[1])):
        for home, (group, side) in enumerate(parts_of(place)):
            columns = slice(side * half, (side + 1) * half)
            for share in range(SHARES):
                row = pl.multiple_of((2 * group + core) * (SHARES * each) + share * each, 8)
                piece = jnp.concatenate([t[pl.ds(row, each), columns] for t in totals], 0)
                out[home, share, start : start + piece.shape[0], :] = piece.astype(BF16)


def wide_gradient_kernel(place, left, right, send, keep, first, second):
    for half in range(2):
        start = 2 * half * SIDE
        first[...] = dot(left[...], right[:, start : start + SIDE], CONTRACT_FIRST)
        second[...] = dot(left[...], right[:, start + SIDE : start + 2 * SIDE], CONTRACT_FIRST)
        stack_pieces(place, (first, second), send, keep, half * PIECE // 2)


def wide_gradient(place, left, right, cost=1.0):
    eight = low(8, SHARES, PIECE, SIDE // 2)
    return call(
        wide_gradient_kernel,
        "wide_gradient",
        (place,),
        (left, right),
        (eight, eight),
        scratch=[pltpu.VMEM((SIDE, SIDE), F32)] * 2,
        cost=cost,
    )


def square_gradients_kernel(place, context, acts, mixed, dq, dk, dv, sums, send, keep, first, second):
    for out, core in ((send, 1 - place[1]), (keep, place[1])):
        for home, (group, side) in enumerate(parts_of(place)):
            for share in range(SHARES):
                piece = sums[(2 * group + core) * SHARES + share] if side == 0 else jnp.zeros(sums.shape[1:], F32)
                out[home, share, PIECE:, :] = piece.astype(BF16)
    first[...] = dot(context[...], mixed[...], CONTRACT_FIRST)
    second[...] = dot(acts[...], dq[...], CONTRACT_FIRST)
    stack_pieces(place, (first, second), send, keep, 0)
    first[...] = dot(acts[...], dk[...], CONTRACT_FIRST)
    second[...] = dot(acts[...], dv[...], CONTRACT_FIRST)
    stack_pieces(place, (first, second), send, keep, PIECE // 2)


def square_gradients(place, arrays, after, cost=0.1):
    eight = low(8, SHARES, PIECE + 8, SIDE // 2)
    return call(
        square_gradients_kernel,
        "square_gradients",
        (place,),
        arrays,
        (eight, eight),
        scratch=[pltpu.VMEM((SIDE, SIDE), F32)] * 2,
        after=after,
        cost=cost,
    )


def first_sums_kernel(keep, got, to_x, to_y):
    to_x[...] = total([keep[0:2], got[0:2]]).astype(BF16)
    to_y[...] = total([keep[2:4], got[2:4]]).astype(BF16)


def second_sums_kernel(start, keep, got, from_x, from_y, to_y, to_x):
    to_y[...] = total([keep[start], got[start], from_x[0]]).astype(BF16)
    to_x[...] = total([keep[start + 1], got[start + 1], from_y[0]]).astype(BF16)


def third_sums_kernel(start, place, keep, got, from_x, from_y, then_y, then_x, send, kept):
    half = SIDE // 2
    bit = place[0] & 1
    for out, share_bit in ((send, 1 - bit), (kept, bit)):
        for high in range(SHARES // 2):
            share = 2 * high + share_bit
            a = total([keep[start + 2, share], got[start + 2, share], from_x[1, share], then_y[share]])
            b = total([keep[start + 3, share], got[start + 3, share], from_y[1, share], then_x[share]])
            out[high, :, :half] = a.astype(out.dtype)
            out[high, :, half:] = b.astype(out.dtype)


def fourth_sums_kernel(place, kept, got, send):
    other = 1 - (place[0] >> 1)
    send[...] = total([kept[other], got[other]]).astype(BF16)


def last_sums_kernel(form, place, kept, got, last, *outs):
    mine = place[0] >> 1
    result = total([kept[mine], got[mine], last[...]])
    each = PIECE // 4
    if form == "tall":
        outs[0][...] = result
    else:
        for i in range(4):
            rows = result[i * each : (i + 1) * each]
            if form == "wide":
                outs[0][:, i * SIDE : (i + 1) * SIDE] = rows
            else:
                outs[i][...] = rows
    if form == "square":
        outs[4][...] = result[PIECE:, : SIDE // 2]


class Halving:
    def __init__(self, place, send, keep):
        self.place, self.keep = place, keep
        self.got = [swap_pairs(part, "batch", 1) for part in send]
        self.late = 0 if len(keep) > 1 else 4

    def step(self, kernel, name, scalars, arrays, outs, after, cost=0.5):
        results = call(kernel, name, scalars, arrays, outs, after=after, cost=cost)
        self.done = results[:1]
        return results

    def first(self, after=(), cost=0.5):
        half = low(2, *self.keep[0].shape[1:])
        arrays = (self.keep[0], self.got[0])
        to = self.step(first_sums_kernel, "first_sums", (), arrays, (half, half), after, cost)
        self.from_x, self.from_y = swap_pairs(to[0], "batch", 2), swap_pairs(to[1], "batch", 4)

    def second(self, after=(), cost=0.5):
        quarter = low(*self.keep[0].shape[1:])
        arrays = (self.keep[-1], self.got[-1], self.from_x, self.from_y)
        kernel = functools.partial(second_sums_kernel, self.late)
        to = self.step(kernel, "second_sums", (), arrays, (quarter, quarter), after, cost)
        self.then_y, self.then_x = swap_pairs(to[0], "batch", 4), swap_pairs(to[1], "batch", 2)

    def third(self, after=(), cost=0.5):
        shape = (SHARES // 2, self.keep[0].shape[2], SIDE)
        arrays = (self.keep[-1], self.got[-1], self.from_x, self.from_y, self.then_y, self.then_x)
        outs = (low(*shape), full(*shape))
        kernel = functools.partial(third_sums_kernel, self.late)
        to, self.kept = self.step(kernel, "third_sums", (self.place,), arrays, outs, after, cost)
        self.pair = swap_pairs(to, "seq", 1)

    def fourth(self, after=(), cost=0.5):
        arrays = (self.kept, self.pair)
        outs = (low(*self.kept.shape[1:]),)
        (to,) = self.step(fourth_sums_kernel, "fourth_sums", (self.place,), arrays, outs, after, cost)
        self.others = swap_pairs(to, "seq", 2)

    def last(self, form, after=()):
        each = PIECE // 4
        shapes = {
            "tall": [(PIECE, SIDE)],
            "wide": [(each, 4 * SIDE)],
            "square": [(each, SIDE)] * 4 + [(8, SIDE // 2)],
        }[form]
        arrays = (self.kept, self.pair, self.others)
        outs = tuple(full(*shape) for shape in shapes)
        kernel = functools.partial(last_sums_kernel, form)
        self.result = self.step(kernel, "last_sums", (self.place,), arrays, outs, after)


def add_pieces(pieces):
    batch, seq = lax.axis_size("batch"), lax.axis_size("seq")
    parts = [pieces.reshape((2,) * ((batch * seq).bit_length() - 1) + pieces.shape[1:])]
    for axis in ("batch", "seq"):
        bits = lax.axis_size(axis).bit_length() - 1
        for bit in range(bits):
            parts = [total(halve(parts, bits - 1 - bit, axis, bit, F32))]
    return parts[0]


def per_device(
    hidden,
    groups,
    answer_flags,
    lengths,
    answer_embed,
    query_weight,
    query_bias,
    key_weight,
    value_weight,
    value_bias,
    output_weight,
    output_bias,
    first_gain,
    first_shift,
    inner_weight,
    inner_bias,
    outer_weight,
    outer_bias,
    second_gain,
    second_shift,
    cotangent,
):
    items, block_rows, width = hidden.shape
    batch, seq = lax.axis_size("batch"), lax.axis_size("seq")
    me, group = lax.axis_index("seq"), lax.axis_index("batch")
    place = jnp.stack([me, group & 1, (group >> 1) & 1, (group >> 2) & 1]).astype(jnp.int32)
    high = inner_weight.shape[1]
    even = (batch, seq, width, high) == (8, SHARES, SIDE, 4 * SIDE)

    got = exchange(entry_blocks(place, hidden, answer_flags, answer_embed))
    upper = exchange(flagged_blocks(place, cotangent, answer_flags, got[1:]))
    acts, queries, keys, values, context, exponents, inverse_sums = attend(
        place, lengths, groups, got, (query_weight, query_bias, key_weight, value_weight, value_bias)
    )
    settled, hat, inverse, active, slope, hat_two, inverse_two, *output = feed(
        place,
        acts,
        context,
        (
            output_weight,
            output_bias,
            first_gain,
            first_shift,
            inner_weight,
            inner_bias,
            outer_weight,
            outer_bias,
            second_gain,
            second_shift,
        ),
        items,
    )
    d_second, branch, sums = turn(place, hat_two, inverse_two, second_gain, upper)
    if even:
        send = tall_gradient(place, active, branch, False)
        keep = tall_gradient(place, active, branch, True, (send,))
        outer = Halving(place, (send,), (keep,))
        outer.first()
        after = outer.done
    else:
        outer_weight_gradient = scatter(dot(active, branch, CONTRACT_FIRST))
        after = ()
    output = exchange(output)
    d_inner, d_first, mixed, d_context, sums = feed_back(
        (
            branch,
            outer_weight,
            slope,
            inner_weight,
            d_second,
            hat,
            inverse,
            first_gain,
            output_weight,
            sums,
        ),
        after,
    )
    if even:
        send, keep = wide_gradient(place, settled, d_inner)
        inner = Halving(place, (send,), (keep,))
        outer.second((send,))
        output = join_blocks(place, output, outer.done)
        after = (output,)
    else:
        inner_weight_gradient = scatter(dot(settled, d_inner, CONTRACT_FIRST))
    d_queries, d_keys, d_values = attend_back(
        (exponents, queries, keys, values, context, inverse_sums, d_context), after
    )
    if even:
        inner.first((d_queries,))
        after = inner.done
    *input_gradient, sums = entry_back(
        place,
        (d_first, d_queries, d_keys, d_values, query_weight, key_weight, value_weight, sums),
        upper,
        batch * seq,
        after,
    )
    back = exchange(input_gradient)
    if even:
        outer.third((input_gradient[0],))
        send, keep = square_gradients(
            place, (context, acts, mixed, d_queries, d_keys, d_values, sums), outer.done
        )
        narrow = Halving(place, (send,), (keep,))
        inner.second((send,))
        outer.fourth(inner.done, cost=25.0)
        narrow.first((*outer.done, back[2]))
        inner.third((*narrow.done, back[3]))
        outer.last("tall", inner.done)
        narrow.second((*outer.done, back[1]))
        inner.fourth(narrow.done)
        narrow.third(inner.done)
        inner.last("wide", narrow.done)
        narrow.fourth(inner.done)
        narrow.last("square")
        (outer_weight_gradient,), (inner_weight_gradient,) = outer.result, inner.result
        *narrow, pieces = narrow.result
    else:
        narrow = jnp.concatenate(
            [
                dot(left, right, CONTRACT_FIRST).astype(BF16)
                for left, right in (
                    (context, mixed),
                    (acts, d_queries),
                    (acts, d_keys),
                    (acts, d_values),
                )
            ],
            1,
        )
        narrow = jnp.split(scatter(narrow), 4, 1)
        pieces = add_pieces(sums)
    output_weight_gradient, query_weight_gradient, key_weight_gradient, value_weight_gradient = narrow
    if not even:
        output = join_blocks(place, output)
    input_gradient = join_blocks(place, back)
    early, later = pieces[:, : width // (batch * seq)], pieces[:, LANES : LANES + width // (batch * seq)]
    return (
        output,
        input_gradient,
        later[0:2],
        query_weight_gradient,
        later[2],
        key_weight_gradient,
        value_weight_gradient,
        later[3],
        output_weight_gradient,
        early[0],
        early[1],
        early[2],
        inner_weight_gradient,
        pieces[0, 2 * LANES : 2 * LANES + high // (batch * seq)],
        outer_weight_gradient,
        early[3],
        early[4],
        early[5],
    )


def solution(mesh):
    both = ("batch", "seq")
    in_specs = (
        (P("batch", "seq", None), P("batch", None), P("batch", "seq"), P("batch"))
        + (P(),) * 16
        + (P("batch", "seq", None),)
    )
    matrix, vector = P(both, None), P(both)
    out_specs = (
        P("batch", "seq", None),
        P("batch", "seq", None),
        P(None, both),
        matrix,
        vector,
        matrix,
        matrix,
        vector,
        matrix,
        vector,
        vector,
        vector,
        matrix,
        vector,
        matrix,
        vector,
        vector,
        vector,
    )
    return jax.shard_map(
        per_device, mesh=mesh, in_specs=in_specs, out_specs=out_specs, check_vma=False
    )
```

```python
import functools
import math

import jax
import jax.numpy as jnp
from jax import lax
from jax.experimental import pallas as pl
from jax.experimental.pallas import tpu as pltpu
from jax.sharding import PartitionSpec as P

HEAD_DIM = 64
LANES = 128
EPSILON = 1e-12
BF16 = jnp.bfloat16
F32 = jnp.float32

CONTRACT_LAST = (((1,), (1,)), ((), ()))
CONTRACT_FIRST = (((0,), (0,)), ((), ()))
GROUPS, SHARES, PIECE, SIDE = 4, 4, 96, 768
MICROSECOND = 1150000000
PARTS = 4


def dot(a, b, dims=(((1,), (0,)), ((), ()))):
    return lax.dot_general(a, b, dims, preferred_element_type=F32)


def low(*shape):
    return jax.ShapeDtypeStruct(shape, BF16)


def full(*shape):
    return jax.ShapeDtypeStruct(shape, F32)


def call(kernel, name, scalars, arrays, outs, limit=4, scratch=(), far=(), after=(), cost=4.0):
    count = len(scalars) + len(arrays) + len(far)

    def body(*refs):
        kernel(*refs[:count], *refs[count + len(after) :])

    single = not isinstance(outs, tuple)
    vmem, hbm = pl.BlockSpec(memory_space=pltpu.VMEM), pl.BlockSpec(memory_space=pltpu.HBM)
    return pl.pallas_call(
        body,
        in_specs=[pl.BlockSpec(memory_space=pltpu.SMEM)] * len(scalars)
        + [vmem] * len(arrays)
        + [hbm] * len(far)
        + [pl.BlockSpec(memory_space=pl.ANY)] * len(after),
        out_specs=vmem if single else (vmem,) * len(outs),
        out_shape=outs,
        scratch_shapes=list(scratch),
        compiler_params=pltpu.CompilerParams(vmem_limit_bytes=limit << 20),
        cost_estimate=pl.CostEstimate(flops=int(cost * MICROSECOND), bytes_accessed=1 << 16, transcendentals=0),
        name=name,
    )(*scalars, *arrays, *(pltpu.with_memory_space_constraint(a, pltpu.HBM) for a in far), *after)


def fetch(sources, targets, semaphores, parts=1):
    copies = []
    for source, target in zip(sources, targets):
        rows = source.shape[0] // parts
        for part in range(parts):
            own = pl.ds(part * rows, rows)
            copies.append(
                pltpu.make_async_copy(source.at[own], target.at[own], semaphores.at[len(copies)])
            )
    for copy in copies:
        copy.start()
    return copies


def line(ref):
    return ref[...].astype(F32)[None]


def block_rows_of(place, mask, each):
    return pl.ds(pl.multiple_of((place[0] ^ mask) * each, each), each)


def entry_kernel(count, place, *refs):
    sources, outs, (hidden, flags, embed, semaphores) = refs[:3], refs[3 : 3 + count], refs[3 + count :]
    for copy in fetch(sources, (hidden, flags, embed), semaphores):
        copy.wait()
    rows = hidden.shape[1]
    row = lax.broadcasted_iota(jnp.int32, (rows, rows), 0)
    column = lax.broadcasted_iota(jnp.int32, (rows, rows), 1)
    first, second = embed[0:1].astype(F32), embed[1:2].astype(F32)
    for mask in range(count):
        item = place[0] ^ mask
        flag = flags[pl.ds(item, 1), :].astype(F32)
        upright = jnp.sum(jnp.where(row == column, flag, 0.0), 1, keepdims=True)
        added = jnp.where(upright == 1.0, second, first)
        outs[mask][...] = (hidden[item].astype(F32) + added).astype(BF16)


def entry_blocks(place, *arrays):
    count, rows, width = arrays[0].shape
    return call(
        functools.partial(entry_kernel, count),
        "entry_blocks",
        (place,),
        (),
        (low(rows, width),) * count,
        scratch=[pltpu.VMEM(a.shape, a.dtype) for a in arrays] + [pltpu.SemaphoreType.DMA((3,))],
        far=arrays,
    )


def flagged_kernel(count, place, cotangent, flags, *outs):
    rows = cotangent.shape[1]
    for mask in range(count):
        item = place[0] ^ mask
        outs[mask][pl.ds(0, rows), :] = cotangent[item]
        outs[mask][pl.ds(rows, 16), :] = jnp.zeros((16, cotangent.shape[2]), BF16)
        flag = jnp.broadcast_to(flags[pl.ds(item, 1), :].astype(F32), (16, rows))
        outs[mask][pl.ds(rows, 16), pl.ds(0, rows)] = flag.astype(BF16)


def flagged_blocks(place, cotangent, flags, after):
    count, rows, width = cotangent.shape
    return call(
        functools.partial(flagged_kernel, count),
        "flagged_blocks",
        (place,),
        (cotangent, flags),
        (low(rows + 16, width),) * count,
        after=after,
    )


def join_kernel(count, place, *refs):
    for mask in range(count):
        refs[count][place[0] ^ mask] = refs[mask][...]


def join_blocks(place, blocks, after=()):
    return call(
        functools.partial(join_kernel, len(blocks)),
        "join_blocks",
        (place,),
        blocks,
        low(len(blocks), *blocks[0].shape),
        after=after,
        cost=0.5,
    )


def swap_pairs(array, axis, mask):
    size = lax.axis_size(axis)
    return lax.ppermute(array, axis, [(i, i ^ mask) for i in range(size)])


def pick(array, index, dim):
    return lax.dynamic_index_in_dim(array, index, dim, keepdims=False)


def exchange(blocks):
    order = sorted(range(1, len(blocks)), key=lambda mask: mask < 2)
    got = {mask: swap_pairs(blocks[mask], "seq", mask) for mask in order}
    return [blocks[0]] + [got[mask] for mask in range(1, len(blocks))]


def total(parts):
    result = parts[0].astype(F32)
    for part in parts[1:]:
        result = result + part.astype(F32)
    return result


def halve(parts, dim, axis, bit, dtype=BF16):
    mine = (lax.axis_index(axis) >> bit) & 1
    sent = total([pick(part, 1 - mine, dim) for part in parts]).astype(dtype)
    got = swap_pairs(sent, axis, 1 << bit)
    return [pick(part, mine, dim) for part in parts] + [got]


def scatter(gradient):
    batch, seq = lax.axis_size("batch"), lax.axis_size("seq")
    rows, columns = gradient.shape
    batch_bits, seq_bits = batch.bit_length() - 1, seq.bit_length() - 1
    each = rows // (batch * seq)
    shape = (2,) * (batch_bits + seq_bits) + (each, columns)
    parts = [gradient.astype(BF16).reshape(shape)]
    parts = halve(parts, batch_bits - 1, "batch", 0)
    ways = []
    for way in range(2):
        half = [
            lax.slice_in_dim(part, way * (columns // 2), (way + 1) * (columns // 2), axis=part.ndim - 1)
            for part in parts
        ]
        bits = list(range(1, batch_bits))
        if way:
            bits = bits[::-1]
        left = list(range(batch_bits - 1, 0, -1))
        for bit in bits:
            dim = left.index(bit)
            half = halve(half, dim, "batch", bit)
            left.remove(bit)
        ways.append(half)
    parts = [jnp.concatenate([a, b], -1) for a, b in zip(*ways)]
    for bit in range(seq_bits):
        parts = halve(parts, seq_bits - 1 - bit, "seq", bit)
    return total(parts)


def norm_parts(values):
    centre = values - jnp.mean(values, -1, keepdims=True)
    inverse = lax.rsqrt(jnp.mean(centre * centre, -1, keepdims=True) + EPSILON)
    return centre * inverse, inverse


def norm_back(upper, hat, inverse, gain):
    g = upper * gain
    return inverse * (
        g - jnp.mean(g, -1, keepdims=True) - hat * jnp.mean(g * hat, -1, keepdims=True)
    )


def gate_parts(u):
    share = 0.5 + 0.5 * lax.erf(u * 0.7071067811865476)
    return u * share, share + u * (jnp.exp(-0.5 * u * u) * 0.3989422804014327)


def load_kernel(*refs):
    count = len(refs) // 2
    for copy in fetch(refs[:count], refs[count:-1], refs[-1], PARTS):
        copy.wait()


def load(weights, after):
    return call(
        load_kernel,
        "load",
        (),
        (),
        tuple(low(*weight.shape) for weight in weights),
        scratch=[pltpu.SemaphoreType.DMA((PARTS * len(weights),))],
        far=weights,
        after=after,
    )


def attend_kernel(count, place, lengths, groups, *refs):
    blocks = refs[:count]
    query_weight, query_bias, key_weight, value_weight, value_bias = refs[count : count + 5]
    acts, q_ref, k_ref, v_ref, o_ref, e_ref, inverse_ref, bias = refs[count + 5 :]
    rows, width = acts.shape
    each = rows // count
    for mask in range(count):
        acts[block_rows_of(place, mask, each), :] = blocks[mask][...]
    ids = groups[pl.ds(place[0], 1), :].astype(F32)
    key_place = lax.broadcasted_iota(jnp.int32, (1, rows), 1)
    key_ids = jnp.where(key_place < lengths[place[0]], ids, 1e9)
    upright = jnp.transpose(jnp.broadcast_to(ids, (8, rows)))[:, :1]
    bias[...] = jnp.where(key_ids <= upright, 0.0, -1e30)
    lane = lax.broadcasted_iota(jnp.int32, (rows, LANES), 1) // HEAD_DIM
    tile = 2 * LANES
    for start in range(0, width, tile):
        part = slice(start, start + tile)
        x = acts[...]
        q = (dot(x, query_weight[:, part]) + line(query_bias)[:, part]).astype(BF16)
        k = dot(x, key_weight[:, part]).astype(BF16)
        v = (dot(x, value_weight[:, part]) + line(value_bias)[:, part]).astype(BF16)
        q_ref[:, part] = q
        k_ref[:, part] = k
        v_ref[:, part] = v
        q = q * jnp.asarray(1.0 / math.sqrt(HEAD_DIM), BF16)
        for pair in range(tile // LANES):
            at = slice(pair * LANES, (pair + 1) * LANES)
            q2, k2, v2 = q[:, at], k[:, at], v[:, at]
            sums = []
            for head in range(2):
                mine = lane == head
                s = dot(jnp.where(mine, q2, jnp.zeros_like(q2)), k2, CONTRACT_LAST) + bias[...]
                e = jnp.exp(s - jnp.max(s, -1, keepdims=True)).astype(BF16)
                e_ref[(start + pair * LANES) // HEAD_DIM + head] = e
                sums.append(dot(e, jnp.where(mine, v2, jnp.ones_like(v2))))
            top = jnp.where(lane == 0, sums[0], sums[1])
            under = pltpu.roll(jnp.where(lane == 0, sums[1], sums[0]), HEAD_DIM, 1)
            inverse = 1.0 / under
            at = slice(start + pair * LANES, start + (pair + 1) * LANES)
            inverse_ref[:, at] = inverse
            o_ref[:, at] = (top * inverse).astype(BF16)


def attend(place, lengths, groups, blocks, weights, after):
    each, width = blocks[0].shape
    rows = len(blocks) * each
    wide = low(rows, width)
    return call(
        functools.partial(attend_kernel, len(blocks)),
        "attend",
        (place, lengths),
        (groups, *blocks, *weights),
        (wide, wide, wide, wide, wide, low(width // HEAD_DIM, rows, rows), full(rows, width)),
        scratch=[pltpu.VMEM((rows, rows), F32)],
        limit=8,
        after=after,
    )


def attend_back_kernel(e_ref, q_ref, k_ref, v_ref, o_ref, inverse_ref, do_ref, dq_ref, dk_ref, dv_ref):
    rows, width = q_ref.shape
    scale = 1.0 / math.sqrt(HEAD_DIM)
    lane = lax.broadcasted_iota(jnp.int32, (rows, LANES), 1) // HEAD_DIM
    for pair in range(width // LANES):
        at = slice(pair * LANES, (pair + 1) * LANES)
        q, k, v = q_ref[:, at], k_ref[:, at], v_ref[:, at]
        do = do_ref[:, at].astype(F32) * inverse_ref[:, at]
        weighed = do * o_ref[:, at].astype(F32)
        do = do.astype(BF16)
        q_up, do_up = jnp.transpose(q), jnp.transpose(do)
        dq, dk, dv = [], [], []
        for head in range(2):
            mine = lane == head
            part = slice(head * HEAD_DIM, (head + 1) * HEAD_DIM)
            row_dot = jnp.sum(jnp.where(mine, weighed, 0.0), -1, keepdims=True)
            d = dot(jnp.where(mine, do, jnp.zeros_like(do)), v, CONTRACT_LAST) - row_dot
            e = e_ref[2 * pair + head]
            ds = (e.astype(F32) * d).astype(BF16)
            dq.append(dot(ds, k))
            dk.append(dot(q_up[part], ds))
            dv.append(dot(do_up[part], e))
        dq_ref[:, at] = (jnp.where(lane == 0, dq[0], dq[1]) * scale).astype(BF16)
        dk_ref[:, at] = (jnp.transpose(jnp.concatenate(dk, 0)) * scale).astype(BF16)
        dv_ref[:, at] = jnp.transpose(jnp.concatenate(dv, 0)).astype(BF16)


def attend_back(arrays, after):
    wide = low(*arrays[1].shape)
    return call(
        attend_back_kernel, "attend_back", (), arrays, (wide, wide, wide), limit=7, after=after, cost=30.0
    )


def feed_kernel(count, place, *refs):
    (acts, context, output_weight, output_bias, first_gain, first_shift, inner_weight, inner_bias) = refs[:8]
    outer_weight, outer_bias, second_gain, second_shift = refs[8:12]
    settled_low, hat_ref, inverse_ref, active_ref, slope_ref, hat_two, inverse_two = refs[12:19]
    outs = refs[19 : 19 + count]
    acc = refs[19 + count]
    rows, high = active_ref.shape
    hat, inverse = norm_parts(
        acts[...].astype(F32) + dot(context[...], output_weight[...]) + line(output_bias)
    )
    hat_ref[...] = hat.astype(BF16)
    inverse_ref[...] = jnp.broadcast_to(inverse, inverse_ref.shape)
    settled = hat * line(first_gain) + line(first_shift)
    settled_low[...] = settled.astype(BF16)
    acc[...] = settled + line(outer_bias)
    tile = 4 * LANES
    for start in range(0, high, tile):
        part = slice(start, start + tile)
        inner = dot(settled_low[...], inner_weight[:, part]) + line(inner_bias)[:, part]
        active, slope = gate_parts(inner)
        active_ref[:, part] = active.astype(BF16)
        slope_ref[:, part] = slope.astype(BF16)
    acc[...] += dot(active_ref[...], outer_weight[...])
    each = rows // count
    gain, shift = line(second_gain), line(second_shift)
    for mask in range(count):
        own = block_rows_of(place, mask, each)
        hat, inverse = norm_parts(acc[own, :])
        outs[mask][...] = (hat * gain + shift).astype(BF16)
        hat_two[own, :] = hat
        inverse_two[own, :] = jnp.broadcast_to(inverse, (each, LANES))


def feed(place, acts, context, weights, count):
    rows, width = acts.shape
    high = weights[4].shape[1]
    wide = low(rows, width)
    return call(
        functools.partial(feed_kernel, count),
        "feed",
        (place,),
        (acts, context, *weights),
        (
            wide,
            wide,
            full(rows, LANES),
            low(rows, high),
            low(rows, high),
            full(rows, width),
            full(rows, LANES),
        )
        + (low(rows // count, width),) * count,
        limit=9,
        scratch=[pltpu.VMEM((rows, width), F32)],
    )


def turn_kernel(count, place, hat_two, inverse_two, second_gain, *refs):
    cotangents = refs[:count]
    d_second, branch, sums = refs[count:]
    each = hat_two.shape[0] // count
    gain = line(second_gain)
    totals = [0.0, 0.0, 0.0]
    for mask in range(count):
        own = block_rows_of(place, mask, each)
        hat = hat_two[own, :]
        upper = cotangents[mask][pl.ds(0, each), :].astype(F32)
        d = norm_back(upper, hat, inverse_two[own, :1], gain)
        d_low = d.astype(BF16)
        d_second[own, :] = d
        branch[own, :] = d_low
        for i, term in enumerate((d_low.astype(F32), upper * hat, upper)):
            totals[i] = totals[i] + jnp.sum(term, 0, keepdims=True)
    for i in range(3):
        sums[i : i + 1, :] = totals[i]


def turn(place, hat_two, inverse_two, second_gain, cotangents):
    rows, width = hat_two.shape
    return call(
        functools.partial(turn_kernel, len(cotangents)),
        "turn",
        (place,),
        (hat_two, inverse_two, second_gain, *cotangents),
        (full(rows, width), low(rows, width), full(8, width)),
    )


def feed_back_kernel(
    branch,
    outer_weight,
    slope,
    inner_weight,
    d_second,
    hat_ref,
    inverse_ref,
    first_gain,
    output_weight,
    turn_sums,
    d_inner_ref,
    d_first_ref,
    mixed,
    d_context,
    sums,
    acc,
):
    rows, high = slope.shape
    width = acc.shape[1]
    tile = 4 * LANES
    for start in range(0, high, tile):
        part = slice(start, start + tile)
        d_active = dot(branch[...], outer_weight[part, :], CONTRACT_LAST)
        d_inner = (d_active * slope[:, part].astype(F32)).astype(BF16)
        d_inner_ref[:, part] = d_inner
        partial = jnp.sum(d_inner.astype(F32), 0, keepdims=True)
        for lane in range(start, start + tile, LANES):
            row = 6 + lane // width
            sums[row : row + 1, lane % width : lane % width + LANES] = partial[:, lane - start : lane - start + LANES]
    acc[...] = d_second[...] + dot(d_inner_ref[...], inner_weight[...], CONTRACT_LAST)
    parts = 4
    totals = [0.0, 0.0, 0.0]
    gain = line(first_gain)
    for part in range(parts):
        own = slice(part * (rows // parts), (part + 1) * (rows // parts))
        upper = acc[own, :]
        hat = hat_ref[own, :].astype(F32)
        d = norm_back(upper, hat, inverse_ref[own, :1], gain)
        d_low = d.astype(BF16)
        d_first_ref[own, :] = d
        mixed[own, :] = d_low
        for i, term in enumerate((d_low.astype(F32), upper * hat, upper)):
            totals[i] = totals[i] + jnp.sum(term, 0, keepdims=True)
    for i in range(3):
        sums[i : i + 1, :] = totals[i]
    sums[3:6, :] = turn_sums[0:3, :]
    d_context[...] = dot(mixed[...], output_weight[...], CONTRACT_LAST).astype(BF16)


def feed_back(arrays, after):
    rows, width = arrays[0].shape
    high = arrays[2].shape[1]
    wide = low(rows, width)
    return call(
        feed_back_kernel,
        "feed_back",
        (),
        arrays,
        (low(rows, high), full(rows, width), wide, wide, full(16, width)),
        scratch=[pltpu.VMEM((rows, width), F32)],
        after=after,
        limit=7,
    )


def entry_back_kernel(count, place, d_first, dq, dk, dv, wq, wk, wv, *refs):
    outs, acc = refs[:count], refs[count]
    each = dq.shape[0] // count
    acc[...] = (
        d_first[...]
        + dot(dq[...], wq[...], CONTRACT_LAST)
        + dot(dk[...], wk[...], CONTRACT_LAST)
        + dot(dv[...], wv[...], CONTRACT_LAST)
    )
    for mask in range(count):
        outs[mask][...] = acc[block_rows_of(place, mask, each), :].astype(BF16)


def entry_back(place, arrays, count, after):
    rows, width = arrays[1].shape
    return call(
        functools.partial(entry_back_kernel, count),
        "entry_back",
        (place,),
        arrays,
        (low(rows // count, width),) * count,
        scratch=[pltpu.VMEM((rows, width), F32)],
        after=after,
        limit=5,
    )


def add_vectors(place, d_first, dq, dk, dv, weights, early_sums, flagged, sums):
    count = len(flagged)
    each, width = dq.shape[0] // count, dq.shape[1]
    row = lax.broadcasted_iota(jnp.int32, (each, each), 0)
    column = lax.broadcasted_iota(jnp.int32, (each, each), 1)
    zero, one = [0.0] * 4, [0.0] * 4
    for mask in range(count):
        own = block_rows_of(place, mask, each)
        flag = flagged[mask][pl.ds(each, 16), pl.ds(0, each)][:1].astype(F32)
        upright = jnp.sum(jnp.where(row == column, flag, 0.0), 1, keepdims=True)
        for i, array in enumerate((d_first, dq, dk, dv)):
            value = array[own, :].astype(F32)
            zero[i] = zero[i] + jnp.sum(value * (1.0 - upright), 0, keepdims=True)
            one[i] = one[i] + jnp.sum(value * upright, 0, keepdims=True)
    by_flag = jnp.concatenate([zero[0], one[0]] + [jnp.zeros((6, width), F32)], 0)
    for i, weight in enumerate(weights):
        pair = jnp.concatenate([zero[i + 1], one[i + 1]] + [jnp.zeros((6, width), F32)], 0)
        by_flag = by_flag + dot(pair.astype(BF16), weight[...], CONTRACT_LAST)
    second = jnp.concatenate([by_flag[:2], zero[1] + one[1], zero[3] + one[3]], 0)
    first = early_sums[0:6, :]
    pieces = sums.shape[0]
    piece = width // pieces
    sums[...] = jnp.zeros(sums.shape, F32)
    for i in range(pieces):
        part = slice(i * piece, (i + 1) * piece)
        at, lane = divmod(i * 4 * piece, width)
        sums[i, 0:6, 0:piece] = first[:, part]
        sums[i, 0:4, LANES : LANES + piece] = second[:, part]
        sums[i, 0:1, 2 * LANES : 2 * LANES + 4 * piece] = early_sums[6 + at : 7 + at, lane : lane + 4 * piece]


def vector_pieces_kernel(place, d_first, dq, dk, dv, wq, wk, wv, early_sums, *refs):
    add_vectors(place, d_first, dq, dk, dv, (wq, wk, wv), early_sums, refs[:-1], refs[-1])


def vector_pieces(place, arrays, flagged, pieces):
    return call(
        vector_pieces_kernel,
        "vector_pieces",
        (place,),
        (*arrays, *flagged),
        full(pieces, 8, SIDE // 2),
    )


def parts_of(place):
    x, y = place[2], place[3]
    far, beside, behind, own = 2 * (1 - y) + 1 - x, 2 * y + 1 - x, 2 * (1 - y) + x, 2 * y + x
    return ((far, 0), (beside, 0), (far, 1), (behind, 1), (behind, 0), (beside, 1), (own, 0), (own, 1))


def tall_gradient_kernel(keep, place, left, right, out):
    rows = left.shape[1] // GROUPS // 2
    core = place[1] if keep else 1 - place[1]
    parts = parts_of(place)
    half = SIDE // 2
    for group, homes in ((0, (0, 2)), (1, (1, 5)), (3, (4, 3)), (6, (6, 7))):
        columns = pl.ds(pl.multiple_of((2 * parts[group][0] + core) * rows, LANES), rows)
        product = dot(left[:, columns], right[...], CONTRACT_FIRST).reshape(SHARES, PIECE, SIDE)
        for side, home in enumerate(homes):
            out[home] = product[:, :, side * half : (side + 1) * half].astype(BF16)


def tall_gradient(place, left, right, keep, after=(), cost=2.0):
    return call(
        functools.partial(tall_gradient_kernel, keep),
        "tall_gradient",
        (place,),
        (left, right),
        low(8, SHARES, PIECE, SIDE // 2),
        after=after,
        cost=cost,
    )


def stack_pieces(place, totals, send, keep, start, last=None):
    each = SIDE // (GROUPS * SHARES * 2)
    half = SIDE // 2
    for out, core in ((send, 1 - place[1]), (keep, place[1])):
        for home, (group, side) in enumerate(parts_of(place)):
            columns = slice(side * half, (side + 1) * half)
            for share in range(SHARES):
                index = (2 * group + core) * SHARES + share
                row = pl.multiple_of(index * each, 8)
                pieces = [t[pl.ds(row, each), columns] for t in totals]
                if last is not None:
                    pieces.append(last[index] if side == 0 else jnp.zeros(last.shape[1:], F32))
                piece = jnp.concatenate(pieces, 0)
                out[home, share, start : start + piece.shape[0], :] = piece.astype(BF16)


def wide_gradient_kernel(place, left, right, context, mixed, send, keep, first, second):
    for half in range(2):
        start = 2 * half * SIDE
        first[...] = dot(left[...], right[:, start : start + SIDE], CONTRACT_FIRST)
        second[...] = dot(left[...], right[:, start + SIDE : start + 2 * SIDE], CONTRACT_FIRST)
        stack_pieces(place, (first, second), send, keep, half * PIECE // 2)
    first[...] = dot(context[...], mixed[...], CONTRACT_FIRST)
    stack_pieces(place, (first,), send, keep, PIECE)


def wide_gradient(place, arrays, cost=1.0):
    eight = low(8, SHARES, PIECE + PIECE // 4, SIDE // 2)
    return call(
        wide_gradient_kernel,
        "wide_gradient",
        (place,),
        arrays,
        (eight, eight),
        scratch=[pltpu.VMEM((SIDE, SIDE), F32)] * 2,
        cost=cost,
        limit=8,
    )


def square_gradients_kernel(place, acts, d_first, dq, dk, dv, wq, wk, wv, early_sums, *refs):
    flagged, (send, keep, first, second, sums) = refs[:-5], refs[-5:]
    first[...] = dot(acts[...], dq[...], CONTRACT_FIRST)
    second[...] = dot(acts[...], dk[...], CONTRACT_FIRST)
    add_vectors(place, d_first, dq, dk, dv, (wq, wk, wv), early_sums, flagged, sums)
    stack_pieces(place, (first, second), send, keep, 0)
    first[...] = dot(acts[...], dv[...], CONTRACT_FIRST)
    stack_pieces(place, (first,), send, keep, PIECE // 2, sums)


def square_gradients(place, arrays, flagged, pieces, after, cost=0.1):
    eight = low(8, SHARES, 3 * PIECE // 4 + 8, SIDE // 2)
    return call(
        square_gradients_kernel,
        "square_gradients",
        (place,),
        (*arrays, *flagged),
        (eight, eight),
        scratch=[pltpu.VMEM((SIDE, SIDE), F32)] * 2 + [pltpu.VMEM((pieces, 8, SIDE // 2), F32)],
        after=after,
        cost=cost,
        limit=9,
    )


def first_sums_kernel(keep, got, to_x, to_y):
    to_x[...] = total([keep[0:2], got[0:2]]).astype(BF16)
    to_y[...] = total([keep[2:4], got[2:4]]).astype(BF16)


def second_sums_kernel(start, keep, got, from_x, from_y, to_y, to_x):
    to_y[...] = total([keep[start], got[start], from_x[0]]).astype(BF16)
    to_x[...] = total([keep[start + 1], got[start + 1], from_y[0]]).astype(BF16)


def third_sums_kernel(start, place, keep, got, from_x, from_y, then_y, then_x, send, kept):
    half = SIDE // 2
    bit = place[0] & 1
    for out, share_bit in ((send, 1 - bit), (kept, bit)):
        for high in range(SHARES // 2):
            share = 2 * high + share_bit
            a = total([keep[start + 2, share], got[start + 2, share], from_x[1, share], then_y[share]])
            b = total([keep[start + 3, share], got[start + 3, share], from_y[1, share], then_x[share]])
            out[high, :, :half] = a.astype(out.dtype)
            out[high, :, half:] = b.astype(out.dtype)


def fourth_sums_kernel(place, kept, got, send):
    other = 1 - (place[0] >> 1)
    send[...] = total([kept[other], got[other]]).astype(BF16)


def last_sums_kernel(form, place, kept, got, last, *outs):
    mine = place[0] >> 1
    result = total([kept[mine], got[mine], last[...]])
    each = PIECE // 4
    rows = [result[i * each : (i + 1) * each] for i in range(result.shape[0] // each)]
    if form == "tall":
        outs[0][...] = result
    elif form == "wide":
        for i in range(4):
            outs[0][:, i * SIDE : (i + 1) * SIDE] = rows[i]
        outs[1][...] = rows[4]
    else:
        for i in range(3):
            outs[i][...] = rows[i]
        outs[3][...] = result[3 * each :, : SIDE // 2]


class Halving:
    def __init__(self, place, send, keep):
        self.place, self.keep = place, keep
        self.got = [swap_pairs(part, "batch", 1) for part in send]
        self.late = 0 if len(keep) > 1 else 4

    def step(self, kernel, name, scalars, arrays, outs, after, cost=0.5):
        results = call(kernel, name, scalars, arrays, outs, after=after, cost=cost)
        self.done = results[:1]
        return results

    def first(self, after=(), cost=0.5):
        half = low(2, *self.keep[0].shape[1:])
        arrays = (self.keep[0], self.got[0])
        to = self.step(first_sums_kernel, "first_sums", (), arrays, (half, half), after, cost)
        self.from_x, self.from_y = swap_pairs(to[0], "batch", 2), swap_pairs(to[1], "batch", 4)

    def second(self, after=(), cost=0.5):
        quarter = low(*self.keep[0].shape[1:])
        arrays = (self.keep[-1], self.got[-1], self.from_x, self.from_y)
        kernel = functools.partial(second_sums_kernel, self.late)
        to = self.step(kernel, "second_sums", (), arrays, (quarter, quarter), after, cost)
        self.then_y, self.then_x = swap_pairs(to[0], "batch", 4), swap_pairs(to[1], "batch", 2)

    def third(self, after=(), cost=0.5):
        shape = (SHARES // 2, self.keep[0].shape[2], SIDE)
        arrays = (self.keep[-1], self.got[-1], self.from_x, self.from_y, self.then_y, self.then_x)
        outs = (low(*shape), full(*shape))
        kernel = functools.partial(third_sums_kernel, self.late)
        to, self.kept = self.step(kernel, "third_sums", (self.place,), arrays, outs, after, cost)
        self.pair = swap_pairs(to, "seq", 1)

    def fourth(self, after=(), cost=0.5):
        arrays = (self.kept, self.pair)
        outs = (low(*self.kept.shape[1:]),)
        (to,) = self.step(fourth_sums_kernel, "fourth_sums", (self.place,), arrays, outs, after, cost)
        self.others = swap_pairs(to, "seq", 2)

    def last(self, form, after=()):
        each = PIECE // 4
        shapes = {
            "tall": [(PIECE, SIDE)],
            "wide": [(each, 4 * SIDE), (each, SIDE)],
            "square": [(each, SIDE)] * 3 + [(8, SIDE // 2)],
        }[form]
        arrays = (self.kept, self.pair, self.others)
        outs = tuple(full(*shape) for shape in shapes)
        kernel = functools.partial(last_sums_kernel, form)
        self.result = self.step(kernel, "last_sums", (self.place,), arrays, outs, after)


def add_pieces(pieces):
    batch, seq = lax.axis_size("batch"), lax.axis_size("seq")
    parts = [pieces.reshape((2,) * ((batch * seq).bit_length() - 1) + pieces.shape[1:])]
    for axis in ("batch", "seq"):
        bits = lax.axis_size(axis).bit_length() - 1
        for bit in range(bits):
            parts = [total(halve(parts, bits - 1 - bit, axis, bit, F32))]
    return parts[0]


def per_device(
    hidden,
    groups,
    answer_flags,
    lengths,
    answer_embed,
    query_weight,
    query_bias,
    key_weight,
    value_weight,
    value_bias,
    output_weight,
    output_bias,
    first_gain,
    first_shift,
    inner_weight,
    inner_bias,
    outer_weight,
    outer_bias,
    second_gain,
    second_shift,
    cotangent,
):
    items, block_rows, width = hidden.shape
    batch, seq = lax.axis_size("batch"), lax.axis_size("seq")
    me, group = lax.axis_index("seq"), lax.axis_index("batch")
    place = jnp.stack([me, group & 1, (group >> 1) & 1, (group >> 2) & 1]).astype(jnp.int32)
    high = inner_weight.shape[1]
    even = (batch, seq, width, high) == (8, SHARES, SIDE, 4 * SIDE)

    got = exchange(entry_blocks(place, hidden, answer_flags, answer_embed))
    output_near, inner_near, outer_near = load((output_weight, inner_weight, outer_weight), got[1:2])
    upper = exchange(flagged_blocks(place, cotangent, answer_flags, (*got[1:], output_near)))
    acts, queries, keys, values, context, exponents, inverse_sums = attend(
        place,
        lengths,
        groups,
        got,
        (query_weight, query_bias, key_weight, value_weight, value_bias),
        (),
    )
    settled, hat, inverse, active, slope, hat_two, inverse_two, *output = feed(
        place,
        acts,
        context,
        (
            output_near,
            output_bias,
            first_gain,
            first_shift,
            inner_near,
            inner_bias,
            outer_near,
            outer_bias,
            second_gain,
            second_shift,
        ),
        items,
    )
    d_second, branch, sums = turn(place, hat_two, inverse_two, second_gain, upper)
    if even:
        send = tall_gradient(place, active, branch, False)
        keep = tall_gradient(place, active, branch, True, (send,))
        outer = Halving(place, (send,), (keep,))
        outer.first()
        after = outer.done
    else:
        outer_weight_gradient = scatter(dot(active, branch, CONTRACT_FIRST))
        after = ()
    output = exchange(output)
    d_inner, d_first, mixed, d_context, sums = feed_back(
        (
            branch,
            outer_near,
            slope,
            inner_near,
            d_second,
            hat,
            inverse,
            first_gain,
            output_near,
            sums,
        ),
        after,
    )
    if even:
        send, keep = wide_gradient(place, (settled, d_inner, context, mixed))
        inner = Halving(place, (send,), (keep,))
        outer.second((send,))
        after = (*outer.done, *output[1:])
    else:
        inner_weight_gradient = scatter(dot(settled, d_inner, CONTRACT_FIRST))
    d_queries, d_keys, d_values = attend_back(
        (exponents, queries, keys, values, context, inverse_sums, d_context), after
    )
    weights = (query_weight, key_weight, value_weight)
    if even:
        inner.first((d_queries,))
        outer.third(inner.done)
        send, keep = square_gradients(
            place,
            (acts, d_first, d_queries, d_keys, d_values, *weights, sums),
            upper,
            batch * seq,
            outer.done,
        )
        narrow = Halving(place, (send,), (keep,))
        after = (send,)
    input_gradient = entry_back(
        place, (d_first, d_queries, d_keys, d_values, *weights), items, after
    )
    back = exchange(input_gradient)
    if even:
        outer.fourth(input_gradient[:1])
        inner.second(outer.done, cost=25.0)
        narrow.first(inner.done)
        output = join_blocks(place, output, narrow.done)
        outer.last("tall", (output,))
        narrow.second(outer.done)
        inner.third((*narrow.done, back[2]))
        narrow.third((*inner.done, back[3]))
        inner.fourth(narrow.done)
        narrow.fourth(inner.done)
        inner.last("wide", narrow.done)
        narrow.last("square")
        (outer_weight_gradient,), (inner_weight_gradient, output_weight_gradient) = outer.result, inner.result
        *narrow, pieces = narrow.result
        input_gradient = join_blocks(place, back, narrow[:0])
    else:
        squares = jnp.concatenate(
            [
                dot(left, right, CONTRACT_FIRST).astype(BF16)
                for left, right in (
                    (context, mixed),
                    (acts, d_queries),
                    (acts, d_keys),
                    (acts, d_values),
                )
            ],
            1,
        )
        output_weight_gradient, *narrow = jnp.split(scatter(squares), 4, 1)
        pieces = add_pieces(
            vector_pieces(
                place, (d_first, d_queries, d_keys, d_values, *weights, sums), upper, batch * seq
            )
        )
        output = join_blocks(place, output)
        input_gradient = join_blocks(place, back)
    query_weight_gradient, key_weight_gradient, value_weight_gradient = narrow
    early, later = pieces[:, : width // (batch * seq)], pieces[:, LANES : LANES + width // (batch * seq)]
    return (
        output,
        input_gradient,
        later[0:2],
        query_weight_gradient,
        later[2],
        key_weight_gradient,
        value_weight_gradient,
        later[3],
        output_weight_gradient,
        early[0],
        early[1],
        early[2],
        inner_weight_gradient,
        pieces[0, 2 * LANES : 2 * LANES + high // (batch * seq)],
        outer_weight_gradient,
        early[3],
        early[4],
        early[5],
    )


def solution(mesh):
    both = ("batch", "seq")
    in_specs = (
        (P("batch", "seq", None), P("batch", None), P("batch", "seq"), P("batch"))
        + (P(),) * 16
        + (P("batch", "seq", None),)
    )
    matrix, vector = P(both, None), P(both)
    out_specs = (
        P("batch", "seq", None),
        P("batch", "seq", None),
        P(None, both),
        matrix,
        vector,
        matrix,
        matrix,
        vector,
        matrix,
        vector,
        vector,
        vector,
        matrix,
        vector,
        matrix,
        vector,
        vector,
        vector,
    )
    return jax.shard_map(
        per_device, mesh=mesh, in_specs=in_specs, out_specs=out_specs, check_vma=False
    )
```

```python
import functools
import math

import jax
import jax.numpy as jnp
from jax import lax
from jax.experimental import pallas as pl
from jax.experimental.pallas import tpu as pltpu
from jax.sharding import PartitionSpec as P

HEAD_DIM = 64
LANES = 128
EPSILON = 1e-12
BF16 = jnp.bfloat16
F32 = jnp.float32

CONTRACT_LAST = (((1,), (1,)), ((), ()))
CONTRACT_FIRST = (((0,), (0,)), ((), ()))
GROUPS, SHARES, PIECE, SIDE = 4, 4, 96, 768
MICROSECOND = 1150000000
PARTS = 4


def dot(a, b, dims=(((1,), (0,)), ((), ()))):
    return lax.dot_general(a, b, dims, preferred_element_type=F32)


def low(*shape):
    return jax.ShapeDtypeStruct(shape, BF16)


def full(*shape):
    return jax.ShapeDtypeStruct(shape, F32)


def call(kernel, name, scalars, arrays, outs, limit=4, scratch=(), far=(), after=(), cost=4.0):
    count = len(scalars) + len(arrays) + len(far)

    def body(*refs):
        kernel(*refs[:count], *refs[count + len(after) :])

    single = not isinstance(outs, tuple)
    vmem, hbm = pl.BlockSpec(memory_space=pltpu.VMEM), pl.BlockSpec(memory_space=pltpu.HBM)
    return pl.pallas_call(
        body,
        in_specs=[pl.BlockSpec(memory_space=pltpu.SMEM)] * len(scalars)
        + [vmem] * len(arrays)
        + [hbm] * len(far)
        + [pl.BlockSpec(memory_space=pl.ANY)] * len(after),
        out_specs=vmem if single else (vmem,) * len(outs),
        out_shape=outs,
        scratch_shapes=list(scratch),
        compiler_params=pltpu.CompilerParams(vmem_limit_bytes=int(limit * (1 << 20))),
        cost_estimate=pl.CostEstimate(flops=int(cost * MICROSECOND), bytes_accessed=1 << 16, transcendentals=0),
        name=name,
    )(*scalars, *arrays, *(pltpu.with_memory_space_constraint(a, pltpu.HBM) for a in far), *after)


def fetch(sources, targets, semaphores, parts=1):
    copies = []
    for source, target in zip(sources, targets):
        rows = source.shape[0] // parts
        for part in range(parts):
            own = pl.ds(part * rows, rows)
            copies.append(
                pltpu.make_async_copy(source.at[own], target.at[own], semaphores.at[len(copies)])
            )
    for copy in copies:
        copy.start()
    return copies


def line(ref):
    return ref[...].astype(F32)[None]


def block_rows_of(place, mask, each):
    return pl.ds(pl.multiple_of((place[0] ^ mask) * each, each), each)


def entry_kernel(count, place, *refs):
    sources, outs, (hidden, flags, embed, semaphores) = refs[:3], refs[3 : 3 + count], refs[3 + count :]
    for copy in fetch(sources, (hidden, flags, embed), semaphores):
        copy.wait()
    rows = hidden.shape[1]
    row = lax.broadcasted_iota(jnp.int32, (rows, rows), 0)
    column = lax.broadcasted_iota(jnp.int32, (rows, rows), 1)
    first, second = embed[0:1].astype(F32), embed[1:2].astype(F32)
    for mask in range(count):
        item = place[0] ^ mask
        flag = flags[pl.ds(item, 1), :].astype(F32)
        upright = jnp.sum(jnp.where(row == column, flag, 0.0), 1, keepdims=True)
        added = jnp.where(upright == 1.0, second, first)
        outs[mask][...] = (hidden[item].astype(F32) + added).astype(BF16)


def entry_blocks(place, *arrays):
    count, rows, width = arrays[0].shape
    return call(
        functools.partial(entry_kernel, count),
        "entry_blocks",
        (place,),
        (),
        (low(rows, width),) * count,
        scratch=[pltpu.VMEM(a.shape, a.dtype) for a in arrays] + [pltpu.SemaphoreType.DMA((3,))],
        far=arrays,
    )


def flagged_kernel(count, place, cotangent, flags, *outs):
    rows = cotangent.shape[1]
    for mask in range(count):
        item = place[0] ^ mask
        outs[mask][pl.ds(0, rows), :] = cotangent[item]
        outs[mask][pl.ds(rows, 16), :] = jnp.zeros((16, cotangent.shape[2]), BF16)
        flag = jnp.broadcast_to(flags[pl.ds(item, 1), :].astype(F32), (16, rows))
        outs[mask][pl.ds(rows, 16), pl.ds(0, rows)] = flag.astype(BF16)


def flagged_blocks(place, cotangent, flags, after):
    count, rows, width = cotangent.shape
    return call(
        functools.partial(flagged_kernel, count),
        "flagged_blocks",
        (place,),
        (cotangent, flags),
        (low(rows + 16, width),) * count,
        after=after,
    )


def join_kernel(count, place, *refs):
    for mask in range(count):
        refs[count][place[0] ^ mask] = refs[mask][...]


def join_blocks(place, blocks, after=()):
    return call(
        functools.partial(join_kernel, len(blocks)),
        "join_blocks",
        (place,),
        blocks,
        low(len(blocks), *blocks[0].shape),
        after=after,
        cost=0.5,
    )


def swap_pairs(array, axis, mask):
    size = lax.axis_size(axis)
    return lax.ppermute(array, axis, [(i, i ^ mask) for i in range(size)])


def pick(array, index, dim):
    return lax.dynamic_index_in_dim(array, index, dim, keepdims=False)


def exchange(blocks):
    order = sorted(range(1, len(blocks)), key=lambda mask: mask < 2)
    got = {mask: swap_pairs(blocks[mask], "seq", mask) for mask in order}
    return [blocks[0]] + [got[mask] for mask in range(1, len(blocks))]


def total(parts):
    result = parts[0].astype(F32)
    for part in parts[1:]:
        result = result + part.astype(F32)
    return result


def halve(parts, dim, axis, bit, dtype=BF16):
    mine = (lax.axis_index(axis) >> bit) & 1
    sent = total([pick(part, 1 - mine, dim) for part in parts]).astype(dtype)
    got = swap_pairs(sent, axis, 1 << bit)
    return [pick(part, mine, dim) for part in parts] + [got]


def scatter(gradient):
    batch, seq = lax.axis_size("batch"), lax.axis_size("seq")
    rows, columns = gradient.shape
    batch_bits, seq_bits = batch.bit_length() - 1, seq.bit_length() - 1
    each = rows // (batch * seq)
    shape = (2,) * (batch_bits + seq_bits) + (each, columns)
    parts = [gradient.astype(BF16).reshape(shape)]
    parts = halve(parts, batch_bits - 1, "batch", 0)
    ways = []
    for way in range(2):
        half = [
            lax.slice_in_dim(part, way * (columns // 2), (way + 1) * (columns // 2), axis=part.ndim - 1)
            for part in parts
        ]
        bits = list(range(1, batch_bits))
        if way:
            bits = bits[::-1]
        left = list(range(batch_bits - 1, 0, -1))
        for bit in bits:
            dim = left.index(bit)
            half = halve(half, dim, "batch", bit)
            left.remove(bit)
        ways.append(half)
    parts = [jnp.concatenate([a, b], -1) for a, b in zip(*ways)]
    for bit in range(seq_bits):
        parts = halve(parts, seq_bits - 1 - bit, "seq", bit)
    return total(parts)


def norm_parts(values):
    centre = values - jnp.mean(values, -1, keepdims=True)
    inverse = lax.rsqrt(jnp.mean(centre * centre, -1, keepdims=True) + EPSILON)
    return centre * inverse, inverse


def norm_back(upper, hat, inverse, gain):
    g = upper * gain
    return inverse * (
        g - jnp.mean(g, -1, keepdims=True) - hat * jnp.mean(g * hat, -1, keepdims=True)
    )


def gate_parts(u):
    share = 0.5 + 0.5 * lax.erf(u * 0.7071067811865476)
    return u * share, share + u * (jnp.exp(-0.5 * u * u) * 0.3989422804014327)


def load_kernel(*refs):
    count = len(refs) // 2
    for copy in fetch(refs[:count], refs[count:-1], refs[-1], PARTS):
        copy.wait()


def load(weights, after):
    return call(
        load_kernel,
        "load",
        (),
        (),
        tuple(low(*weight.shape) for weight in weights),
        scratch=[pltpu.SemaphoreType.DMA((PARTS * len(weights),))],
        far=weights,
        after=after,
    )


def attend_kernel(count, place, lengths, groups, *refs):
    blocks = refs[:count]
    query_weight, query_bias, key_weight, value_weight, value_bias = refs[count : count + 5]
    acts, q_ref, k_ref, v_ref, o_ref, e_ref, inverse_ref, bias = refs[count + 5 :]
    rows, width = acts.shape
    each = rows // count
    for mask in range(count):
        acts[block_rows_of(place, mask, each), :] = blocks[mask][...]
    ids = groups[pl.ds(place[0], 1), :].astype(F32)
    key_place = lax.broadcasted_iota(jnp.int32, (1, rows), 1)
    key_ids = jnp.where(key_place < lengths[place[0]], ids, 1e9)
    upright = jnp.transpose(jnp.broadcast_to(ids, (8, rows)))[:, :1]
    bias[...] = jnp.where(key_ids <= upright, 0.0, -1e30)
    place_of = lax.broadcasted_iota(jnp.int32, (rows, LANES), 1)
    lane = place_of // HEAD_DIM
    inverses = jnp.zeros((rows, LANES), F32)
    tile = 2 * LANES
    for start in range(0, width, tile):
        part = slice(start, start + tile)
        x = acts[...]
        q = (dot(x, query_weight[:, part]) + line(query_bias)[:, part]).astype(BF16)
        k = dot(x, key_weight[:, part]).astype(BF16)
        v = (dot(x, value_weight[:, part]) + line(value_bias)[:, part]).astype(BF16)
        q_ref[:, part] = q
        k_ref[:, part] = k
        v_ref[:, part] = v
        q = q * jnp.asarray(1.0 / math.sqrt(HEAD_DIM), BF16)
        for pair in range(tile // LANES):
            at = slice(pair * LANES, (pair + 1) * LANES)
            q2, k2, v2 = q[:, at], k[:, at], v[:, at]
            sums = []
            for head in range(2):
                mine = lane == head
                s = dot(jnp.where(mine, q2, jnp.zeros_like(q2)), k2, CONTRACT_LAST) + bias[...]
                e = jnp.exp(s - jnp.max(s, -1, keepdims=True)).astype(BF16)
                e_ref[(start + pair * LANES) // HEAD_DIM + head] = e
                sums.append(dot(e, jnp.where(mine, v2, jnp.ones_like(v2))))
            top = jnp.where(lane == 0, sums[0], sums[1])
            under = pltpu.roll(jnp.where(lane == 0, sums[1], sums[0]), HEAD_DIM, 1)
            inverse = 1.0 / under
            first = (start + pair * LANES) // HEAD_DIM
            inverses = jnp.where(place_of == first, inverse, inverses)
            inverses = jnp.where(place_of == first + 1, pltpu.roll(inverse, HEAD_DIM, 1), inverses)
            o_ref[:, start + pair * LANES : start + (pair + 1) * LANES] = (top * inverse).astype(BF16)
    inverse_ref[...] = inverses


def attend(place, lengths, groups, blocks, weights, after):
    each, width = blocks[0].shape
    rows = len(blocks) * each
    wide = low(rows, width)
    return call(
        functools.partial(attend_kernel, len(blocks)),
        "attend",
        (place, lengths),
        (groups, *blocks, *weights),
        (wide, wide, wide, wide, wide, low(width // HEAD_DIM, rows, rows), full(rows, LANES)),
        scratch=[pltpu.VMEM((rows, rows), F32)],
        limit=6,
        after=after,
    )


def attend_back_kernel(e_ref, q_ref, k_ref, v_ref, o_ref, inverse_ref, do_ref, dq_ref, dk_ref, dv_ref):
    rows, width = q_ref.shape
    scale = 1.0 / math.sqrt(HEAD_DIM)
    lane = lax.broadcasted_iota(jnp.int32, (rows, LANES), 1) // HEAD_DIM
    for pair in range(width // LANES):
        at = slice(pair * LANES, (pair + 1) * LANES)
        q, k, v = q_ref[:, at], k_ref[:, at], v_ref[:, at]
        inverse = jnp.where(
            lane == 0, inverse_ref[:, 2 * pair : 2 * pair + 1], inverse_ref[:, 2 * pair + 1 : 2 * pair + 2]
        )
        do = do_ref[:, at].astype(F32) * inverse
        weighed = do * o_ref[:, at].astype(F32)
        do = do.astype(BF16)
        q_up, do_up = jnp.transpose(q), jnp.transpose(do)
        dq, dk, dv = [], [], []
        for head in range(2):
            mine = lane == head
            part = slice(head * HEAD_DIM, (head + 1) * HEAD_DIM)
            row_dot = jnp.sum(jnp.where(mine, weighed, 0.0), -1, keepdims=True)
            d = dot(jnp.where(mine, do, jnp.zeros_like(do)), v, CONTRACT_LAST) - row_dot
            e = e_ref[2 * pair + head]
            ds = (e.astype(F32) * d).astype(BF16)
            dq.append(dot(ds, k))
            dk.append(dot(q_up[part], ds))
            dv.append(dot(do_up[part], e))
        dq_ref[:, at] = (jnp.where(lane == 0, dq[0], dq[1]) * scale).astype(BF16)
        dk_ref[:, at] = (jnp.transpose(jnp.concatenate(dk, 0)) * scale).astype(BF16)
        dv_ref[:, at] = jnp.transpose(jnp.concatenate(dv, 0)).astype(BF16)


def attend_back(arrays, after):
    wide = low(*arrays[1].shape)
    return call(
        attend_back_kernel,
        "attend_back",
        (),
        arrays,
        (wide, wide, wide),
        limit=5.5,
        after=after,
        cost=30.0,
    )


def feed_kernel(count, place, *refs):
    (acts, context, output_weight, output_bias, first_gain, first_shift, inner_weight, inner_bias) = refs[:8]
    outer_weight, outer_bias, second_gain, second_shift = refs[8:12]
    settled_low, hat_ref, inverse_ref, active_ref, slope_ref, hat_two, inverse_two = refs[12:19]
    outs = refs[19 : 19 + count]
    acc = refs[19 + count]
    rows, high = active_ref.shape
    hat, inverse = norm_parts(
        acts[...].astype(F32) + dot(context[...], output_weight[...]) + line(output_bias)
    )
    hat_ref[...] = hat.astype(BF16)
    inverse_ref[...] = jnp.broadcast_to(inverse, inverse_ref.shape)
    settled = hat * line(first_gain) + line(first_shift)
    settled_low[...] = settled.astype(BF16)
    acc[...] = settled + line(outer_bias)
    tile = 4 * LANES
    for start in range(0, high, tile):
        part = slice(start, start + tile)
        inner = dot(settled_low[...], inner_weight[:, part]) + line(inner_bias)[:, part]
        active, slope = gate_parts(inner)
        active_ref[:, part] = active.astype(BF16)
        slope_ref[:, part] = slope.astype(BF16)
    acc[...] += dot(active_ref[...], outer_weight[...])
    each = rows // count
    gain, shift = line(second_gain), line(second_shift)
    for mask in range(count):
        own = block_rows_of(place, mask, each)
        hat, inverse = norm_parts(acc[own, :])
        outs[mask][...] = (hat * gain + shift).astype(BF16)
        hat_two[own, :] = hat
        inverse_two[own, :] = jnp.broadcast_to(inverse, (each, LANES))


def feed(place, acts, context, weights, count):
    rows, width = acts.shape
    high = weights[4].shape[1]
    wide = low(rows, width)
    return call(
        functools.partial(feed_kernel, count),
        "feed",
        (place,),
        (acts, context, *weights),
        (
            wide,
            wide,
            full(rows, LANES),
            low(rows, high),
            low(rows, high),
            full(rows, width),
            full(rows, LANES),
        )
        + (low(rows // count, width),) * count,
        limit=7.5,
        scratch=[pltpu.VMEM((rows, width), F32)],
    )


def turn_kernel(count, place, hat_two, inverse_two, second_gain, *refs):
    cotangents = refs[:count]
    d_second, branch, sums = refs[count:]
    each = hat_two.shape[0] // count
    gain = line(second_gain)
    totals = [0.0, 0.0, 0.0]
    for mask in range(count):
        own = block_rows_of(place, mask, each)
        hat = hat_two[own, :]
        upper = cotangents[mask][pl.ds(0, each), :].astype(F32)
        d = norm_back(upper, hat, inverse_two[own, :1], gain)
        d_low = d.astype(BF16)
        d_second[own, :] = d
        branch[own, :] = d_low
        for i, term in enumerate((d_low.astype(F32), upper * hat, upper)):
            totals[i] = totals[i] + jnp.sum(term, 0, keepdims=True)
    for i in range(3):
        sums[i : i + 1, :] = totals[i]


def turn(place, hat_two, inverse_two, second_gain, cotangents):
    rows, width = hat_two.shape
    return call(
        functools.partial(turn_kernel, len(cotangents)),
        "turn",
        (place,),
        (hat_two, inverse_two, second_gain, *cotangents),
        (full(rows, width), low(rows, width), full(8, width)),
    )


def feed_back_kernel(
    branch,
    outer_weight,
    slope,
    inner_weight,
    d_second,
    hat_ref,
    inverse_ref,
    first_gain,
    output_weight,
    turn_sums,
    d_inner_ref,
    d_first_ref,
    mixed,
    d_context,
    sums,
    acc,
):
    rows, high = slope.shape
    width = acc.shape[1]
    tile = 4 * LANES
    for start in range(0, high, tile):
        part = slice(start, start + tile)
        d_active = dot(branch[...], outer_weight[part, :], CONTRACT_LAST)
        d_inner = (d_active * slope[:, part].astype(F32)).astype(BF16)
        d_inner_ref[:, part] = d_inner
        partial = jnp.sum(d_inner.astype(F32), 0, keepdims=True)
        for lane in range(start, start + tile, LANES):
            row = 6 + lane // width
            sums[row : row + 1, lane % width : lane % width + LANES] = partial[:, lane - start : lane - start + LANES]
    acc[...] = d_second[...] + dot(d_inner_ref[...], inner_weight[...], CONTRACT_LAST)
    parts = 4
    totals = [0.0, 0.0, 0.0]
    gain = line(first_gain)
    for part in range(parts):
        own = slice(part * (rows // parts), (part + 1) * (rows // parts))
        upper = acc[own, :]
        hat = hat_ref[own, :].astype(F32)
        d = norm_back(upper, hat, inverse_ref[own, :1], gain)
        d_low = d.astype(BF16)
        d_first_ref[own, :] = d
        mixed[own, :] = d_low
        for i, term in enumerate((d_low.astype(F32), upper * hat, upper)):
            totals[i] = totals[i] + jnp.sum(term, 0, keepdims=True)
    for i in range(3):
        sums[i : i + 1, :] = totals[i]
    sums[3:6, :] = turn_sums[0:3, :]
    d_context[...] = dot(mixed[...], output_weight[...], CONTRACT_LAST).astype(BF16)


def feed_back(arrays, after):
    rows, width = arrays[0].shape
    high = arrays[2].shape[1]
    wide = low(rows, width)
    return call(
        feed_back_kernel,
        "feed_back",
        (),
        arrays,
        (low(rows, high), full(rows, width), wide, wide, full(16, width)),
        scratch=[pltpu.VMEM((rows, width), F32)],
        after=after,
        cost=30.0,
        limit=5,
    )


def entry_back_kernel(count, place, d_first, dq, dk, dv, wq, wk, wv, *refs):
    outs, acc = refs[:count], refs[count]
    each = dq.shape[0] // count
    acc[...] = (
        d_first[...]
        + dot(dq[...], wq[...], CONTRACT_LAST)
        + dot(dk[...], wk[...], CONTRACT_LAST)
        + dot(dv[...], wv[...], CONTRACT_LAST)
    )
    for mask in range(count):
        outs[mask][...] = acc[block_rows_of(place, mask, each), :].astype(BF16)


def entry_back(place, arrays, count, after):
    rows, width = arrays[1].shape
    return call(
        functools.partial(entry_back_kernel, count),
        "entry_back",
        (place,),
        arrays,
        (low(rows // count, width),) * count,
        scratch=[pltpu.VMEM((rows, width), F32)],
        after=after,
        limit=4,
    )


def add_vectors(place, d_first, dq, dk, dv, weights, early_sums, flagged, sums):
    count = len(flagged)
    each, width = dq.shape[0] // count, dq.shape[1]
    row = lax.broadcasted_iota(jnp.int32, (each, each), 0)
    column = lax.broadcasted_iota(jnp.int32, (each, each), 1)
    zero, one = [0.0] * 4, [0.0] * 4
    for mask in range(count):
        own = block_rows_of(place, mask, each)
        flag = flagged[mask][pl.ds(each, 16), pl.ds(0, each)][:1].astype(F32)
        upright = jnp.sum(jnp.where(row == column, flag, 0.0), 1, keepdims=True)
        for i, array in enumerate((d_first, dq, dk, dv)):
            value = array[own, :].astype(F32)
            zero[i] = zero[i] + jnp.sum(value * (1.0 - upright), 0, keepdims=True)
            one[i] = one[i] + jnp.sum(value * upright, 0, keepdims=True)
    by_flag = jnp.concatenate([zero[0], one[0]] + [jnp.zeros((6, width), F32)], 0)
    for i, weight in enumerate(weights):
        pair = jnp.concatenate([zero[i + 1], one[i + 1]] + [jnp.zeros((6, width), F32)], 0)
        by_flag = by_flag + dot(pair.astype(BF16), weight[...], CONTRACT_LAST)
    second = jnp.concatenate([by_flag[:2], zero[1] + one[1], zero[3] + one[3]], 0)
    first = early_sums[0:6, :]
    pieces = sums.shape[0]
    piece = width // pieces
    sums[...] = jnp.zeros(sums.shape, F32)
    for i in range(pieces):
        part = slice(i * piece, (i + 1) * piece)
        at, lane = divmod(i * 4 * piece, width)
        sums[i, 0:6, 0:piece] = first[:, part]
        sums[i, 0:4, LANES : LANES + piece] = second[:, part]
        sums[i, 0:1, 2 * LANES : 2 * LANES + 4 * piece] = early_sums[6 + at : 7 + at, lane : lane + 4 * piece]


def vector_pieces_kernel(place, d_first, dq, dk, dv, wq, wk, wv, early_sums, *refs):
    add_vectors(place, d_first, dq, dk, dv, (wq, wk, wv), early_sums, refs[:-1], refs[-1])


def vector_pieces(place, arrays, flagged, pieces):
    return call(
        vector_pieces_kernel,
        "vector_pieces",
        (place,),
        (*arrays, *flagged),
        full(pieces, 8, SIDE // 2),
    )


def parts_of(place):
    x, y = place[2], place[3]
    far, beside, behind, own = 2 * (1 - y) + 1 - x, 2 * y + 1 - x, 2 * (1 - y) + x, 2 * y + x
    return ((far, 0), (beside, 0), (far, 1), (behind, 1), (behind, 0), (beside, 1), (own, 0), (own, 1))


def tall_gradient_kernel(keep, place, left, right, out):
    rows = left.shape[1] // GROUPS // 2
    core = place[1] if keep else 1 - place[1]
    parts = parts_of(place)
    half = SIDE // 2
    for group, homes in ((0, (0, 2)), (1, (1, 5)), (3, (4, 3)), (6, (6, 7))):
        columns = pl.ds(pl.multiple_of((2 * parts[group][0] + core) * rows, LANES), rows)
        product = dot(left[:, columns], right[...], CONTRACT_FIRST).reshape(SHARES, PIECE, SIDE)
        for side, home in enumerate(homes):
            out[home] = product[:, :, side * half : (side + 1) * half].astype(BF16)


def tall_gradient(place, left, right, keep, after=(), cost=2.0):
    return call(
        functools.partial(tall_gradient_kernel, keep),
        "tall_gradient",
        (place,),
        (left, right),
        low(8, SHARES, PIECE, SIDE // 2),
        after=after,
        cost=cost,
    )


def stack_pieces(place, totals, send, keep, start, last=None):
    each = SIDE // (GROUPS * SHARES * 2)
    half = SIDE // 2
    for out, core in ((send, 1 - place[1]), (keep, place[1])):
        for home, (group, side) in enumerate(parts_of(place)):
            columns = slice(side * half, (side + 1) * half)
            for share in range(SHARES):
                index = (2 * group + core) * SHARES + share
                row = pl.multiple_of(index * each, 8)
                pieces = [t[pl.ds(row, each), columns] for t in totals]
                if last is not None:
                    pieces.append(last[index] if side == 0 else jnp.zeros(last.shape[1:], F32))
                piece = jnp.concatenate(pieces, 0)
                out[home, share, start : start + piece.shape[0], :] = piece.astype(BF16)


def wide_gradient_kernel(place, left, right, context, mixed, send, keep, first, second):
    for half in range(2):
        start = 2 * half * SIDE
        first[...] = dot(left[...], right[:, start : start + SIDE], CONTRACT_FIRST)
        second[...] = dot(left[...], right[:, start + SIDE : start + 2 * SIDE], CONTRACT_FIRST)
        stack_pieces(place, (first, second), send, keep, half * PIECE // 2)
    first[...] = dot(context[...], mixed[...], CONTRACT_FIRST)
    stack_pieces(place, (first,), send, keep, PIECE)


def wide_gradient(place, arrays, cost=1.0):
    eight = low(8, SHARES, PIECE + PIECE // 4, SIDE // 2)
    return call(
        wide_gradient_kernel,
        "wide_gradient",
        (place,),
        arrays,
        (eight, eight),
        scratch=[pltpu.VMEM((SIDE, SIDE), F32)] * 2,
        cost=cost,
        limit=6.5,
    )


def square_gradients_kernel(place, acts, d_first, dq, dk, dv, wq, wk, wv, early_sums, *refs):
    flagged, (send, keep, first, second, sums) = refs[:-5], refs[-5:]
    first[...] = dot(acts[...], dq[...], CONTRACT_FIRST)
    second[...] = dot(acts[...], dk[...], CONTRACT_FIRST)
    add_vectors(place, d_first, dq, dk, dv, (wq, wk, wv), early_sums, flagged, sums)
    stack_pieces(place, (first, second), send, keep, 0)
    first[...] = dot(acts[...], dv[...], CONTRACT_FIRST)
    stack_pieces(place, (first,), send, keep, PIECE // 2, sums)


def square_gradients(place, arrays, flagged, pieces, after, cost=0.1):
    eight = low(8, SHARES, 3 * PIECE // 4 + 8, SIDE // 2)
    return call(
        square_gradients_kernel,
        "square_gradients",
        (place,),
        (*arrays, *flagged),
        (eight, eight),
        scratch=[pltpu.VMEM((SIDE, SIDE), F32)] * 2 + [pltpu.VMEM((pieces, 8, SIDE // 2), F32)],
        after=after,
        cost=cost,
        limit=8,
    )


def first_sums_kernel(keep, got, to_x, to_y):
    to_x[...] = total([keep[0:2], got[0:2]]).astype(BF16)
    to_y[...] = total([keep[2:4], got[2:4]]).astype(BF16)


def second_sums_kernel(start, keep, got, from_x, from_y, to_y, to_x):
    to_y[...] = total([keep[start], got[start], from_x[0]]).astype(BF16)
    to_x[...] = total([keep[start + 1], got[start + 1], from_y[0]]).astype(BF16)


def third_sums_kernel(start, place, keep, got, from_x, from_y, then_y, then_x, send, kept):
    half = SIDE // 2
    bit = place[0] & 1
    for out, share_bit in ((send, 1 - bit), (kept, bit)):
        for high in range(SHARES // 2):
            share = 2 * high + share_bit
            a = total([keep[start + 2, share], got[start + 2, share], from_x[1, share], then_y[share]])
            b = total([keep[start + 3, share], got[start + 3, share], from_y[1, share], then_x[share]])
            out[high, :, :half] = a.astype(out.dtype)
            out[high, :, half:] = b.astype(out.dtype)


def fourth_sums_kernel(place, kept, got, send):
    other = 1 - (place[0] >> 1)
    send[...] = total([kept[other], got[other]]).astype(BF16)


def last_sums_kernel(form, place, kept, got, last, *outs):
    mine = place[0] >> 1
    result = total([kept[mine], got[mine], last[...]])
    each = PIECE // 4
    rows = [result[i * each : (i + 1) * each] for i in range(result.shape[0] // each)]
    if form == "tall":
        outs[0][...] = result
    elif form == "wide":
        for i in range(4):
            outs[0][:, i * SIDE : (i + 1) * SIDE] = rows[i]
        outs[1][...] = rows[4]
    else:
        for i in range(3):
            outs[i][...] = rows[i]
        outs[3][...] = result[3 * each :, : SIDE // 2]


class Halving:
    def __init__(self, place, send, keep):
        self.place, self.keep = place, keep
        self.got = [swap_pairs(part, "batch", 1) for part in send]
        self.late = 0 if len(keep) > 1 else 4

    def step(self, kernel, name, scalars, arrays, outs, after, cost=0.5):
        results = call(kernel, name, scalars, arrays, outs, after=after, cost=cost)
        self.done = results[:1]
        return results

    def first(self, after=(), cost=0.5):
        half = low(2, *self.keep[0].shape[1:])
        arrays = (self.keep[0], self.got[0])
        to = self.step(first_sums_kernel, "first_sums", (), arrays, (half, half), after, cost)
        self.from_x, self.from_y = swap_pairs(to[0], "batch", 2), swap_pairs(to[1], "batch", 4)

    def second(self, after=(), cost=0.5):
        quarter = low(*self.keep[0].shape[1:])
        arrays = (self.keep[-1], self.got[-1], self.from_x, self.from_y)
        kernel = functools.partial(second_sums_kernel, self.late)
        to = self.step(kernel, "second_sums", (), arrays, (quarter, quarter), after, cost)
        self.then_y, self.then_x = swap_pairs(to[0], "batch", 4), swap_pairs(to[1], "batch", 2)

    def third(self, after=(), cost=0.5):
        shape = (SHARES // 2, self.keep[0].shape[2], SIDE)
        arrays = (self.keep[-1], self.got[-1], self.from_x, self.from_y, self.then_y, self.then_x)
        outs = (low(*shape), full(*shape))
        kernel = functools.partial(third_sums_kernel, self.late)
        to, self.kept = self.step(kernel, "third_sums", (self.place,), arrays, outs, after, cost)
        self.pair = swap_pairs(to, "seq", 1)

    def fourth(self, after=(), cost=0.5):
        arrays = (self.kept, self.pair)
        outs = (low(*self.kept.shape[1:]),)
        (to,) = self.step(fourth_sums_kernel, "fourth_sums", (self.place,), arrays, outs, after, cost)
        self.others = swap_pairs(to, "seq", 2)

    def last(self, form, after=()):
        each = PIECE // 4
        shapes = {
            "tall": [(PIECE, SIDE)],
            "wide": [(each, 4 * SIDE), (each, SIDE)],
            "square": [(each, SIDE)] * 3 + [(8, SIDE // 2)],
        }[form]
        arrays = (self.kept, self.pair, self.others)
        outs = tuple(full(*shape) for shape in shapes)
        kernel = functools.partial(last_sums_kernel, form)
        self.result = self.step(kernel, "last_sums", (self.place,), arrays, outs, after)


def add_pieces(pieces):
    batch, seq = lax.axis_size("batch"), lax.axis_size("seq")
    parts = [pieces.reshape((2,) * ((batch * seq).bit_length() - 1) + pieces.shape[1:])]
    for axis in ("batch", "seq"):
        bits = lax.axis_size(axis).bit_length() - 1
        for bit in range(bits):
            parts = [total(halve(parts, bits - 1 - bit, axis, bit, F32))]
    return parts[0]


def per_device(
    hidden,
    groups,
    answer_flags,
    lengths,
    answer_embed,
    query_weight,
    query_bias,
    key_weight,
    value_weight,
    value_bias,
    output_weight,
    output_bias,
    first_gain,
    first_shift,
    inner_weight,
    inner_bias,
    outer_weight,
    outer_bias,
    second_gain,
    second_shift,
    cotangent,
):
    items, block_rows, width = hidden.shape
    batch, seq = lax.axis_size("batch"), lax.axis_size("seq")
    me, group = lax.axis_index("seq"), lax.axis_index("batch")
    place = jnp.stack([me, group & 1, (group >> 1) & 1, (group >> 2) & 1]).astype(jnp.int32)
    high = inner_weight.shape[1]
    even = (batch, seq, width, high) == (8, SHARES, SIDE, 4 * SIDE)

    blocks = entry_blocks(place, hidden, answer_flags, answer_embed)
    got = exchange(blocks)
    output_near, inner_near, outer_near = load((output_weight, inner_weight, outer_weight), blocks[:1])
    upper = exchange(flagged_blocks(place, cotangent, answer_flags, (*got[2:], output_near)))
    acts, queries, keys, values, context, exponents, inverse_sums = attend(
        place,
        lengths,
        groups,
        got,
        (query_weight, query_bias, key_weight, value_weight, value_bias),
        (),
    )
    settled, hat, inverse, active, slope, hat_two, inverse_two, *output = feed(
        place,
        acts,
        context,
        (
            output_near,
            output_bias,
            first_gain,
            first_shift,
            inner_near,
            inner_bias,
            outer_near,
            outer_bias,
            second_gain,
            second_shift,
        ),
        items,
    )
    d_second, branch, sums = turn(place, hat_two, inverse_two, second_gain, upper)
    if even:
        send = tall_gradient(place, active, branch, False)
        keep = tall_gradient(place, active, branch, True, (send,))
        outer = Halving(place, (send,), (keep,))
        outer.first()
        after = outer.done
    else:
        outer_weight_gradient = scatter(dot(active, branch, CONTRACT_FIRST))
        after = ()
    output = exchange(output)
    d_inner, d_first, mixed, d_context, sums = feed_back(
        (
            branch,
            outer_near,
            slope,
            inner_near,
            d_second,
            hat,
            inverse,
            first_gain,
            output_near,
            sums,
        ),
        after,
    )
    if even:
        send, keep = wide_gradient(place, (settled, d_inner, context, mixed))
        inner = Halving(place, (send,), (keep,))
        outer.second((send,))
        after = (*outer.done, *output[1:])
    else:
        inner_weight_gradient = scatter(dot(settled, d_inner, CONTRACT_FIRST))
    weights = (query_weight, key_weight, value_weight)
    d_queries, d_keys, d_values = attend_back(
        (exponents, queries, keys, values, context, inverse_sums, d_context),
        after,
    )
    if even:
        inner.first((d_queries,))
        outer.third(inner.done)
        after = outer.done
    input_gradient = entry_back(
        place, (d_first, d_queries, d_keys, d_values, *weights), items, after
    )
    back = exchange(input_gradient)
    if even:
        send, keep = square_gradients(
            place,
            (acts, d_first, d_queries, d_keys, d_values, *weights, sums),
            upper,
            batch * seq,
            input_gradient[:1],
        )
        narrow = Halving(place, (send,), (keep,))
        outer.fourth((send, back[2]))
        inner.second(outer.done, cost=25.0)
        narrow.first(inner.done)
        output = join_blocks(place, output, narrow.done)
        narrow.second((output, back[3]))
        inner.third((*narrow.done, outer.others))
        narrow.third((*inner.done, back[1]))
        outer.last("tall", narrow.done)
        inner.fourth(outer.done)
        narrow.fourth(inner.done)
        inner.last("wide", narrow.done)
        narrow.last("square")
        (outer_weight_gradient,), (inner_weight_gradient, output_weight_gradient) = outer.result, inner.result
        *narrow, pieces = narrow.result
        input_gradient = join_blocks(place, back, narrow[:0])
    else:
        squares = jnp.concatenate(
            [
                dot(left, right, CONTRACT_FIRST).astype(BF16)
                for left, right in (
                    (context, mixed),
                    (acts, d_queries),
                    (acts, d_keys),
                    (acts, d_values),
                )
            ],
            1,
        )
        output_weight_gradient, *narrow = jnp.split(scatter(squares), 4, 1)
        pieces = add_pieces(
            vector_pieces(
                place, (d_first, d_queries, d_keys, d_values, *weights, sums), upper, batch * seq
            )
        )
        output = join_blocks(place, output)
        input_gradient = join_blocks(place, back)
    query_weight_gradient, key_weight_gradient, value_weight_gradient = narrow
    early, later = pieces[:, : width // (batch * seq)], pieces[:, LANES : LANES + width // (batch * seq)]
    return (
        output,
        input_gradient,
        later[0:2],
        query_weight_gradient,
        later[2],
        key_weight_gradient,
        value_weight_gradient,
        later[3],
        output_weight_gradient,
        early[0],
        early[1],
        early[2],
        inner_weight_gradient,
        pieces[0, 2 * LANES : 2 * LANES + high // (batch * seq)],
        outer_weight_gradient,
        early[3],
        early[4],
        early[5],
    )


def solution(mesh):
    both = ("batch", "seq")
    in_specs = (
        (P("batch", "seq", None), P("batch", None), P("batch", "seq"), P("batch"))
        + (P(),) * 16
        + (P("batch", "seq", None),)
    )
    matrix, vector = P(both, None), P(both)
    out_specs = (
        P("batch", "seq", None),
        P("batch", "seq", None),
        P(None, both),
        matrix,
        vector,
        matrix,
        matrix,
        vector,
        matrix,
        vector,
        vector,
        vector,
        matrix,
        vector,
        matrix,
        vector,
        vector,
        vector,
    )
    return jax.shard_map(
        per_device, mesh=mesh, in_specs=in_specs, out_specs=out_specs, check_vma=False
    )
```

```python
import functools
import math

import jax
import jax.numpy as jnp
from jax import lax
from jax.experimental import pallas as pl
from jax.experimental.pallas import tpu as pltpu
from jax.sharding import PartitionSpec as P

HEAD_DIM = 64
LANES = 128
EPSILON = 1e-12
BF16 = jnp.bfloat16
F32 = jnp.float32

CONTRACT_LAST = (((1,), (1,)), ((), ()))
CONTRACT_FIRST = (((0,), (0,)), ((), ()))
GROUPS, SHARES, PIECE, SIDE = 4, 4, 96, 768
MICROSECOND = 1150000000
PARTS = 4


def dot(a, b, dims=(((1,), (0,)), ((), ()))):
    return lax.dot_general(a, b, dims, preferred_element_type=F32)


def low(*shape):
    return jax.ShapeDtypeStruct(shape, BF16)


def full(*shape):
    return jax.ShapeDtypeStruct(shape, F32)


def call(kernel, name, scalars, arrays, outs, limit=4, scratch=(), far=(), after=(), cost=4.0, out_far=False):
    count = len(scalars) + len(arrays) + len(far)

    def body(*refs):
        kernel(*refs[:count], *refs[count + len(after) :])

    single = not isinstance(outs, tuple)
    vmem, hbm = pl.BlockSpec(memory_space=pltpu.VMEM), pl.BlockSpec(memory_space=pltpu.HBM)
    specs = () if single else (vmem,) * len(outs)
    if out_far:
        specs = (hbm,) * len(outs) + (vmem,)
        outs = tuple(pltpu.HBM(o.shape, o.dtype) for o in outs) + (full(8, LANES),)
    return pl.pallas_call(
        body,
        in_specs=[pl.BlockSpec(memory_space=pltpu.SMEM)] * len(scalars)
        + [vmem] * len(arrays)
        + [hbm] * len(far)
        + [pl.BlockSpec(memory_space=pl.ANY)] * len(after),
        out_specs=vmem if single else specs,
        out_shape=outs,
        scratch_shapes=list(scratch),
        compiler_params=pltpu.CompilerParams(vmem_limit_bytes=int(limit * (1 << 20))),
        cost_estimate=pl.CostEstimate(flops=int(cost * MICROSECOND), bytes_accessed=1 << 16, transcendentals=0),
        name=name,
    )(*scalars, *arrays, *(pltpu.with_memory_space_constraint(a, pltpu.HBM) for a in far), *after)


def fetch(sources, targets, semaphores, parts=1):
    copies = []
    for source, target in zip(sources, targets):
        rows = source.shape[0] // parts
        for part in range(parts):
            own = pl.ds(part * rows, rows)
            copies.append(
                pltpu.make_async_copy(source.at[own], target.at[own], semaphores.at[len(copies)])
            )
    for copy in copies:
        copy.start()
    return copies


def line(ref):
    return ref[...].astype(F32)[None]


def block_rows_of(place, mask, each):
    return pl.ds(pl.multiple_of((place[0] ^ mask) * each, each), each)


def entry_kernel(count, place, *refs):
    sources, outs, (hidden, flags, embed, semaphores) = refs[:3], refs[3 : 3 + count], refs[3 + count :]
    for copy in fetch(sources, (hidden, flags, embed), semaphores):
        copy.wait()
    rows = hidden.shape[1]
    row = lax.broadcasted_iota(jnp.int32, (rows, rows), 0)
    column = lax.broadcasted_iota(jnp.int32, (rows, rows), 1)
    first, second = embed[0:1].astype(F32), embed[1:2].astype(F32)
    for mask in range(count):
        item = place[0] ^ mask
        flag = flags[pl.ds(item, 1), :].astype(F32)
        upright = jnp.sum(jnp.where(row == column, flag, 0.0), 1, keepdims=True)
        added = jnp.where(upright == 1.0, second, first)
        outs[mask][...] = (hidden[item].astype(F32) + added).astype(BF16)


def entry_blocks(place, *arrays):
    count, rows, width = arrays[0].shape
    return call(
        functools.partial(entry_kernel, count),
        "entry_blocks",
        (place,),
        (),
        (low(rows, width),) * count,
        scratch=[pltpu.VMEM(a.shape, a.dtype) for a in arrays] + [pltpu.SemaphoreType.DMA((3,))],
        far=arrays,
    )


def flagged_kernel(count, place, cotangent, flags, *outs):
    rows = cotangent.shape[1]
    for mask in range(count):
        item = place[0] ^ mask
        outs[mask][pl.ds(0, rows), :] = cotangent[item]
        outs[mask][pl.ds(rows, 16), :] = jnp.zeros((16, cotangent.shape[2]), BF16)
        flag = jnp.broadcast_to(flags[pl.ds(item, 1), :].astype(F32), (16, rows))
        outs[mask][pl.ds(rows, 16), pl.ds(0, rows)] = flag.astype(BF16)


def flagged_blocks(place, cotangent, flags, after):
    count, rows, width = cotangent.shape
    return call(
        functools.partial(flagged_kernel, count),
        "flagged_blocks",
        (place,),
        (cotangent, flags),
        (low(rows + 16, width),) * count,
        after=after,
    )


def join_kernel(count, place, *refs):
    blocks, (out, token, semaphores) = refs[:count], refs[count:]
    token[...] = jnp.zeros(token.shape, F32)
    copies = [
        pltpu.make_async_copy(blocks[mask], out.at[place[0] ^ mask], semaphores.at[mask])
        for mask in range(count)
    ]
    for copy in copies:
        copy.start()
    for copy in copies:
        copy.wait()


def join_blocks(place, blocks, after=()):
    return call(
        functools.partial(join_kernel, len(blocks)),
        "join_blocks",
        (place,),
        blocks,
        (low(len(blocks), *blocks[0].shape),),
        scratch=[pltpu.SemaphoreType.DMA((len(blocks),))],
        after=after,
        cost=0.5,
        out_far=True,
    )


def swap_pairs(array, axis, mask):
    size = lax.axis_size(axis)
    return lax.ppermute(array, axis, [(i, i ^ mask) for i in range(size)])


def pick(array, index, dim):
    return lax.dynamic_index_in_dim(array, index, dim, keepdims=False)


def exchange(blocks):
    order = sorted(range(1, len(blocks)), key=lambda mask: mask < 2)
    got = {mask: swap_pairs(blocks[mask], "seq", mask) for mask in order}
    return [blocks[0]] + [got[mask] for mask in range(1, len(blocks))]


def total(parts):
    result = parts[0].astype(F32)
    for part in parts[1:]:
        result = result + part.astype(F32)
    return result


def halve(parts, dim, axis, bit, dtype=BF16):
    mine = (lax.axis_index(axis) >> bit) & 1
    sent = total([pick(part, 1 - mine, dim) for part in parts]).astype(dtype)
    got = swap_pairs(sent, axis, 1 << bit)
    return [pick(part, mine, dim) for part in parts] + [got]


def scatter(gradient):
    batch, seq = lax.axis_size("batch"), lax.axis_size("seq")
    rows, columns = gradient.shape
    batch_bits, seq_bits = batch.bit_length() - 1, seq.bit_length() - 1
    each = rows // (batch * seq)
    shape = (2,) * (batch_bits + seq_bits) + (each, columns)
    parts = [gradient.astype(BF16).reshape(shape)]
    parts = halve(parts, batch_bits - 1, "batch", 0)
    ways = []
    for way in range(2):
        half = [
            lax.slice_in_dim(part, way * (columns // 2), (way + 1) * (columns // 2), axis=part.ndim - 1)
            for part in parts
        ]
        bits = list(range(1, batch_bits))
        if way:
            bits = bits[::-1]
        left = list(range(batch_bits - 1, 0, -1))
        for bit in bits:
            dim = left.index(bit)
            half = halve(half, dim, "batch", bit)
            left.remove(bit)
        ways.append(half)
    parts = [jnp.concatenate([a, b], -1) for a, b in zip(*ways)]
    for bit in range(seq_bits):
        parts = halve(parts, seq_bits - 1 - bit, "seq", bit)
    return total(parts)


def norm_parts(values):
    centre = values - jnp.mean(values, -1, keepdims=True)
    inverse = lax.rsqrt(jnp.mean(centre * centre, -1, keepdims=True) + EPSILON)
    return centre * inverse, inverse


def norm_back(upper, hat, inverse, gain):
    g = upper * gain
    return inverse * (
        g - jnp.mean(g, -1, keepdims=True) - hat * jnp.mean(g * hat, -1, keepdims=True)
    )


def gate_parts(u):
    share = 0.5 + 0.5 * lax.erf(u * 0.7071067811865476)
    return u * share, share + u * (jnp.exp(-0.5 * u * u) * 0.3989422804014327)


def load_kernel(*refs):
    count = len(refs) // 2
    for copy in fetch(refs[:count], refs[count:-1], refs[-1], PARTS):
        copy.wait()


def load(weights, after):
    return call(
        load_kernel,
        "load",
        (),
        (),
        tuple(low(*weight.shape) for weight in weights),
        scratch=[pltpu.SemaphoreType.DMA((PARTS * len(weights),))],
        far=weights,
        after=after,
    )


def attend_kernel(count, place, lengths, groups, *refs):
    blocks = refs[:count]
    query_weight, query_bias, key_weight, value_weight, value_bias = refs[count : count + 5]
    acts, q_ref, k_ref, v_ref, o_ref, e_ref, inverse_ref, bias = refs[count + 5 :]
    rows, width = acts.shape
    each = rows // count
    for mask in range(count):
        acts[block_rows_of(place, mask, each), :] = blocks[mask][...]
    ids = groups[pl.ds(place[0], 1), :].astype(F32)
    key_place = lax.broadcasted_iota(jnp.int32, (1, rows), 1)
    key_ids = jnp.where(key_place < lengths[place[0]], ids, 1e9)
    upright = jnp.transpose(jnp.broadcast_to(ids, (8, rows)))[:, :1]
    bias[...] = jnp.where(key_ids <= upright, 0.0, -1e30)
    place_of = lax.broadcasted_iota(jnp.int32, (rows, LANES), 1)
    lane = place_of // HEAD_DIM
    inverses = jnp.zeros((rows, LANES), F32)
    tile = 2 * LANES
    for start in range(0, width, tile):
        part = slice(start, start + tile)
        x = acts[...]
        q = (dot(x, query_weight[:, part]) + line(query_bias)[:, part]).astype(BF16)
        k = dot(x, key_weight[:, part]).astype(BF16)
        v = (dot(x, value_weight[:, part]) + line(value_bias)[:, part]).astype(BF16)
        q_ref[:, part] = q
        k_ref[:, part] = k
        v_ref[:, part] = v
        q = q * jnp.asarray(1.0 / math.sqrt(HEAD_DIM), BF16)
        for pair in range(tile // LANES):
            at = slice(pair * LANES, (pair + 1) * LANES)
            q2, k2, v2 = q[:, at], k[:, at], v[:, at]
            sums = []
            for head in range(2):
                mine = lane == head
                s = dot(jnp.where(mine, q2, jnp.zeros_like(q2)), k2, CONTRACT_LAST) + bias[...]
                e = jnp.exp(s - jnp.max(s, -1, keepdims=True)).astype(BF16)
                e_ref[(start + pair * LANES) // HEAD_DIM + head] = e
                sums.append(dot(e, jnp.where(mine, v2, jnp.ones_like(v2))))
            top = jnp.where(lane == 0, sums[0], sums[1])
            under = pltpu.roll(jnp.where(lane == 0, sums[1], sums[0]), HEAD_DIM, 1)
            inverse = 1.0 / under
            first = (start + pair * LANES) // HEAD_DIM
            inverses = jnp.where(place_of == first, inverse, inverses)
            inverses = jnp.where(place_of == first + 1, pltpu.roll(inverse, HEAD_DIM, 1), inverses)
            o_ref[:, start + pair * LANES : start + (pair + 1) * LANES] = (top * inverse).astype(BF16)
    inverse_ref[...] = inverses


def attend(place, lengths, groups, blocks, weights, after):
    each, width = blocks[0].shape
    rows = len(blocks) * each
    wide = low(rows, width)
    return call(
        functools.partial(attend_kernel, len(blocks)),
        "attend",
        (place, lengths),
        (groups, *blocks, *weights),
        (wide, wide, wide, wide, wide, low(width // HEAD_DIM, rows, rows), full(rows, LANES)),
        scratch=[pltpu.VMEM((rows, rows), F32)],
        limit=6,
        after=after,
    )


def attend_back_kernel(e_ref, q_ref, k_ref, v_ref, o_ref, inverse_ref, do_ref, dq_ref, dk_ref, dv_ref):
    rows, width = q_ref.shape
    scale = 1.0 / math.sqrt(HEAD_DIM)
    lane = lax.broadcasted_iota(jnp.int32, (rows, LANES), 1) // HEAD_DIM
    for pair in range(width // LANES):
        at = slice(pair * LANES, (pair + 1) * LANES)
        q, k, v = q_ref[:, at], k_ref[:, at], v_ref[:, at]
        inverse = jnp.where(
            lane == 0, inverse_ref[:, 2 * pair : 2 * pair + 1], inverse_ref[:, 2 * pair + 1 : 2 * pair + 2]
        )
        do = do_ref[:, at].astype(F32) * inverse
        weighed = do * o_ref[:, at].astype(F32)
        do = do.astype(BF16)
        q_up, do_up = jnp.transpose(q), jnp.transpose(do)
        dq, dk, dv = [], [], []
        for head in range(2):
            mine = lane == head
            part = slice(head * HEAD_DIM, (head + 1) * HEAD_DIM)
            row_dot = jnp.sum(jnp.where(mine, weighed, 0.0), -1, keepdims=True)
            d = dot(jnp.where(mine, do, jnp.zeros_like(do)), v, CONTRACT_LAST) - row_dot
            e = e_ref[2 * pair + head]
            ds = (e.astype(F32) * d).astype(BF16)
            dq.append(dot(ds, k))
            dk.append(dot(q_up[part], ds))
            dv.append(dot(do_up[part], e))
        dq_ref[:, at] = (jnp.where(lane == 0, dq[0], dq[1]) * scale).astype(BF16)
        dk_ref[:, at] = (jnp.transpose(jnp.concatenate(dk, 0)) * scale).astype(BF16)
        dv_ref[:, at] = jnp.transpose(jnp.concatenate(dv, 0)).astype(BF16)


def attend_back(arrays, after):
    wide = low(*arrays[1].shape)
    return call(
        attend_back_kernel,
        "attend_back",
        (),
        arrays,
        (wide, wide, wide),
        limit=5.5,
        after=after,
        cost=30.0,
    )


def feed_kernel(count, place, *refs):
    (acts, context, output_weight, output_bias, first_gain, first_shift, inner_weight, inner_bias) = refs[:8]
    outer_weight, outer_bias, second_gain, second_shift = refs[8:12]
    settled_low, hat_ref, inverse_ref, active_ref, slope_ref, hat_two, inverse_two = refs[12:19]
    outs = refs[19 : 19 + count]
    acc = refs[19 + count]
    rows, high = active_ref.shape
    hat, inverse = norm_parts(
        acts[...].astype(F32) + dot(context[...], output_weight[...]) + line(output_bias)
    )
    hat_ref[...] = hat.astype(BF16)
    inverse_ref[...] = jnp.broadcast_to(inverse, inverse_ref.shape)
    settled = hat * line(first_gain) + line(first_shift)
    settled_low[...] = settled.astype(BF16)
    acc[...] = settled + line(outer_bias)
    tile = 4 * LANES
    for start in range(0, high, tile):
        part = slice(start, start + tile)
        inner = dot(settled_low[...], inner_weight[:, part]) + line(inner_bias)[:, part]
        active, slope = gate_parts(inner)
        active_ref[:, part] = active.astype(BF16)
        slope_ref[:, part] = slope.astype(BF16)
    acc[...] += dot(active_ref[...], outer_weight[...])
    each = rows // count
    gain, shift = line(second_gain), line(second_shift)
    for mask in range(count):
        own = block_rows_of(place, mask, each)
        hat, inverse = norm_parts(acc[own, :])
        outs[mask][...] = (hat * gain + shift).astype(BF16)
        hat_two[own, :] = hat
        inverse_two[own, :] = jnp.broadcast_to(inverse, (each, LANES))


def feed(place, acts, context, weights, count):
    rows, width = acts.shape
    high = weights[4].shape[1]
    wide = low(rows, width)
    return call(
        functools.partial(feed_kernel, count),
        "feed",
        (place,),
        (acts, context, *weights),
        (
            wide,
            wide,
            full(rows, LANES),
            low(rows, high),
            low(rows, high),
            full(rows, width),
            full(rows, LANES),
        )
        + (low(rows // count, width),) * count,
        limit=7.5,
        scratch=[pltpu.VMEM((rows, width), F32)],
    )


def turn_kernel(count, place, hat_two, inverse_two, second_gain, *refs):
    cotangents = refs[:count]
    d_second, branch, sums = refs[count:]
    each = hat_two.shape[0] // count
    gain = line(second_gain)
    totals = [0.0, 0.0, 0.0]
    for mask in range(count):
        own = block_rows_of(place, mask, each)
        hat = hat_two[own, :]
        upper = cotangents[mask][pl.ds(0, each), :].astype(F32)
        d = norm_back(upper, hat, inverse_two[own, :1], gain)
        d_low = d.astype(BF16)
        d_second[own, :] = d
        branch[own, :] = d_low
        for i, term in enumerate((d_low.astype(F32), upper * hat, upper)):
            totals[i] = totals[i] + jnp.sum(term, 0, keepdims=True)
    for i in range(3):
        sums[i : i + 1, :] = totals[i]


def turn(place, hat_two, inverse_two, second_gain, cotangents):
    rows, width = hat_two.shape
    return call(
        functools.partial(turn_kernel, len(cotangents)),
        "turn",
        (place,),
        (hat_two, inverse_two, second_gain, *cotangents),
        (full(rows, width), low(rows, width), full(8, width)),
    )


def feed_back_kernel(
    branch,
    outer_weight,
    slope,
    inner_weight,
    d_second,
    hat_ref,
    inverse_ref,
    first_gain,
    output_weight,
    turn_sums,
    d_inner_ref,
    d_first_ref,
    mixed,
    d_context,
    sums,
    acc,
):
    rows, high = slope.shape
    width = acc.shape[1]
    tile = 4 * LANES
    for start in range(0, high, tile):
        part = slice(start, start + tile)
        d_active = dot(branch[...], outer_weight[part, :], CONTRACT_LAST)
        d_inner = (d_active * slope[:, part].astype(F32)).astype(BF16)
        d_inner_ref[:, part] = d_inner
        partial = jnp.sum(d_inner.astype(F32), 0, keepdims=True)
        for lane in range(start, start + tile, LANES):
            row = 6 + lane // width
            sums[row : row + 1, lane % width : lane % width + LANES] = partial[:, lane - start : lane - start + LANES]
    acc[...] = d_second[...] + dot(d_inner_ref[...], inner_weight[...], CONTRACT_LAST)
    parts = 4
    totals = [0.0, 0.0, 0.0]
    gain = line(first_gain)
    for part in range(parts):
        own = slice(part * (rows // parts), (part + 1) * (rows // parts))
        upper = acc[own, :]
        hat = hat_ref[own, :].astype(F32)
        d = norm_back(upper, hat, inverse_ref[own, :1], gain)
        d_low = d.astype(BF16)
        d_first_ref[own, :] = d
        mixed[own, :] = d_low
        for i, term in enumerate((d_low.astype(F32), upper * hat, upper)):
            totals[i] = totals[i] + jnp.sum(term, 0, keepdims=True)
    for i in range(3):
        sums[i : i + 1, :] = totals[i]
    sums[3:6, :] = turn_sums[0:3, :]
    d_context[...] = dot(mixed[...], output_weight[...], CONTRACT_LAST).astype(BF16)


def feed_back(arrays, after):
    rows, width = arrays[0].shape
    high = arrays[2].shape[1]
    wide = low(rows, width)
    return call(
        feed_back_kernel,
        "feed_back",
        (),
        arrays,
        (low(rows, high), full(rows, width), wide, wide, full(16, width)),
        scratch=[pltpu.VMEM((rows, width), F32)],
        after=after,
        cost=30.0,
        limit=5,
    )


def entry_back_kernel(count, place, d_first, dq, dk, dv, wq, wk, wv, *refs):
    outs, acc = refs[:count], refs[count]
    each = dq.shape[0] // count
    acc[...] = (
        d_first[...]
        + dot(dq[...], wq[...], CONTRACT_LAST)
        + dot(dk[...], wk[...], CONTRACT_LAST)
        + dot(dv[...], wv[...], CONTRACT_LAST)
    )
    for mask in range(count):
        outs[mask][...] = acc[block_rows_of(place, mask, each), :].astype(BF16)


def entry_back(place, arrays, count, after):
    rows, width = arrays[1].shape
    return call(
        functools.partial(entry_back_kernel, count),
        "entry_back",
        (place,),
        arrays,
        (low(rows // count, width),) * count,
        scratch=[pltpu.VMEM((rows, width), F32)],
        after=after,
        limit=4,
    )


def add_vectors(place, d_first, dq, dk, dv, weights, early_sums, flagged, sums):
    count = len(flagged)
    each, width = dq.shape[0] // count, dq.shape[1]
    row = lax.broadcasted_iota(jnp.int32, (each, each), 0)
    column = lax.broadcasted_iota(jnp.int32, (each, each), 1)
    zero, one = [0.0] * 4, [0.0] * 4
    for mask in range(count):
        own = block_rows_of(place, mask, each)
        flag = flagged[mask][pl.ds(each, 16), pl.ds(0, each)][:1].astype(F32)
        upright = jnp.sum(jnp.where(row == column, flag, 0.0), 1, keepdims=True)
        for i, array in enumerate((d_first, dq, dk, dv)):
            value = array[own, :].astype(F32)
            zero[i] = zero[i] + jnp.sum(value * (1.0 - upright), 0, keepdims=True)
            one[i] = one[i] + jnp.sum(value * upright, 0, keepdims=True)
    by_flag = jnp.concatenate([zero[0], one[0]] + [jnp.zeros((6, width), F32)], 0)
    for i, weight in enumerate(weights):
        pair = jnp.concatenate([zero[i + 1], one[i + 1]] + [jnp.zeros((6, width), F32)], 0)
        by_flag = by_flag + dot(pair.astype(BF16), weight[...], CONTRACT_LAST)
    second = jnp.concatenate([by_flag[:2], zero[1] + one[1], zero[3] + one[3]], 0)
    first = early_sums[0:6, :]
    pieces = sums.shape[0]
    piece = width // pieces
    sums[...] = jnp.zeros(sums.shape, F32)
    for i in range(pieces):
        part = slice(i * piece, (i + 1) * piece)
        at, lane = divmod(i * 4 * piece, width)
        sums[i, 0:6, 0:piece] = first[:, part]
        sums[i, 0:4, LANES : LANES + piece] = second[:, part]
        sums[i, 0:1, 2 * LANES : 2 * LANES + 4 * piece] = early_sums[6 + at : 7 + at, lane : lane + 4 * piece]


def vector_pieces_kernel(place, d_first, dq, dk, dv, wq, wk, wv, early_sums, *refs):
    add_vectors(place, d_first, dq, dk, dv, (wq, wk, wv), early_sums, refs[:-1], refs[-1])


def vector_pieces(place, arrays, flagged, pieces):
    return call(
        vector_pieces_kernel,
        "vector_pieces",
        (place,),
        (*arrays, *flagged),
        full(pieces, 8, SIDE // 2),
    )


def parts_of(place):
    x, y = place[2], place[3]
    far, beside, behind, own = 2 * (1 - y) + 1 - x, 2 * y + 1 - x, 2 * (1 - y) + x, 2 * y + x
    return ((far, 0), (beside, 0), (far, 1), (behind, 1), (behind, 0), (beside, 1), (own, 0), (own, 1))


def tall_gradient_kernel(keep, place, left, right, out):
    rows = left.shape[1] // GROUPS // 2
    core = place[1] if keep else 1 - place[1]
    parts = parts_of(place)
    half = SIDE // 2
    for group, homes in ((0, (0, 2)), (1, (1, 5)), (3, (4, 3)), (6, (6, 7))):
        columns = pl.ds(pl.multiple_of((2 * parts[group][0] + core) * rows, LANES), rows)
        product = dot(left[:, columns], right[...], CONTRACT_FIRST).reshape(SHARES, PIECE, SIDE)
        for side, home in enumerate(homes):
            out[home] = product[:, :, side * half : (side + 1) * half].astype(BF16)


def tall_gradient(place, left, right, keep, after=(), cost=2.0):
    return call(
        functools.partial(tall_gradient_kernel, keep),
        "tall_gradient",
        (place,),
        (left, right),
        low(8, SHARES, PIECE, SIDE // 2),
        after=after,
        cost=cost,
    )


def stack_pieces(place, totals, send, keep, start, last=None):
    each = SIDE // (GROUPS * SHARES * 2)
    half = SIDE // 2
    for out, core in ((send, 1 - place[1]), (keep, place[1])):
        for home, (group, side) in enumerate(parts_of(place)):
            columns = slice(side * half, (side + 1) * half)
            for share in range(SHARES):
                index = (2 * group + core) * SHARES + share
                row = pl.multiple_of(index * each, 8)
                pieces = [t[pl.ds(row, each), columns] for t in totals]
                if last is not None:
                    pieces.append(last[index] if side == 0 else jnp.zeros(last.shape[1:], F32))
                piece = jnp.concatenate(pieces, 0)
                out[home, share, start : start + piece.shape[0], :] = piece.astype(BF16)


def wide_gradient_kernel(place, left, right, context, mixed, send, keep, first, second):
    for half in range(2):
        start = 2 * half * SIDE
        first[...] = dot(left[...], right[:, start : start + SIDE], CONTRACT_FIRST)
        second[...] = dot(left[...], right[:, start + SIDE : start + 2 * SIDE], CONTRACT_FIRST)
        stack_pieces(place, (first, second), send, keep, half * PIECE // 2)
    first[...] = dot(context[...], mixed[...], CONTRACT_FIRST)
    stack_pieces(place, (first,), send, keep, PIECE)


def wide_gradient(place, arrays, cost=1.0):
    eight = low(8, SHARES, PIECE + PIECE // 4, SIDE // 2)
    return call(
        wide_gradient_kernel,
        "wide_gradient",
        (place,),
        arrays,
        (eight, eight),
        scratch=[pltpu.VMEM((SIDE, SIDE), F32)] * 2,
        cost=cost,
        limit=6.5,
    )


def square_gradients_kernel(place, acts, d_first, dq, dk, dv, wq, wk, wv, early_sums, *refs):
    flagged, (send, keep, first, second, sums) = refs[:-5], refs[-5:]
    first[...] = dot(acts[...], dq[...], CONTRACT_FIRST)
    second[...] = dot(acts[...], dk[...], CONTRACT_FIRST)
    add_vectors(place, d_first, dq, dk, dv, (wq, wk, wv), early_sums, flagged, sums)
    stack_pieces(place, (first, second), send, keep, 0)
    first[...] = dot(acts[...], dv[...], CONTRACT_FIRST)
    stack_pieces(place, (first,), send, keep, PIECE // 2, sums)


def square_gradients(place, arrays, flagged, pieces, after, cost=0.1):
    eight = low(8, SHARES, 3 * PIECE // 4 + 8, SIDE // 2)
    return call(
        square_gradients_kernel,
        "square_gradients",
        (place,),
        (*arrays, *flagged),
        (eight, eight),
        scratch=[pltpu.VMEM((SIDE, SIDE), F32)] * 2 + [pltpu.VMEM((pieces, 8, SIDE // 2), F32)],
        after=after,
        cost=cost,
        limit=8,
    )


def first_sums_kernel(keep, got, to_x, to_y):
    to_x[...] = total([keep[0:2], got[0:2]]).astype(BF16)
    to_y[...] = total([keep[2:4], got[2:4]]).astype(BF16)


def second_sums_kernel(start, keep, got, from_x, from_y, to_y, to_x):
    to_y[...] = total([keep[start], got[start], from_x[0]]).astype(BF16)
    to_x[...] = total([keep[start + 1], got[start + 1], from_y[0]]).astype(BF16)


def third_sums_kernel(start, place, keep, got, from_x, from_y, then_y, then_x, send, kept):
    half = SIDE // 2
    bit = place[0] & 1
    for out, share_bit in ((send, 1 - bit), (kept, bit)):
        for high in range(SHARES // 2):
            share = 2 * high + share_bit
            a = total([keep[start + 2, share], got[start + 2, share], from_x[1, share], then_y[share]])
            b = total([keep[start + 3, share], got[start + 3, share], from_y[1, share], then_x[share]])
            out[high, :, :half] = a.astype(out.dtype)
            out[high, :, half:] = b.astype(out.dtype)


def fourth_sums_kernel(place, kept, got, send):
    other = 1 - (place[0] >> 1)
    send[...] = total([kept[other], got[other]]).astype(BF16)


def last_sums_kernel(form, place, kept, got, last, *refs):
    count = (len(refs) - 2) // 2
    outs, token, staged, semaphores = refs[:count], refs[count], refs[count + 1 : -1], refs[-1]
    token[...] = jnp.zeros(token.shape, F32)
    mine = place[0] >> 1
    result = total([kept[mine], got[mine], last[...]])
    each = PIECE // 4
    rows = [result[i * each : (i + 1) * each] for i in range(result.shape[0] // each)]
    if form == "tall":
        staged[0][...] = result
    elif form == "wide":
        for i in range(4):
            staged[0][:, i * SIDE : (i + 1) * SIDE] = rows[i]
        staged[1][...] = rows[4]
    else:
        for i in range(3):
            staged[i][...] = rows[i]
        vectors = result[3 * each :]
        staged[3][...] = vectors[0:2, LANES : LANES + each]
        staged[4][...] = vectors[0, 2 * LANES : 2 * LANES + 4 * each]
        for i in range(8):
            row, lane = (i, 0) if i < 6 else (i - 4, LANES)
            staged[5 + i][...] = vectors[row, lane : lane + each]
    for copy in fetch(staged, outs, semaphores):
        copy.wait()


class Halving:
    def __init__(self, place, send, keep):
        self.place, self.keep = place, keep
        self.got = [swap_pairs(part, "batch", 1) for part in send]
        self.late = 0 if len(keep) > 1 else 4

    def step(self, kernel, name, scalars, arrays, outs, after, cost=0.5):
        results = call(kernel, name, scalars, arrays, outs, after=after, cost=cost)
        self.done = results[:1]
        return results

    def first(self, after=(), cost=0.5):
        half = low(2, *self.keep[0].shape[1:])
        arrays = (self.keep[0], self.got[0])
        to = self.step(first_sums_kernel, "first_sums", (), arrays, (half, half), after, cost)
        self.from_x, self.from_y = swap_pairs(to[0], "batch", 2), swap_pairs(to[1], "batch", 4)

    def second(self, after=(), cost=0.5):
        quarter = low(*self.keep[0].shape[1:])
        arrays = (self.keep[-1], self.got[-1], self.from_x, self.from_y)
        kernel = functools.partial(second_sums_kernel, self.late)
        to = self.step(kernel, "second_sums", (), arrays, (quarter, quarter), after, cost)
        self.then_y, self.then_x = swap_pairs(to[0], "batch", 4), swap_pairs(to[1], "batch", 2)

    def third(self, after=(), cost=0.5):
        shape = (SHARES // 2, self.keep[0].shape[2], SIDE)
        arrays = (self.keep[-1], self.got[-1], self.from_x, self.from_y, self.then_y, self.then_x)
        outs = (low(*shape), full(*shape))
        kernel = functools.partial(third_sums_kernel, self.late)
        to, self.kept = self.step(kernel, "third_sums", (self.place,), arrays, outs, after, cost)
        self.pair = swap_pairs(to, "seq", 1)

    def fourth(self, after=(), cost=0.5):
        arrays = (self.kept, self.pair)
        outs = (low(*self.kept.shape[1:]),)
        (to,) = self.step(fourth_sums_kernel, "fourth_sums", (self.place,), arrays, outs, after, cost)
        self.others = swap_pairs(to, "seq", 2)

    def last(self, form, after=()):
        each = PIECE // 4
        shapes = {
            "tall": [(PIECE, SIDE)],
            "wide": [(each, 4 * SIDE), (each, SIDE)],
            "square": [(each, SIDE)] * 3 + [(2, each), (4 * each,)] + [(each,)] * 8,
        }[form]
        *self.result, token = call(
            functools.partial(last_sums_kernel, form),
            "last_sums",
            (self.place,),
            (self.kept, self.pair, self.others),
            tuple(full(*shape) for shape in shapes),
            scratch=[pltpu.VMEM(shape, F32) for shape in shapes] + [pltpu.SemaphoreType.DMA((len(shapes),))],
            after=after,
            cost=0.5,
            out_far=True,
        )
        self.done = (token,)


def add_pieces(pieces):
    batch, seq = lax.axis_size("batch"), lax.axis_size("seq")
    parts = [pieces.reshape((2,) * ((batch * seq).bit_length() - 1) + pieces.shape[1:])]
    for axis in ("batch", "seq"):
        bits = lax.axis_size(axis).bit_length() - 1
        for bit in range(bits):
            parts = [total(halve(parts, bits - 1 - bit, axis, bit, F32))]
    return parts[0]


def per_device(
    hidden,
    groups,
    answer_flags,
    lengths,
    answer_embed,
    query_weight,
    query_bias,
    key_weight,
    value_weight,
    value_bias,
    output_weight,
    output_bias,
    first_gain,
    first_shift,
    inner_weight,
    inner_bias,
    outer_weight,
    outer_bias,
    second_gain,
    second_shift,
    cotangent,
):
    items, block_rows, width = hidden.shape
    batch, seq = lax.axis_size("batch"), lax.axis_size("seq")
    me, group = lax.axis_index("seq"), lax.axis_index("batch")
    place = jnp.stack([me, group & 1, (group >> 1) & 1, (group >> 2) & 1]).astype(jnp.int32)
    high = inner_weight.shape[1]
    even = (batch, seq, width, high) == (8, SHARES, SIDE, 4 * SIDE)

    blocks = entry_blocks(place, hidden, answer_flags, answer_embed)
    got = exchange(blocks)
    output_near, inner_near, outer_near = load((output_weight, inner_weight, outer_weight), blocks[:1])
    upper = exchange(flagged_blocks(place, cotangent, answer_flags, (*got[2:], output_near)))
    acts, queries, keys, values, context, exponents, inverse_sums = attend(
        place,
        lengths,
        groups,
        got,
        (query_weight, query_bias, key_weight, value_weight, value_bias),
        (),
    )
    settled, hat, inverse, active, slope, hat_two, inverse_two, *output = feed(
        place,
        acts,
        context,
        (
            output_near,
            output_bias,
            first_gain,
            first_shift,
            inner_near,
            inner_bias,
            outer_near,
            outer_bias,
            second_gain,
            second_shift,
        ),
        items,
    )
    d_second, branch, sums = turn(place, hat_two, inverse_two, second_gain, upper)
    if even:
        send = tall_gradient(place, active, branch, False)
        keep = tall_gradient(place, active, branch, True, (send,))
        outer = Halving(place, (send,), (keep,))
        outer.first()
        after = outer.done
    else:
        outer_weight_gradient = scatter(dot(active, branch, CONTRACT_FIRST))
        after = ()
    output = exchange(output)
    d_inner, d_first, mixed, d_context, sums = feed_back(
        (
            branch,
            outer_near,
            slope,
            inner_near,
            d_second,
            hat,
            inverse,
            first_gain,
            output_near,
            sums,
        ),
        after,
    )
    if even:
        send, keep = wide_gradient(place, (settled, d_inner, context, mixed))
        inner = Halving(place, (send,), (keep,))
        outer.second((send,))
        after = (*outer.done, *output[1:])
    else:
        inner_weight_gradient = scatter(dot(settled, d_inner, CONTRACT_FIRST))
    weights = (query_weight, key_weight, value_weight)
    d_queries, d_keys, d_values = attend_back(
        (exponents, queries, keys, values, context, inverse_sums, d_context),
        after,
    )
    if even:
        inner.first((d_queries,))
        outer.third(inner.done)
        after = outer.done
    input_gradient = entry_back(
        place, (d_first, d_queries, d_keys, d_values, *weights), items, after
    )
    back = exchange(input_gradient)
    if even:
        send, keep = square_gradients(
            place,
            (acts, d_first, d_queries, d_keys, d_values, *weights, sums),
            upper,
            batch * seq,
            input_gradient[:1],
        )
        narrow = Halving(place, (send,), (keep,))
        output, token = join_blocks(place, output, (send,))
        outer.fourth((token, back[2]))
        inner.second(outer.done, cost=25.0)
        narrow.first(inner.done)
        inner.third((*narrow.done, back[3]))
        narrow.second(inner.done)
        inner.fourth((*narrow.done, outer.others))
        outer.last("tall", inner.done)
        narrow.third((*outer.done, back[1]))
        input_gradient, token = join_blocks(place, back, narrow.done)
        narrow.fourth((token,))
        inner.last("wide", narrow.done)
        narrow.last("square")
        (outer_weight_gradient,), (inner_weight_gradient, output_weight_gradient) = outer.result, inner.result
        vectors = narrow.result[5:]
        *narrow, embed_gradient, inner_bias_gradient = narrow.result[:5]
    else:
        squares = jnp.concatenate(
            [
                dot(left, right, CONTRACT_FIRST).astype(BF16)
                for left, right in (
                    (context, mixed),
                    (acts, d_queries),
                    (acts, d_keys),
                    (acts, d_values),
                )
            ],
            1,
        )
        output_weight_gradient, *narrow = jnp.split(scatter(squares), 4, 1)
        pieces = add_pieces(
            vector_pieces(
                place, (d_first, d_queries, d_keys, d_values, *weights, sums), upper, batch * seq
            )
        )
        early, later = pieces[:, : width // (batch * seq)], pieces[:, LANES : LANES + width // (batch * seq)]
        embed_gradient, inner_bias_gradient = later[0:2], pieces[0, 2 * LANES : 2 * LANES + high // (batch * seq)]
        vectors = [early[i] for i in range(6)] + [later[2], later[3]]
        output, _ = join_blocks(place, output)
        input_gradient, _ = join_blocks(place, back)
    query_weight_gradient, key_weight_gradient, value_weight_gradient = narrow
    return (
        output,
        input_gradient,
        embed_gradient,
        query_weight_gradient,
        vectors[6],
        key_weight_gradient,
        value_weight_gradient,
        vectors[7],
        output_weight_gradient,
        vectors[0],
        vectors[1],
        vectors[2],
        inner_weight_gradient,
        inner_bias_gradient,
        outer_weight_gradient,
        vectors[3],
        vectors[4],
        vectors[5],
    )


def solution(mesh):
    both = ("batch", "seq")
    in_specs = (
        (P("batch", "seq", None), P("batch", None), P("batch", "seq"), P("batch"))
        + (P(),) * 16
        + (P("batch", "seq", None),)
    )
    matrix, vector = P(both, None), P(both)
    out_specs = (
        P("batch", "seq", None),
        P("batch", "seq", None),
        P(None, both),
        matrix,
        vector,
        matrix,
        matrix,
        vector,
        matrix,
        vector,
        vector,
        vector,
        matrix,
        vector,
        matrix,
        vector,
        vector,
        vector,
    )
    return jax.shard_map(
        per_device, mesh=mesh, in_specs=in_specs, out_specs=out_specs, check_vma=False
    )
```

```python
import functools
import math

import jax
import jax.numpy as jnp
from jax import lax
from jax.experimental import pallas as pl
from jax.experimental.pallas import tpu as pltpu
from jax.sharding import PartitionSpec as P

HEAD_DIM = 64
LANES = 128
EPSILON = 1e-12
BF16 = jnp.bfloat16
F32 = jnp.float32

CONTRACT_LAST = (((1,), (1,)), ((), ()))
CONTRACT_FIRST = (((0,), (0,)), ((), ()))
GROUPS, SHARES, PIECE, SIDE = 4, 4, 96, 768
MICROSECOND = 1150000000
PARTS = 4


def dot(a, b, dims=(((1,), (0,)), ((), ()))):
    return lax.dot_general(a, b, dims, preferred_element_type=F32)


def low(*shape):
    return jax.ShapeDtypeStruct(shape, BF16)


def full(*shape):
    return jax.ShapeDtypeStruct(shape, F32)


def call(kernel, name, scalars, arrays, outs, limit=4, scratch=(), far=(), after=(), cost=4.0, out_far=False):
    count = len(scalars) + len(arrays) + len(far)

    def body(*refs):
        kernel(*refs[:count], *refs[count + len(after) :])

    single = not isinstance(outs, tuple)
    vmem, hbm = pl.BlockSpec(memory_space=pltpu.VMEM), pl.BlockSpec(memory_space=pltpu.HBM)
    specs = () if single else (vmem,) * len(outs)
    if out_far:
        specs = (hbm,) * len(outs) + (vmem,)
        outs = tuple(pltpu.HBM(o.shape, o.dtype) for o in outs) + (full(8, LANES),)
    return pl.pallas_call(
        body,
        in_specs=[pl.BlockSpec(memory_space=pltpu.SMEM)] * len(scalars)
        + [vmem] * len(arrays)
        + [hbm] * len(far)
        + [pl.BlockSpec(memory_space=pl.ANY)] * len(after),
        out_specs=vmem if single else specs,
        out_shape=outs,
        scratch_shapes=list(scratch),
        compiler_params=pltpu.CompilerParams(vmem_limit_bytes=int(limit * (1 << 20))),
        cost_estimate=pl.CostEstimate(flops=int(cost * MICROSECOND), bytes_accessed=1 << 16, transcendentals=0),
        name=name,
    )(*scalars, *arrays, *(pltpu.with_memory_space_constraint(a, pltpu.HBM) for a in far), *after)


def fetch(sources, targets, semaphores, parts=1):
    copies = []
    for source, target in zip(sources, targets):
        rows = source.shape[0] // parts
        for part in range(parts):
            own = pl.ds(part * rows, rows)
            copies.append(
                pltpu.make_async_copy(source.at[own], target.at[own], semaphores.at[len(copies)])
            )
    for copy in copies:
        copy.start()
    return copies


def line(ref):
    return ref[...].astype(F32)[None]


def order(count):
    return sorted(range(count), key=lambda mask: (mask != 0, mask < 2, mask))


def block_rows_of(place, mask, each):
    return pl.ds(pl.multiple_of((place[0] ^ mask) * each, each), each)


def entry_kernel(masks, place, hidden, flags, embed, *refs):
    count = len(masks)
    outs, (near, near_flags, near_embed, semaphores) = refs[:count], refs[count:]
    items = [place[0] ^ mask for mask in masks]
    sources = [hidden.at[item] for item in items] + [flags, embed]
    targets = [near.at[i] for i in range(count)] + [near_flags, near_embed]
    for copy in fetch(sources, targets, semaphores):
        copy.wait()
    rows = hidden.shape[1]
    row = lax.broadcasted_iota(jnp.int32, (rows, rows), 0)
    column = lax.broadcasted_iota(jnp.int32, (rows, rows), 1)
    first, second = near_embed[0:1].astype(F32), near_embed[1:2].astype(F32)
    for i, item in enumerate(items):
        flag = near_flags[pl.ds(item, 1), :].astype(F32)
        upright = jnp.sum(jnp.where(row == column, flag, 0.0), 1, keepdims=True)
        added = jnp.where(upright == 1.0, second, first)
        outs[i][...] = (near[i].astype(F32) + added).astype(BF16)


def entry_blocks(place, masks, arrays, after=()):
    hidden, flags, embed = arrays
    rows, width = hidden.shape[1:]
    count = len(masks)
    return call(
        functools.partial(entry_kernel, masks),
        "entry_blocks",
        (place,),
        (),
        (low(rows, width),) * count,
        scratch=[
            pltpu.VMEM((count, rows, width), BF16),
            pltpu.VMEM(flags.shape, flags.dtype),
            pltpu.VMEM(embed.shape, embed.dtype),
            pltpu.SemaphoreType.DMA((count + 2,)),
        ],
        far=arrays,
        after=after,
        cost=0.5,
    )


def flagged_kernel(count, place, cotangent, flags, *outs):
    rows = cotangent.shape[1]
    for i, mask in enumerate(order(count)):
        item = place[0] ^ mask
        outs[i][pl.ds(0, rows), :] = cotangent[item]
        outs[i][pl.ds(rows, 16), :] = jnp.zeros((16, cotangent.shape[2]), BF16)
        flag = jnp.broadcast_to(flags[pl.ds(item, 1), :].astype(F32), (16, rows))
        outs[i][pl.ds(rows, 16), pl.ds(0, rows)] = flag.astype(BF16)


def flagged_blocks(place, cotangent, flags, after):
    count, rows, width = cotangent.shape
    return call(
        functools.partial(flagged_kernel, count),
        "flagged_blocks",
        (place,),
        (cotangent, flags),
        (low(rows + 16, width),) * count,
        after=after,
    )


def join_kernel(count, place, *refs):
    blocks, (out, token, semaphores) = refs[:count], refs[count:]
    token[...] = jnp.zeros(token.shape, F32)
    copies = [
        pltpu.make_async_copy(blocks[i], out.at[place[0] ^ mask], semaphores.at[i])
        for i, mask in enumerate(order(count))
    ]
    for copy in copies:
        copy.start()
    for copy in copies:
        copy.wait()


def join_blocks(place, blocks, after=()):
    return call(
        functools.partial(join_kernel, len(blocks)),
        "join_blocks",
        (place,),
        blocks,
        (low(len(blocks), *blocks[0].shape),),
        scratch=[pltpu.SemaphoreType.DMA((len(blocks),))],
        after=after,
        cost=0.5,
        out_far=True,
    )


def relay_kernel(near, got, out):
    out[0] = near[...]
    out[1] = got[1]


def relay(near, got, after):
    return call(relay_kernel, "relay", (), (near, got), low(2, *near.shape), after=after, cost=0.5)


def join_pairs_kernel(place, own, got, near_got, out, token, semaphores):
    token[...] = jnp.zeros(token.shape, F32)
    me = place[0]
    sources = (own, got.at[0], near_got.at[0], near_got.at[1])
    for copy in fetch(sources, [out.at[me ^ mask] for mask in (0, 2, 1, 3)], semaphores):
        copy.wait()


def join_pairs(place, own, got, near_got, after):
    return call(
        join_pairs_kernel,
        "join_pairs",
        (place,),
        (own, got, near_got),
        (low(4, *own.shape),),
        scratch=[pltpu.SemaphoreType.DMA((4,))],
        after=after,
        cost=0.5,
        out_far=True,
    )


def swap_pairs(array, axis, mask):
    size = lax.axis_size(axis)
    return lax.ppermute(array, axis, [(i, i ^ mask) for i in range(size)])


def pick(array, index, dim):
    return lax.dynamic_index_in_dim(array, index, dim, keepdims=False)


def exchange(blocks):
    pairs = list(zip(order(len(blocks)), blocks))
    return [block if mask == 0 else swap_pairs(block, "seq", mask) for mask, block in pairs]


def total(parts):
    result = parts[0].astype(F32)
    for part in parts[1:]:
        result = result + part.astype(F32)
    return result


def halve(parts, dim, axis, bit, dtype=BF16):
    mine = (lax.axis_index(axis) >> bit) & 1
    sent = total([pick(part, 1 - mine, dim) for part in parts]).astype(dtype)
    got = swap_pairs(sent, axis, 1 << bit)
    return [pick(part, mine, dim) for part in parts] + [got]


def scatter(gradient):
    batch, seq = lax.axis_size("batch"), lax.axis_size("seq")
    rows, columns = gradient.shape
    batch_bits, seq_bits = batch.bit_length() - 1, seq.bit_length() - 1
    each = rows // (batch * seq)
    shape = (2,) * (batch_bits + seq_bits) + (each, columns)
    parts = [gradient.astype(BF16).reshape(shape)]
    parts = halve(parts, batch_bits - 1, "batch", 0)
    ways = []
    for way in range(2):
        half = [
            lax.slice_in_dim(part, way * (columns // 2), (way + 1) * (columns // 2), axis=part.ndim - 1)
            for part in parts
        ]
        bits = list(range(1, batch_bits))
        if way:
            bits = bits[::-1]
        left = list(range(batch_bits - 1, 0, -1))
        for bit in bits:
            dim = left.index(bit)
            half = halve(half, dim, "batch", bit)
            left.remove(bit)
        ways.append(half)
    parts = [jnp.concatenate([a, b], -1) for a, b in zip(*ways)]
    for bit in range(seq_bits):
        parts = halve(parts, seq_bits - 1 - bit, "seq", bit)
    return total(parts)


def norm_parts(values):
    centre = values - jnp.mean(values, -1, keepdims=True)
    inverse = lax.rsqrt(jnp.mean(centre * centre, -1, keepdims=True) + EPSILON)
    return centre * inverse, inverse


def norm_back(upper, hat, inverse, gain):
    g = upper * gain
    return inverse * (
        g - jnp.mean(g, -1, keepdims=True) - hat * jnp.mean(g * hat, -1, keepdims=True)
    )


def gate_parts(u):
    share = 0.5 + 0.5 * lax.erf(u * 0.7071067811865476)
    return u * share, share + u * (jnp.exp(-0.5 * u * u) * 0.3989422804014327)


def load_kernel(*refs):
    count = len(refs) // 2
    for copy in fetch(refs[:count], refs[count:-1], refs[-1], PARTS):
        copy.wait()


def load(weights, after):
    return call(
        load_kernel,
        "load",
        (),
        (),
        tuple(low(*weight.shape) for weight in weights),
        scratch=[pltpu.SemaphoreType.DMA((PARTS * len(weights),))],
        far=weights,
        after=after,
    )


def attend_kernel(count, place, lengths, groups, *refs):
    blocks = refs[:count]
    query_weight, query_bias, key_weight, value_weight, value_bias = refs[count : count + 5]
    acts, q_ref, k_ref, v_ref, o_ref, e_ref, inverse_ref, bias = refs[count + 5 :]
    rows, width = acts.shape
    each = rows // count
    for i, mask in enumerate(order(count)):
        acts[block_rows_of(place, mask, each), :] = blocks[i][...]
    ids = groups[pl.ds(place[0], 1), :].astype(F32)
    key_place = lax.broadcasted_iota(jnp.int32, (1, rows), 1)
    key_ids = jnp.where(key_place < lengths[place[0]], ids, 1e9)
    upright = jnp.transpose(jnp.broadcast_to(ids, (8, rows)))[:, :1]
    bias[...] = jnp.where(key_ids <= upright, 0.0, -1e30)
    place_of = lax.broadcasted_iota(jnp.int32, (rows, LANES), 1)
    lane = place_of // HEAD_DIM
    inverses = jnp.zeros((rows, LANES), F32)
    tile = 2 * LANES
    for start in range(0, width, tile):
        part = slice(start, start + tile)
        x = acts[...]
        q = (dot(x, query_weight[:, part]) + line(query_bias)[:, part]).astype(BF16)
        k = dot(x, key_weight[:, part]).astype(BF16)
        v = (dot(x, value_weight[:, part]) + line(value_bias)[:, part]).astype(BF16)
        q_ref[:, part] = q
        k_ref[:, part] = k
        v_ref[:, part] = v
        q = q * jnp.asarray(1.0 / math.sqrt(HEAD_DIM), BF16)
        for pair in range(tile // LANES):
            at = slice(pair * LANES, (pair + 1) * LANES)
            q2, k2, v2 = q[:, at], k[:, at], v[:, at]
            sums = []
            for head in range(2):
                mine = lane == head
                s = dot(jnp.where(mine, q2, jnp.zeros_like(q2)), k2, CONTRACT_LAST) + bias[...]
                e = jnp.exp(s - jnp.max(s, -1, keepdims=True)).astype(BF16)
                e_ref[(start + pair * LANES) // HEAD_DIM + head] = e
                sums.append(dot(e, jnp.where(mine, v2, jnp.ones_like(v2))))
            top = jnp.where(lane == 0, sums[0], sums[1])
            under = pltpu.roll(jnp.where(lane == 0, sums[1], sums[0]), HEAD_DIM, 1)
            inverse = 1.0 / under
            first = (start + pair * LANES) // HEAD_DIM
            inverses = jnp.where(place_of == first, inverse, inverses)
            inverses = jnp.where(place_of == first + 1, pltpu.roll(inverse, HEAD_DIM, 1), inverses)
            o_ref[:, start + pair * LANES : start + (pair + 1) * LANES] = (top * inverse).astype(BF16)
    inverse_ref[...] = inverses


def attend(place, lengths, groups, blocks, weights, after):
    each, width = blocks[0].shape
    rows = len(blocks) * each
    wide = low(rows, width)
    return call(
        functools.partial(attend_kernel, len(blocks)),
        "attend",
        (place, lengths),
        (groups, *blocks, *weights),
        (wide, wide, wide, wide, wide, low(width // HEAD_DIM, rows, rows), full(rows, LANES)),
        scratch=[pltpu.VMEM((rows, rows), F32)],
        limit=6,
        after=after,
    )


def attend_back_kernel(e_ref, q_ref, k_ref, v_ref, o_ref, inverse_ref, do_ref, dq_ref, dk_ref, dv_ref):
    rows, width = q_ref.shape
    scale = 1.0 / math.sqrt(HEAD_DIM)
    lane = lax.broadcasted_iota(jnp.int32, (rows, LANES), 1) // HEAD_DIM
    for pair in range(width // LANES):
        at = slice(pair * LANES, (pair + 1) * LANES)
        q, k, v = q_ref[:, at], k_ref[:, at], v_ref[:, at]
        inverse = jnp.where(
            lane == 0, inverse_ref[:, 2 * pair : 2 * pair + 1], inverse_ref[:, 2 * pair + 1 : 2 * pair + 2]
        )
        do = do_ref[:, at].astype(F32) * inverse
        weighed = do * o_ref[:, at].astype(F32)
        do = do.astype(BF16)
        q_up, do_up = jnp.transpose(q), jnp.transpose(do)
        dq, dk, dv = [], [], []
        for head in range(2):
            mine = lane == head
            part = slice(head * HEAD_DIM, (head + 1) * HEAD_DIM)
            row_dot = jnp.sum(jnp.where(mine, weighed, 0.0), -1, keepdims=True)
            d = dot(jnp.where(mine, do, jnp.zeros_like(do)), v, CONTRACT_LAST) - row_dot
            e = e_ref[2 * pair + head]
            ds = (e.astype(F32) * d).astype(BF16)
            dq.append(dot(ds, k))
            dk.append(dot(q_up[part], ds))
            dv.append(dot(do_up[part], e))
        dq_ref[:, at] = (jnp.where(lane == 0, dq[0], dq[1]) * scale).astype(BF16)
        dk_ref[:, at] = (jnp.transpose(jnp.concatenate(dk, 0)) * scale).astype(BF16)
        dv_ref[:, at] = jnp.transpose(jnp.concatenate(dv, 0)).astype(BF16)


def attend_back(arrays, after):
    wide = low(*arrays[1].shape)
    return call(
        attend_back_kernel,
        "attend_back",
        (),
        arrays,
        (wide, wide, wide),
        limit=5.5,
        after=after,
        cost=30.0,
    )


def feed_kernel(count, place, *refs):
    (acts, context, output_weight, output_bias, first_gain, first_shift, inner_weight, inner_bias) = refs[:8]
    outer_weight, outer_bias, second_gain, second_shift = refs[8:12]
    settled_low, hat_ref, inverse_ref, active_ref, slope_ref, hat_two, inverse_two = refs[12:19]
    own_block, far_pair, near_block, acc = refs[19:]
    outs = (own_block, far_pair.at[0], far_pair.at[1], near_block)
    rows, high = active_ref.shape
    hat, inverse = norm_parts(
        acts[...].astype(F32) + dot(context[...], output_weight[...]) + line(output_bias)
    )
    hat_ref[...] = hat.astype(BF16)
    inverse_ref[...] = jnp.broadcast_to(inverse, inverse_ref.shape)
    settled = hat * line(first_gain) + line(first_shift)
    settled_low[...] = settled.astype(BF16)
    acc[...] = settled + line(outer_bias)
    tile = 4 * LANES
    for start in range(0, high, tile):
        part = slice(start, start + tile)
        inner = dot(settled_low[...], inner_weight[:, part]) + line(inner_bias)[:, part]
        active, slope = gate_parts(inner)
        active_ref[:, part] = active.astype(BF16)
        slope_ref[:, part] = slope.astype(BF16)
    acc[...] += dot(active_ref[...], outer_weight[...])
    each = rows // count
    gain, shift = line(second_gain), line(second_shift)
    for i, mask in enumerate(order(count)):
        own = block_rows_of(place, mask, each)
        hat, inverse = norm_parts(acc[own, :])
        outs[i][...] = (hat * gain + shift).astype(BF16)
        hat_two[own, :] = hat
        inverse_two[own, :] = jnp.broadcast_to(inverse, (each, LANES))


def feed(place, acts, context, weights, count):
    rows, width = acts.shape
    high = weights[4].shape[1]
    wide = low(rows, width)
    return call(
        functools.partial(feed_kernel, count),
        "feed",
        (place,),
        (acts, context, *weights),
        (
            wide,
            wide,
            full(rows, LANES),
            low(rows, high),
            low(rows, high),
            full(rows, width),
            full(rows, LANES),
        )
        + (low(rows // count, width), low(2, rows // count, width), low(rows // count, width)),
        limit=7.5,
        scratch=[pltpu.VMEM((rows, width), F32)],
    )


def turn_kernel(count, place, hat_two, inverse_two, second_gain, *refs):
    cotangents = refs[:count]
    branch, sums = refs[count:]
    each = hat_two.shape[0] // count
    gain = line(second_gain)
    totals = [0.0, 0.0, 0.0]
    for i, mask in enumerate(order(count)):
        own = block_rows_of(place, mask, each)
        hat = hat_two[own, :]
        upper = cotangents[i][pl.ds(0, each), :].astype(F32)
        d = norm_back(upper, hat, inverse_two[own, :1], gain)
        d_low = d.astype(BF16)
        branch[own, :] = d_low
        for j, term in enumerate((d_low.astype(F32), upper * hat, upper)):
            totals[j] = totals[j] + jnp.sum(term, 0, keepdims=True)
    for i in range(3):
        sums[i : i + 1, :] = totals[i]


def turn(place, hat_two, inverse_two, second_gain, cotangents):
    rows, width = hat_two.shape
    return call(
        functools.partial(turn_kernel, len(cotangents)),
        "turn",
        (place,),
        (hat_two, inverse_two, second_gain, *cotangents),
        (low(rows, width), full(8, width)),
    )


def feed_back_kernel(
    branch,
    outer_weight,
    slope,
    inner_weight,
    hat_ref,
    inverse_ref,
    first_gain,
    output_weight,
    turn_sums,
    d_inner_ref,
    mixed,
    d_context,
    sums,
    acc,
):
    rows, high = slope.shape
    width = acc.shape[1]
    tile = 4 * LANES
    for start in range(0, high, tile):
        part = slice(start, start + tile)
        d_active = dot(branch[...], outer_weight[part, :], CONTRACT_LAST)
        d_inner = (d_active * slope[:, part].astype(F32)).astype(BF16)
        d_inner_ref[:, part] = d_inner
        partial = jnp.sum(d_inner.astype(F32), 0, keepdims=True)
        for lane in range(start, start + tile, LANES):
            row = 6 + lane // width
            sums[row : row + 1, lane % width : lane % width + LANES] = partial[:, lane - start : lane - start + LANES]
    acc[...] = branch[...].astype(F32) + dot(d_inner_ref[...], inner_weight[...], CONTRACT_LAST)
    parts = 4
    totals = [0.0, 0.0, 0.0]
    gain = line(first_gain)
    for part in range(parts):
        own = slice(part * (rows // parts), (part + 1) * (rows // parts))
        upper = acc[own, :]
        hat = hat_ref[own, :].astype(F32)
        d = norm_back(upper, hat, inverse_ref[own, :1], gain)
        d_low = d.astype(BF16)
        mixed[own, :] = d_low
        for i, term in enumerate((d_low.astype(F32), upper * hat, upper)):
            totals[i] = totals[i] + jnp.sum(term, 0, keepdims=True)
    for i in range(3):
        sums[i : i + 1, :] = totals[i]
    sums[3:6, :] = turn_sums[0:3, :]
    d_context[...] = dot(mixed[...], output_weight[...], CONTRACT_LAST).astype(BF16)


def feed_back(arrays, after):
    rows, width = arrays[0].shape
    high = arrays[2].shape[1]
    wide = low(rows, width)
    return call(
        feed_back_kernel,
        "feed_back",
        (),
        arrays,
        (low(rows, high), wide, wide, full(16, width)),
        scratch=[pltpu.VMEM((rows, width), F32)],
        after=after,
        cost=30.0,
        limit=5,
    )


def entry_back_kernel(count, place, d_first, dq, dk, dv, wq, wk, wv, *refs):
    outs, acc = refs[:count], refs[count]
    each = dq.shape[0] // count
    acc[...] = (
        d_first[...].astype(F32)
        + dot(dq[...], wq[...], CONTRACT_LAST)
        + dot(dk[...], wk[...], CONTRACT_LAST)
        + dot(dv[...], wv[...], CONTRACT_LAST)
    )
    for i, mask in enumerate(order(count)):
        outs[i][...] = acc[block_rows_of(place, mask, each), :].astype(BF16)


def entry_back(place, arrays, count, after):
    rows, width = arrays[1].shape
    return call(
        functools.partial(entry_back_kernel, count),
        "entry_back",
        (place,),
        arrays,
        (low(rows // count, width),) * count,
        scratch=[pltpu.VMEM((rows, width), F32)],
        after=after,
        limit=4,
    )


def add_vectors(place, d_first, dq, dk, dv, weights, early_sums, flagged, sums):
    count = len(flagged)
    each, width = dq.shape[0] // count, dq.shape[1]
    row = lax.broadcasted_iota(jnp.int32, (each, each), 0)
    column = lax.broadcasted_iota(jnp.int32, (each, each), 1)
    zero, one = [0.0] * 4, [0.0] * 4
    for at, mask in enumerate(order(count)):
        own = block_rows_of(place, mask, each)
        flag = flagged[at][pl.ds(each, 16), pl.ds(0, each)][:1].astype(F32)
        upright = jnp.sum(jnp.where(row == column, flag, 0.0), 1, keepdims=True)
        for i, array in enumerate((d_first, dq, dk, dv)):
            value = array[own, :].astype(F32)
            zero[i] = zero[i] + jnp.sum(value * (1.0 - upright), 0, keepdims=True)
            one[i] = one[i] + jnp.sum(value * upright, 0, keepdims=True)
    by_flag = jnp.concatenate([zero[0], one[0]] + [jnp.zeros((6, width), F32)], 0)
    for i, weight in enumerate(weights):
        pair = jnp.concatenate([zero[i + 1], one[i + 1]] + [jnp.zeros((6, width), F32)], 0)
        by_flag = by_flag + dot(pair.astype(BF16), weight[...], CONTRACT_LAST)
    second = jnp.concatenate([by_flag[:2], zero[1] + one[1], zero[3] + one[3]], 0)
    first = early_sums[0:6, :]
    pieces = sums.shape[0]
    piece = width // pieces
    sums[...] = jnp.zeros(sums.shape, F32)
    for i in range(pieces):
        part = slice(i * piece, (i + 1) * piece)
        at, lane = divmod(i * 4 * piece, width)
        sums[i, 0:6, 0:piece] = first[:, part]
        sums[i, 0:4, LANES : LANES + piece] = second[:, part]
        sums[i, 0:1, 2 * LANES : 2 * LANES + 4 * piece] = early_sums[6 + at : 7 + at, lane : lane + 4 * piece]


def vector_pieces_kernel(place, d_first, dq, dk, dv, wq, wk, wv, early_sums, *refs):
    add_vectors(place, d_first, dq, dk, dv, (wq, wk, wv), early_sums, refs[:-1], refs[-1])


def vector_pieces(place, arrays, flagged, pieces):
    return call(
        vector_pieces_kernel,
        "vector_pieces",
        (place,),
        (*arrays, *flagged),
        full(pieces, 8, SIDE // 2),
    )


def parts_of(place):
    x, y = place[2], place[3]
    far, beside, behind, own = 2 * (1 - y) + 1 - x, 2 * y + 1 - x, 2 * (1 - y) + x, 2 * y + x
    return ((far, 0), (beside, 0), (far, 1), (behind, 1), (behind, 0), (beside, 1), (own, 0), (own, 1))


def tall_gradient_kernel(keep, place, left, right, out):
    rows = left.shape[1] // GROUPS // 2
    core = place[1] if keep else 1 - place[1]
    parts = parts_of(place)
    half = SIDE // 2
    for group, homes in ((0, (0, 2)), (1, (1, 5)), (3, (4, 3)), (6, (6, 7))):
        columns = pl.ds(pl.multiple_of((2 * parts[group][0] + core) * rows, LANES), rows)
        product = dot(left[:, columns], right[...], CONTRACT_FIRST).reshape(SHARES, PIECE, SIDE)
        for side, home in enumerate(homes):
            out[home] = product[:, :, side * half : (side + 1) * half].astype(BF16)


def tall_gradient(place, left, right, keep, after=(), cost=2.0):
    return call(
        functools.partial(tall_gradient_kernel, keep),
        "tall_gradient",
        (place,),
        (left, right),
        low(8, SHARES, PIECE, SIDE // 2),
        after=after,
        cost=cost,
    )


def stack_pieces(place, totals, send, keep, start, last=None):
    each = SIDE // (GROUPS * SHARES * 2)
    half = SIDE // 2
    for out, core in ((send, 1 - place[1]), (keep, place[1])):
        for home, (group, side) in enumerate(parts_of(place)):
            columns = slice(side * half, (side + 1) * half)
            for share in range(SHARES):
                index = (2 * group + core) * SHARES + share
                row = pl.multiple_of(index * each, 8)
                pieces = [t[pl.ds(row, each), columns] for t in totals]
                if last is not None:
                    pieces.append(last[index] if side == 0 else jnp.zeros(last.shape[1:], F32))
                piece = jnp.concatenate(pieces, 0)
                out[home, share, start : start + piece.shape[0], :] = piece.astype(BF16)


def wide_gradient_kernel(place, left, right, context, mixed, send, keep, first, second):
    for half in range(2):
        start = 2 * half * SIDE
        first[...] = dot(left[...], right[:, start : start + SIDE], CONTRACT_FIRST)
        second[...] = dot(left[...], right[:, start + SIDE : start + 2 * SIDE], CONTRACT_FIRST)
        stack_pieces(place, (first, second), send, keep, half * PIECE // 2)
    first[...] = dot(context[...], mixed[...], CONTRACT_FIRST)
    stack_pieces(place, (first,), send, keep, PIECE)


def wide_gradient(place, arrays, cost=1.0):
    eight = low(8, SHARES, PIECE + PIECE // 4, SIDE // 2)
    return call(
        wide_gradient_kernel,
        "wide_gradient",
        (place,),
        arrays,
        (eight, eight),
        scratch=[pltpu.VMEM((SIDE, SIDE), F32)] * 2,
        cost=cost,
        limit=6.5,
    )


def square_gradients_kernel(place, acts, d_first, dq, dk, dv, wq, wk, wv, early_sums, *refs):
    flagged, (send, keep, first, second, sums) = refs[:-5], refs[-5:]
    first[...] = dot(acts[...], dq[...], CONTRACT_FIRST)
    second[...] = dot(acts[...], dk[...], CONTRACT_FIRST)
    add_vectors(place, d_first, dq, dk, dv, (wq, wk, wv), early_sums, flagged, sums)
    stack_pieces(place, (first, second), send, keep, 0)
    first[...] = dot(acts[...], dv[...], CONTRACT_FIRST)
    stack_pieces(place, (first,), send, keep, PIECE // 2, sums)


def square_gradients(place, arrays, flagged, pieces, after, cost=0.1):
    eight = low(8, SHARES, 3 * PIECE // 4 + 8, SIDE // 2)
    return call(
        square_gradients_kernel,
        "square_gradients",
        (place,),
        (*arrays, *flagged),
        (eight, eight),
        scratch=[pltpu.VMEM((SIDE, SIDE), F32)] * 2 + [pltpu.VMEM((pieces, 8, SIDE // 2), F32)],
        after=after,
        cost=cost,
        limit=8,
    )


def first_sums_kernel(keep, got, to_x, to_y):
    to_x[...] = total([keep[0:2], got[0:2]]).astype(BF16)
    to_y[...] = total([keep[2:4], got[2:4]]).astype(BF16)


def second_sums_kernel(start, keep, got, from_x, from_y, to_y, to_x):
    to_y[...] = total([keep[start], got[start], from_x[0]]).astype(BF16)
    to_x[...] = total([keep[start + 1], got[start + 1], from_y[0]]).astype(BF16)


def third_sums_kernel(start, place, keep, got, from_x, from_y, then_y, then_x, send, kept):
    half = SIDE // 2
    bit = place[0] & 1
    for out, share_bit in ((send, 1 - bit), (kept, bit)):
        for high in range(SHARES // 2):
            share = 2 * high + share_bit
            a = total([keep[start + 2, share], got[start + 2, share], from_x[1, share], then_y[share]])
            b = total([keep[start + 3, share], got[start + 3, share], from_y[1, share], then_x[share]])
            out[high, :, :half] = a.astype(out.dtype)
            out[high, :, half:] = b.astype(out.dtype)


def fourth_sums_kernel(place, kept, got, send):
    other = 1 - (place[0] >> 1)
    send[...] = total([kept[other], got[other]]).astype(BF16)


def last_sums_kernel(form, place, kept, got, last, *refs):
    count = (len(refs) - 2) // 2
    outs, token, staged, semaphores = refs[:count], refs[count], refs[count + 1 : -1], refs[-1]
    token[...] = jnp.zeros(token.shape, F32)
    mine = place[0] >> 1
    result = total([kept[mine], got[mine], last[...]])
    each = PIECE // 4
    rows = [result[i * each : (i + 1) * each] for i in range(result.shape[0] // each)]
    if form == "tall":
        staged[0][...] = result
    elif form == "wide":
        for i in range(4):
            staged[0][:, i * SIDE : (i + 1) * SIDE] = rows[i]
        staged[1][...] = rows[4]
    else:
        for i in range(3):
            staged[i][...] = rows[i]
        vectors = result[3 * each :]
        staged[3][...] = vectors[0:2, LANES : LANES + each]
        staged[4][...] = vectors[0, 2 * LANES : 2 * LANES + 4 * each]
        for i in range(8):
            row, lane = (i, 0) if i < 6 else (i - 4, LANES)
            staged[5 + i][...] = vectors[row, lane : lane + each]
    for copy in fetch(staged, outs, semaphores):
        copy.wait()


class Halving:
    def __init__(self, place, send, keep):
        self.place, self.keep = place, keep
        self.got = [swap_pairs(part, "batch", 1) for part in send]
        self.late = 0 if len(keep) > 1 else 4

    def step(self, kernel, name, scalars, arrays, outs, after, cost=0.5):
        results = call(kernel, name, scalars, arrays, outs, after=after, cost=cost)
        self.done = results[:1]
        return results

    def first(self, after=(), cost=0.5):
        half = low(2, *self.keep[0].shape[1:])
        arrays = (self.keep[0], self.got[0])
        to = self.step(first_sums_kernel, "first_sums", (), arrays, (half, half), after, cost)
        self.from_x, self.from_y = swap_pairs(to[0], "batch", 2), swap_pairs(to[1], "batch", 4)

    def second(self, after=(), cost=0.5):
        quarter = low(*self.keep[0].shape[1:])
        arrays = (self.keep[-1], self.got[-1], self.from_x, self.from_y)
        kernel = functools.partial(second_sums_kernel, self.late)
        to = self.step(kernel, "second_sums", (), arrays, (quarter, quarter), after, cost)
        self.then_y, self.then_x = swap_pairs(to[0], "batch", 4), swap_pairs(to[1], "batch", 2)

    def third(self, after=(), cost=0.5):
        shape = (SHARES // 2, self.keep[0].shape[2], SIDE)
        arrays = (self.keep[-1], self.got[-1], self.from_x, self.from_y, self.then_y, self.then_x)
        outs = (low(*shape), full(*shape))
        kernel = functools.partial(third_sums_kernel, self.late)
        to, self.kept = self.step(kernel, "third_sums", (self.place,), arrays, outs, after, cost)
        self.pair = swap_pairs(to, "seq", 1)

    def fourth(self, after=(), cost=0.5):
        arrays = (self.kept, self.pair)
        outs = (low(*self.kept.shape[1:]),)
        (to,) = self.step(fourth_sums_kernel, "fourth_sums", (self.place,), arrays, outs, after, cost)
        self.others = swap_pairs(to, "seq", 2)

    def last(self, form, after=()):
        each = PIECE // 4
        shapes = {
            "tall": [(PIECE, SIDE)],
            "wide": [(each, 4 * SIDE), (each, SIDE)],
            "square": [(each, SIDE)] * 3 + [(2, each), (4 * each,)] + [(each,)] * 8,
        }[form]
        *self.result, token = call(
            functools.partial(last_sums_kernel, form),
            "last_sums",
            (self.place,),
            (self.kept, self.pair, self.others),
            tuple(full(*shape) for shape in shapes),
            scratch=[pltpu.VMEM(shape, F32) for shape in shapes] + [pltpu.SemaphoreType.DMA((len(shapes),))],
            after=after,
            cost=0.5,
            out_far=True,
        )
        self.done = (token,)


def add_pieces(pieces):
    batch, seq = lax.axis_size("batch"), lax.axis_size("seq")
    parts = [pieces.reshape((2,) * ((batch * seq).bit_length() - 1) + pieces.shape[1:])]
    for axis in ("batch", "seq"):
        bits = lax.axis_size(axis).bit_length() - 1
        for bit in range(bits):
            parts = [total(halve(parts, bits - 1 - bit, axis, bit, F32))]
    return parts[0]


def per_device(
    hidden,
    groups,
    answer_flags,
    lengths,
    answer_embed,
    query_weight,
    query_bias,
    key_weight,
    value_weight,
    value_bias,
    output_weight,
    output_bias,
    first_gain,
    first_shift,
    inner_weight,
    inner_bias,
    outer_weight,
    outer_bias,
    second_gain,
    second_shift,
    cotangent,
):
    items, block_rows, width = hidden.shape
    batch, seq = lax.axis_size("batch"), lax.axis_size("seq")
    me, group = lax.axis_index("seq"), lax.axis_index("batch")
    place = jnp.stack([me, group & 1, (group >> 1) & 1, (group >> 2) & 1]).astype(jnp.int32)
    high = inner_weight.shape[1]
    even = (batch, seq, width, high) == (8, SHARES, SIDE, 4 * SIDE)

    arrays = (hidden, answer_flags, answer_embed)
    masks = order(items)
    far_blocks = entry_blocks(place, masks[1:-1], arrays)
    near_blocks = entry_blocks(place, (masks[0], masks[-1]), arrays, far_blocks[:1])
    got = exchange([near_blocks[0], *far_blocks, near_blocks[1]])
    output_near, inner_near, outer_near = load((output_weight, inner_weight, outer_weight), near_blocks[:1])
    upper = exchange(flagged_blocks(place, cotangent, answer_flags, (*got[1:-1], output_near)))
    acts, queries, keys, values, context, exponents, inverse_sums = attend(
        place,
        lengths,
        groups,
        got,
        (query_weight, query_bias, key_weight, value_weight, value_bias),
        (),
    )
    settled, hat, inverse, active, slope, hat_two, inverse_two, *output = feed(
        place,
        acts,
        context,
        (
            output_near,
            output_bias,
            first_gain,
            first_shift,
            inner_near,
            inner_bias,
            outer_near,
            outer_bias,
            second_gain,
            second_shift,
        ),
        items,
    )
    branch, sums = turn(place, hat_two, inverse_two, second_gain, upper)
    if even:
        send = tall_gradient(place, active, branch, False)
        keep = tall_gradient(place, active, branch, True, (send,))
        outer = Halving(place, (send,), (keep,))
        outer.first()
        after = outer.done
    else:
        outer_weight_gradient = scatter(dot(active, branch, CONTRACT_FIRST))
        after = ()
    output_own, output_far, output_near_block = output
    output_got = swap_pairs(output_far, "seq", 2)
    d_inner, mixed, d_context, sums = feed_back(
        (
            branch,
            outer_near,
            slope,
            inner_near,
            hat,
            inverse,
            first_gain,
            output_near,
            sums,
        ),
        after,
    )
    if even:
        send, keep = wide_gradient(place, (settled, d_inner, context, mixed))
        inner = Halving(place, (send,), (keep,))
        outer.second((send,))
        after = (*outer.done, output_got)
    else:
        inner_weight_gradient = scatter(dot(settled, d_inner, CONTRACT_FIRST))
    weights = (query_weight, key_weight, value_weight)
    d_queries, d_keys, d_values = attend_back(
        (exponents, queries, keys, values, context, inverse_sums, d_context),
        after,
    )
    if even:
        inner.first((d_queries,))
        outer.third(inner.done)
        after = outer.done
    input_gradient = entry_back(
        place, (mixed, d_queries, d_keys, d_values, *weights), items, after
    )
    back = exchange(input_gradient)
    if even:
        send, keep = square_gradients(
            place,
            (acts, mixed, d_queries, d_keys, d_values, *weights, sums),
            upper,
            batch * seq,
            input_gradient[:1],
        )
        narrow = Halving(place, (send,), (keep,))
        relayed = relay(output_near_block, output_got, (send,))
        near_got = swap_pairs(relayed, "seq", 1)
        outer.fourth((relayed, back[1]))
        inner.second(outer.done, cost=25.0)
        narrow.first((*inner.done, outer.others))
        output, token = join_pairs(place, output_own, output_got, near_got, narrow.done)
        inner.third((token,))
        outer.last("tall", inner.done)
        narrow.second((*outer.done, back[2]))
        inner.fourth(narrow.done)
        narrow.third((*inner.done, back[3]))
        inner.last("wide", narrow.done)
        input_gradient, token = join_blocks(place, back, inner.done)
        narrow.fourth((token,))
        narrow.last("square")
        (outer_weight_gradient,), (inner_weight_gradient, output_weight_gradient) = outer.result, inner.result
        vectors = narrow.result[5:]
        *narrow, embed_gradient, inner_bias_gradient = narrow.result[:5]
    else:
        squares = jnp.concatenate(
            [
                dot(left, right, CONTRACT_FIRST).astype(BF16)
                for left, right in (
                    (context, mixed),
                    (acts, d_queries),
                    (acts, d_keys),
                    (acts, d_values),
                )
            ],
            1,
        )
        output_weight_gradient, *narrow = jnp.split(scatter(squares), 4, 1)
        pieces = add_pieces(
            vector_pieces(
                place, (mixed, d_queries, d_keys, d_values, *weights, sums), upper, batch * seq
            )
        )
        early, later = pieces[:, : width // (batch * seq)], pieces[:, LANES : LANES + width // (batch * seq)]
        embed_gradient, inner_bias_gradient = later[0:2], pieces[0, 2 * LANES : 2 * LANES + high // (batch * seq)]
        vectors = [early[i] for i in range(6)] + [later[2], later[3]]
        near_got = swap_pairs(relay(output_near_block, output_got, ()), "seq", 1)
        output, _ = join_pairs(place, output_own, output_got, near_got, ())
        input_gradient, _ = join_blocks(place, back)
    query_weight_gradient, key_weight_gradient, value_weight_gradient = narrow
    return (
        output,
        input_gradient,
        embed_gradient,
        query_weight_gradient,
        vectors[6],
        key_weight_gradient,
        value_weight_gradient,
        vectors[7],
        output_weight_gradient,
        vectors[0],
        vectors[1],
        vectors[2],
        inner_weight_gradient,
        inner_bias_gradient,
        outer_weight_gradient,
        vectors[3],
        vectors[4],
        vectors[5],
    )


def solution(mesh):
    both = ("batch", "seq")
    in_specs = (
        (P("batch", "seq", None), P("batch", None), P("batch", "seq"), P("batch"))
        + (P(),) * 16
        + (P("batch", "seq", None),)
    )
    matrix, vector = P(both, None), P(both)
    out_specs = (
        P("batch", "seq", None),
        P("batch", "seq", None),
        P(None, both),
        matrix,
        vector,
        matrix,
        matrix,
        vector,
        matrix,
        vector,
        vector,
        vector,
        matrix,
        vector,
        matrix,
        vector,
        vector,
        vector,
    )
    return jax.shard_map(
        per_device, mesh=mesh, in_specs=in_specs, out_specs=out_specs, check_vma=False
    )
```

```python
import functools
import math

import jax
import jax.numpy as jnp
from jax import lax
from jax.experimental import pallas as pl
from jax.experimental.pallas import tpu as pltpu
from jax.sharding import PartitionSpec as P

HEAD_DIM = 64
LANES = 128
EPSILON = 1e-12
BF16 = jnp.bfloat16
F32 = jnp.float32

CONTRACT_LAST = (((1,), (1,)), ((), ()))
CONTRACT_FIRST = (((0,), (0,)), ((), ()))
GROUPS, SHARES, PIECE, SIDE = 4, 4, 96, 768
MICROSECOND = 1150000000
PARTS = 4


def dot(a, b, dims=(((1,), (0,)), ((), ()))):
    return lax.dot_general(a, b, dims, preferred_element_type=F32)


def low(*shape):
    return jax.ShapeDtypeStruct(shape, BF16)


def full(*shape):
    return jax.ShapeDtypeStruct(shape, F32)


def call(kernel, name, scalars, arrays, outs, limit=4, scratch=(), far=(), after=(), cost=4.0, out_far=False):
    count = len(scalars) + len(arrays) + len(far)

    def body(*refs):
        kernel(*refs[:count], *refs[count + len(after) :])

    single = not isinstance(outs, tuple)
    vmem, hbm = pl.BlockSpec(memory_space=pltpu.VMEM), pl.BlockSpec(memory_space=pltpu.HBM)
    specs = () if single else (vmem,) * len(outs)
    if out_far:
        specs = (hbm,) * len(outs) + (vmem,)
        outs = tuple(pltpu.HBM(o.shape, o.dtype) for o in outs) + (full(8, LANES),)
    return pl.pallas_call(
        body,
        in_specs=[pl.BlockSpec(memory_space=pltpu.SMEM)] * len(scalars)
        + [vmem] * len(arrays)
        + [hbm] * len(far)
        + [pl.BlockSpec(memory_space=pl.ANY)] * len(after),
        out_specs=vmem if single else specs,
        out_shape=outs,
        scratch_shapes=list(scratch),
        compiler_params=pltpu.CompilerParams(vmem_limit_bytes=int(limit * (1 << 20))),
        cost_estimate=pl.CostEstimate(flops=int(cost * MICROSECOND), bytes_accessed=1 << 16, transcendentals=0),
        name=name,
    )(*scalars, *arrays, *(pltpu.with_memory_space_constraint(a, pltpu.HBM) for a in far), *after)


def fetch(sources, targets, semaphores, parts=1):
    copies = []
    for source, target in zip(sources, targets):
        rows = source.shape[0] // parts
        for part in range(parts):
            own = pl.ds(part * rows, rows)
            copies.append(
                pltpu.make_async_copy(source.at[own], target.at[own], semaphores.at[len(copies)])
            )
    for copy in copies:
        copy.start()
    return copies


def line(ref):
    return ref[...].astype(F32)[None]


def order(count):
    return sorted(range(count), key=lambda mask: (mask != 0, mask < 2, mask))


def block_rows_of(place, mask, each):
    return pl.ds(pl.multiple_of((place[0] ^ mask) * each, each), each)


def entry_kernel(masks, place, hidden, flags, embed, *refs):
    count = len(masks)
    outs, (near, near_flags, near_embed, semaphores) = refs[:count], refs[count:]
    items = [place[0] ^ mask for mask in masks]
    sources = [hidden.at[item] for item in items] + [flags, embed]
    targets = [near.at[i] for i in range(count)] + [near_flags, near_embed]
    for copy in fetch(sources, targets, semaphores):
        copy.wait()
    rows = hidden.shape[1]
    row = lax.broadcasted_iota(jnp.int32, (rows, rows), 0)
    column = lax.broadcasted_iota(jnp.int32, (rows, rows), 1)
    first, second = near_embed[0:1].astype(F32), near_embed[1:2].astype(F32)
    for i, item in enumerate(items):
        flag = near_flags[pl.ds(item, 1), :].astype(F32)
        upright = jnp.sum(jnp.where(row == column, flag, 0.0), 1, keepdims=True)
        added = jnp.where(upright == 1.0, second, first)
        outs[i][...] = (near[i].astype(F32) + added).astype(BF16)


def entry_blocks(place, masks, arrays, after=()):
    hidden, flags, embed = arrays
    rows, width = hidden.shape[1:]
    count = len(masks)
    return call(
        functools.partial(entry_kernel, masks),
        "entry_blocks",
        (place,),
        (),
        (low(rows, width),) * count,
        scratch=[
            pltpu.VMEM((count, rows, width), BF16),
            pltpu.VMEM(flags.shape, flags.dtype),
            pltpu.VMEM(embed.shape, embed.dtype),
            pltpu.SemaphoreType.DMA((count + 2,)),
        ],
        far=arrays,
        after=after,
        cost=0.5,
    )


def flagged_kernel(count, place, cotangent, flags, *outs):
    rows = cotangent.shape[1]
    for i, mask in enumerate(order(count)):
        item = place[0] ^ mask
        outs[i][pl.ds(0, rows), :] = cotangent[item]
        outs[i][pl.ds(rows, 16), :] = jnp.zeros((16, cotangent.shape[2]), BF16)
        flag = jnp.broadcast_to(flags[pl.ds(item, 1), :].astype(F32), (16, rows))
        outs[i][pl.ds(rows, 16), pl.ds(0, rows)] = flag.astype(BF16)


def flagged_blocks(place, cotangent, flags, after):
    count, rows, width = cotangent.shape
    return call(
        functools.partial(flagged_kernel, count),
        "flagged_blocks",
        (place,),
        (cotangent, flags),
        (low(rows + 16, width),) * count,
        after=after,
    )


def join_kernel(count, place, *refs):
    blocks, (out, token, semaphores) = refs[:count], refs[count:]
    token[...] = jnp.zeros(token.shape, F32)
    copies = [
        pltpu.make_async_copy(blocks[i], out.at[place[0] ^ mask], semaphores.at[i])
        for i, mask in enumerate(order(count))
    ]
    for copy in copies:
        copy.start()
    for copy in copies:
        copy.wait()


def join_blocks(place, blocks, after=()):
    return call(
        functools.partial(join_kernel, len(blocks)),
        "join_blocks",
        (place,),
        blocks,
        (low(len(blocks), *blocks[0].shape),),
        scratch=[pltpu.SemaphoreType.DMA((len(blocks),))],
        after=after,
        cost=0.5,
        out_far=True,
    )


def relay_kernel(near, got, out):
    out[0] = near[...]
    out[1] = got[1]


def relay(near, got, after):
    return call(relay_kernel, "relay", (), (near, got), low(2, *near.shape), after=after, cost=0.5)


def join_pairs_kernel(place, own, got, near_got, out, token, semaphores):
    token[...] = jnp.zeros(token.shape, F32)
    me = place[0]
    sources = (own, got.at[0], near_got.at[0], near_got.at[1])
    for copy in fetch(sources, [out.at[me ^ mask] for mask in (0, 2, 1, 3)], semaphores):
        copy.wait()


def join_pairs(place, own, got, near_got, after):
    return call(
        join_pairs_kernel,
        "join_pairs",
        (place,),
        (own, got, near_got),
        (low(4, *own.shape),),
        scratch=[pltpu.SemaphoreType.DMA((4,))],
        after=after,
        cost=0.5,
        out_far=True,
    )


def swap_pairs(array, axis, mask):
    size = lax.axis_size(axis)
    return lax.ppermute(array, axis, [(i, i ^ mask) for i in range(size)])


def pick(array, index, dim):
    return lax.dynamic_index_in_dim(array, index, dim, keepdims=False)


def exchange(blocks):
    pairs = list(zip(order(len(blocks)), blocks))
    return [block if mask == 0 else swap_pairs(block, "seq", mask) for mask, block in pairs]


def total(parts):
    result = parts[0].astype(F32)
    for part in parts[1:]:
        result = result + part.astype(F32)
    return result


def halve(parts, dim, axis, bit, dtype=BF16):
    mine = (lax.axis_index(axis) >> bit) & 1
    sent = total([pick(part, 1 - mine, dim) for part in parts]).astype(dtype)
    got = swap_pairs(sent, axis, 1 << bit)
    return [pick(part, mine, dim) for part in parts] + [got]


def scatter(gradient):
    batch, seq = lax.axis_size("batch"), lax.axis_size("seq")
    rows, columns = gradient.shape
    batch_bits, seq_bits = batch.bit_length() - 1, seq.bit_length() - 1
    each = rows // (batch * seq)
    shape = (2,) * (batch_bits + seq_bits) + (each, columns)
    parts = [gradient.astype(BF16).reshape(shape)]
    parts = halve(parts, batch_bits - 1, "batch", 0)
    ways = []
    for way in range(2):
        half = [
            lax.slice_in_dim(part, way * (columns // 2), (way + 1) * (columns // 2), axis=part.ndim - 1)
            for part in parts
        ]
        bits = list(range(1, batch_bits))
        if way:
            bits = bits[::-1]
        left = list(range(batch_bits - 1, 0, -1))
        for bit in bits:
            dim = left.index(bit)
            half = halve(half, dim, "batch", bit)
            left.remove(bit)
        ways.append(half)
    parts = [jnp.concatenate([a, b], -1) for a, b in zip(*ways)]
    for bit in range(seq_bits):
        parts = halve(parts, seq_bits - 1 - bit, "seq", bit)
    return total(parts)


def norm_parts(values):
    centre = values - jnp.mean(values, -1, keepdims=True)
    inverse = lax.rsqrt(jnp.mean(centre * centre, -1, keepdims=True) + EPSILON)
    return centre * inverse, inverse


def norm_back(upper, hat, inverse, gain):
    g = upper * gain
    return inverse * (
        g - jnp.mean(g, -1, keepdims=True) - hat * jnp.mean(g * hat, -1, keepdims=True)
    )


def gate_parts(u):
    share = 0.5 + 0.5 * lax.erf(u * 0.7071067811865476)
    return u * share, share + u * (jnp.exp(-0.5 * u * u) * 0.3989422804014327)


def load_kernel(*refs):
    count = len(refs) // 2
    for copy in fetch(refs[:count], refs[count:-1], refs[-1], PARTS):
        copy.wait()


def load(weights, after):
    return call(
        load_kernel,
        "load",
        (),
        (),
        tuple(low(*weight.shape) for weight in weights),
        scratch=[pltpu.SemaphoreType.DMA((PARTS * len(weights),))],
        far=weights,
        after=after,
    )


def attend_kernel(count, place, lengths, groups, *refs):
    blocks = refs[:count]
    query_weight, query_bias, key_weight, value_weight, value_bias = refs[count : count + 5]
    acts, q_ref, k_ref, v_ref, o_ref, e_ref, inverse_ref, bias = refs[count + 5 :]
    rows, width = acts.shape
    each = rows // count
    for i, mask in enumerate(order(count)):
        acts[block_rows_of(place, mask, each), :] = blocks[i][...]
    ids = groups[pl.ds(place[0], 1), :].astype(F32)
    key_place = lax.broadcasted_iota(jnp.int32, (1, rows), 1)
    key_ids = jnp.where(key_place < lengths[place[0]], ids, 1e9)
    upright = jnp.transpose(jnp.broadcast_to(ids, (8, rows)))[:, :1]
    bias[...] = jnp.where(key_ids <= upright, 0.0, -1e30)
    place_of = lax.broadcasted_iota(jnp.int32, (rows, LANES), 1)
    lane = place_of // HEAD_DIM
    inverses = jnp.zeros((rows, LANES), F32)
    tile = 2 * LANES
    for start in range(0, width, tile):
        part = slice(start, start + tile)
        x = acts[...]
        q = (dot(x, query_weight[:, part]) + line(query_bias)[:, part]).astype(BF16)
        k = dot(x, key_weight[:, part]).astype(BF16)
        v = (dot(x, value_weight[:, part]) + line(value_bias)[:, part]).astype(BF16)
        q_ref[:, part] = q
        k_ref[:, part] = k
        v_ref[:, part] = v
        q = q * jnp.asarray(1.0 / math.sqrt(HEAD_DIM), BF16)
        for pair in range(tile // LANES):
            at = slice(pair * LANES, (pair + 1) * LANES)
            q2, k2, v2 = q[:, at], k[:, at], v[:, at]
            sums = []
            for head in range(2):
                mine = lane == head
                s = dot(jnp.where(mine, q2, jnp.zeros_like(q2)), k2, CONTRACT_LAST) + bias[...]
                e = jnp.exp(s - jnp.max(s, -1, keepdims=True)).astype(BF16)
                e_ref[(start + pair * LANES) // HEAD_DIM + head] = e
                sums.append(dot(e, jnp.where(mine, v2, jnp.ones_like(v2))))
            top = jnp.where(lane == 0, sums[0], sums[1])
            under = pltpu.roll(jnp.where(lane == 0, sums[1], sums[0]), HEAD_DIM, 1)
            inverse = 1.0 / under
            first = (start + pair * LANES) // HEAD_DIM
            inverses = jnp.where(place_of == first, inverse, inverses)
            inverses = jnp.where(place_of == first + 1, pltpu.roll(inverse, HEAD_DIM, 1), inverses)
            o_ref[:, start + pair * LANES : start + (pair + 1) * LANES] = (top * inverse).astype(BF16)
    inverse_ref[...] = inverses


def attend(place, lengths, groups, blocks, weights, after):
    each, width = blocks[0].shape
    rows = len(blocks) * each
    wide = low(rows, width)
    return call(
        functools.partial(attend_kernel, len(blocks)),
        "attend",
        (place, lengths),
        (groups, *blocks, *weights),
        (wide, wide, wide, wide, wide, low(width // HEAD_DIM, rows, rows), full(rows, LANES)),
        scratch=[pltpu.VMEM((rows, rows), F32)],
        limit=6,
        after=after,
    )


def attend_back_kernel(e_ref, q_ref, k_ref, v_ref, o_ref, inverse_ref, do_ref, dq_ref, dk_ref, dv_ref):
    rows, width = q_ref.shape
    scale = 1.0 / math.sqrt(HEAD_DIM)
    lane = lax.broadcasted_iota(jnp.int32, (rows, LANES), 1) // HEAD_DIM
    for pair in range(width // LANES):
        at = slice(pair * LANES, (pair + 1) * LANES)
        q, k, v = q_ref[:, at], k_ref[:, at], v_ref[:, at]
        inverse = jnp.where(
            lane == 0, inverse_ref[:, 2 * pair : 2 * pair + 1], inverse_ref[:, 2 * pair + 1 : 2 * pair + 2]
        )
        do = do_ref[:, at].astype(F32) * inverse
        weighed = do * o_ref[:, at].astype(F32)
        do = do.astype(BF16)
        q_up, do_up = jnp.transpose(q), jnp.transpose(do)
        dq, dk, dv = [], [], []
        for head in range(2):
            mine = lane == head
            part = slice(head * HEAD_DIM, (head + 1) * HEAD_DIM)
            row_dot = jnp.sum(jnp.where(mine, weighed, 0.0), -1, keepdims=True)
            d = dot(jnp.where(mine, do, jnp.zeros_like(do)), v, CONTRACT_LAST) - row_dot
            e = e_ref[2 * pair + head]
            ds = (e.astype(F32) * d).astype(BF16)
            dq.append(dot(ds, k))
            dk.append(dot(q_up[part], ds))
            dv.append(dot(do_up[part], e))
        dq_ref[:, at] = (jnp.where(lane == 0, dq[0], dq[1]) * scale).astype(BF16)
        dk_ref[:, at] = (jnp.transpose(jnp.concatenate(dk, 0)) * scale).astype(BF16)
        dv_ref[:, at] = jnp.transpose(jnp.concatenate(dv, 0)).astype(BF16)


def attend_back(arrays, after):
    wide = low(*arrays[1].shape)
    return call(
        attend_back_kernel,
        "attend_back",
        (),
        arrays,
        (wide, wide, wide),
        limit=5.5,
        after=after,
        cost=30.0,
    )


def feed_kernel(count, place, *refs):
    (acts, context, output_weight, output_bias, first_gain, first_shift, inner_weight, inner_bias) = refs[:8]
    outer_weight, outer_bias, second_gain, second_shift = refs[8:12]
    settled_low, hat_ref, inverse_ref, active_ref, slope_ref, hat_two, inverse_two = refs[12:19]
    own_block, far_pair, near_block, acc = refs[19:]
    outs = (own_block, far_pair.at[0], far_pair.at[1], near_block)
    rows, high = active_ref.shape
    hat, inverse = norm_parts(
        acts[...].astype(F32) + dot(context[...], output_weight[...]) + line(output_bias)
    )
    hat_ref[...] = hat.astype(BF16)
    inverse_ref[...] = jnp.broadcast_to(inverse, inverse_ref.shape)
    settled = hat * line(first_gain) + line(first_shift)
    settled_low[...] = settled.astype(BF16)
    acc[...] = settled + line(outer_bias)
    tile = 4 * LANES
    for start in range(0, high, tile):
        part = slice(start, start + tile)
        inner = dot(settled_low[...], inner_weight[:, part]) + line(inner_bias)[:, part]
        active, slope = gate_parts(inner)
        active_ref[:, part] = active.astype(BF16)
        slope_ref[:, part] = slope.astype(BF16)
    acc[...] += dot(active_ref[...], outer_weight[...])
    each = rows // count
    gain, shift = line(second_gain), line(second_shift)
    for i, mask in enumerate(order(count)):
        own = block_rows_of(place, mask, each)
        hat, inverse = norm_parts(acc[own, :])
        outs[i][...] = (hat * gain + shift).astype(BF16)
        hat_two[own, :] = hat
        inverse_two[own, :] = jnp.broadcast_to(inverse, (each, LANES))


def feed(place, acts, context, weights, count):
    rows, width = acts.shape
    high = weights[4].shape[1]
    wide = low(rows, width)
    return call(
        functools.partial(feed_kernel, count),
        "feed",
        (place,),
        (acts, context, *weights),
        (
            wide,
            wide,
            full(rows, LANES),
            low(rows, high),
            low(rows, high),
            full(rows, width),
            full(rows, LANES),
        )
        + (low(rows // count, width), low(2, rows // count, width), low(rows // count, width)),
        limit=7.5,
        scratch=[pltpu.VMEM((rows, width), F32)],
    )


def turn_kernel(count, place, hat_two, inverse_two, second_gain, *refs):
    cotangents = refs[:count]
    branch, sums = refs[count:]
    each = hat_two.shape[0] // count
    gain = line(second_gain)
    totals = [0.0, 0.0, 0.0]
    for i, mask in enumerate(order(count)):
        own = block_rows_of(place, mask, each)
        hat = hat_two[own, :]
        upper = cotangents[i][pl.ds(0, each), :].astype(F32)
        d = norm_back(upper, hat, inverse_two[own, :1], gain)
        d_low = d.astype(BF16)
        branch[own, :] = d_low
        for j, term in enumerate((d_low.astype(F32), upper * hat, upper)):
            totals[j] = totals[j] + jnp.sum(term, 0, keepdims=True)
    for i in range(3):
        sums[i : i + 1, :] = totals[i]


def turn(place, hat_two, inverse_two, second_gain, cotangents):
    rows, width = hat_two.shape
    return call(
        functools.partial(turn_kernel, len(cotangents)),
        "turn",
        (place,),
        (hat_two, inverse_two, second_gain, *cotangents),
        (low(rows, width), full(8, width)),
    )


def feed_back_kernel(
    branch,
    outer_weight,
    slope,
    inner_weight,
    hat_ref,
    inverse_ref,
    first_gain,
    output_weight,
    turn_sums,
    d_inner_ref,
    mixed,
    d_context,
    sums,
    acc,
):
    rows, high = slope.shape
    width = acc.shape[1]
    tile = 4 * LANES
    for start in range(0, high, tile):
        part = slice(start, start + tile)
        d_active = dot(branch[...], outer_weight[part, :], CONTRACT_LAST)
        d_inner = (d_active * slope[:, part].astype(F32)).astype(BF16)
        d_inner_ref[:, part] = d_inner
        partial = jnp.sum(d_inner.astype(F32), 0, keepdims=True)
        for lane in range(start, start + tile, LANES):
            row = 6 + lane // width
            sums[row : row + 1, lane % width : lane % width + LANES] = partial[:, lane - start : lane - start + LANES]
    acc[...] = branch[...].astype(F32) + dot(d_inner_ref[...], inner_weight[...], CONTRACT_LAST)
    parts = 4
    totals = [0.0, 0.0, 0.0]
    gain = line(first_gain)
    for part in range(parts):
        own = slice(part * (rows // parts), (part + 1) * (rows // parts))
        upper = acc[own, :]
        hat = hat_ref[own, :].astype(F32)
        d = norm_back(upper, hat, inverse_ref[own, :1], gain)
        d_low = d.astype(BF16)
        mixed[own, :] = d_low
        for i, term in enumerate((d_low.astype(F32), upper * hat, upper)):
            totals[i] = totals[i] + jnp.sum(term, 0, keepdims=True)
    for i in range(3):
        sums[i : i + 1, :] = totals[i]
    sums[3:6, :] = turn_sums[0:3, :]
    d_context[...] = dot(mixed[...], output_weight[...], CONTRACT_LAST).astype(BF16)


def feed_back(arrays, after):
    rows, width = arrays[0].shape
    high = arrays[2].shape[1]
    wide = low(rows, width)
    return call(
        feed_back_kernel,
        "feed_back",
        (),
        arrays,
        (low(rows, high), wide, wide, full(16, width)),
        scratch=[pltpu.VMEM((rows, width), F32)],
        after=after,
        cost=30.0,
        limit=5,
    )


def entry_back_kernel(count, place, d_first, dq, dk, dv, wq, wk, wv, *refs):
    outs, acc = refs[:count], refs[count]
    each = dq.shape[0] // count
    acc[...] = (
        d_first[...].astype(F32)
        + dot(dq[...], wq[...], CONTRACT_LAST)
        + dot(dk[...], wk[...], CONTRACT_LAST)
        + dot(dv[...], wv[...], CONTRACT_LAST)
    )
    for i, mask in enumerate(order(count)):
        outs[i][...] = acc[block_rows_of(place, mask, each), :].astype(BF16)


def entry_back(place, arrays, count, after):
    rows, width = arrays[1].shape
    return call(
        functools.partial(entry_back_kernel, count),
        "entry_back",
        (place,),
        arrays,
        (low(rows // count, width),) * count,
        scratch=[pltpu.VMEM((rows, width), F32)],
        after=after,
        limit=4,
    )


def add_vectors(place, d_first, dq, dk, dv, weights, early_sums, flagged, sums):
    count = len(flagged)
    each, width = dq.shape[0] // count, dq.shape[1]
    row = lax.broadcasted_iota(jnp.int32, (each, each), 0)
    column = lax.broadcasted_iota(jnp.int32, (each, each), 1)
    zero, one = [0.0] * 4, [0.0] * 4
    for at, mask in enumerate(order(count)):
        own = block_rows_of(place, mask, each)
        flag = flagged[at][pl.ds(each, 16), pl.ds(0, each)][:1].astype(F32)
        upright = jnp.sum(jnp.where(row == column, flag, 0.0), 1, keepdims=True)
        for i, array in enumerate((d_first, dq, dk, dv)):
            value = array[own, :].astype(F32)
            zero[i] = zero[i] + jnp.sum(value * (1.0 - upright), 0, keepdims=True)
            one[i] = one[i] + jnp.sum(value * upright, 0, keepdims=True)
    by_flag = jnp.concatenate([zero[0], one[0]] + [jnp.zeros((6, width), F32)], 0)
    for i, weight in enumerate(weights):
        pair = jnp.concatenate([zero[i + 1], one[i + 1]] + [jnp.zeros((6, width), F32)], 0)
        by_flag = by_flag + dot(pair.astype(BF16), weight[...], CONTRACT_LAST)
    second = jnp.concatenate([by_flag[:2], zero[1] + one[1], zero[3] + one[3]], 0)
    first = early_sums[0:6, :]
    pieces = sums.shape[0]
    piece = width // pieces
    sums[...] = jnp.zeros(sums.shape, F32)
    for i in range(pieces):
        part = slice(i * piece, (i + 1) * piece)
        at, lane = divmod(i * 4 * piece, width)
        sums[i, 0:6, 0:piece] = first[:, part]
        sums[i, 0:4, LANES : LANES + piece] = second[:, part]
        sums[i, 0:1, 2 * LANES : 2 * LANES + 4 * piece] = early_sums[6 + at : 7 + at, lane : lane + 4 * piece]


def vector_pieces_kernel(place, d_first, dq, dk, dv, wq, wk, wv, early_sums, *refs):
    add_vectors(place, d_first, dq, dk, dv, (wq, wk, wv), early_sums, refs[:-1], refs[-1])


def vector_pieces(place, arrays, flagged, pieces):
    return call(
        vector_pieces_kernel,
        "vector_pieces",
        (place,),
        (*arrays, *flagged),
        full(pieces, 8, SIDE // 2),
    )


def parts_of(place):
    x, y = place[2], place[3]
    far, beside, behind, own = 2 * (1 - y) + 1 - x, 2 * y + 1 - x, 2 * (1 - y) + x, 2 * y + x
    return ((far, 0), (beside, 0), (far, 1), (behind, 1), (behind, 0), (beside, 1), (own, 0), (own, 1))


def tall_gradient_kernel(keep, place, left, right, out):
    rows = left.shape[1] // GROUPS // 2
    core = place[1] if keep else 1 - place[1]
    parts = parts_of(place)
    half = SIDE // 2
    for group, homes in ((0, (0, 2)), (1, (1, 5)), (3, (4, 3)), (6, (6, 7))):
        columns = pl.ds(pl.multiple_of((2 * parts[group][0] + core) * rows, LANES), rows)
        product = dot(left[:, columns], right[...], CONTRACT_FIRST).reshape(SHARES, PIECE, SIDE)
        for side, home in enumerate(homes):
            out[home] = product[:, :, side * half : (side + 1) * half].astype(BF16)


def tall_gradient(place, left, right, keep, after=(), cost=2.0):
    return call(
        functools.partial(tall_gradient_kernel, keep),
        "tall_gradient",
        (place,),
        (left, right),
        low(8, SHARES, PIECE, SIDE // 2),
        after=after,
        cost=cost,
    )


def stack_pieces(place, totals, send, keep, start, last=None):
    each = SIDE // (GROUPS * SHARES * 2)
    half = SIDE // 2
    for out, core in ((send, 1 - place[1]), (keep, place[1])):
        for home, (group, side) in enumerate(parts_of(place)):
            columns = slice(side * half, (side + 1) * half)
            for share in range(SHARES):
                index = (2 * group + core) * SHARES + share
                row = pl.multiple_of(index * each, 8)
                pieces = [t[pl.ds(row, each), columns] for t in totals]
                if last is not None:
                    pieces.append(last[index] if side == 0 else jnp.zeros(last.shape[1:], F32))
                piece = jnp.concatenate(pieces, 0)
                out[home, share, start : start + piece.shape[0], :] = piece.astype(BF16)


def wide_gradient_kernel(place, left, right, context, mixed, send, keep, first, second):
    for half in range(2):
        start = 2 * half * SIDE
        first[...] = dot(left[...], right[:, start : start + SIDE], CONTRACT_FIRST)
        second[...] = dot(left[...], right[:, start + SIDE : start + 2 * SIDE], CONTRACT_FIRST)
        stack_pieces(place, (first, second), send, keep, half * PIECE // 2)
    first[...] = dot(context[...], mixed[...], CONTRACT_FIRST)
    stack_pieces(place, (first,), send, keep, PIECE)


def wide_gradient(place, arrays, cost=1.0):
    eight = low(8, SHARES, PIECE + PIECE // 4, SIDE // 2)
    return call(
        wide_gradient_kernel,
        "wide_gradient",
        (place,),
        arrays,
        (eight, eight),
        scratch=[pltpu.VMEM((SIDE, SIDE), F32)] * 2,
        cost=cost,
        limit=6.5,
    )


def square_gradients_kernel(place, acts, d_first, dq, dk, dv, wq, wk, wv, early_sums, *refs):
    flagged, (send, keep, first, second, sums) = refs[:-5], refs[-5:]
    first[...] = dot(acts[...], dq[...], CONTRACT_FIRST)
    second[...] = dot(acts[...], dk[...], CONTRACT_FIRST)
    add_vectors(place, d_first, dq, dk, dv, (wq, wk, wv), early_sums, flagged, sums)
    stack_pieces(place, (first, second), send, keep, 0)
    first[...] = dot(acts[...], dv[...], CONTRACT_FIRST)
    stack_pieces(place, (first,), send, keep, PIECE // 2, sums)


def square_gradients(place, arrays, flagged, pieces, after, cost=0.1):
    eight = low(8, SHARES, 3 * PIECE // 4 + 8, SIDE // 2)
    return call(
        square_gradients_kernel,
        "square_gradients",
        (place,),
        (*arrays, *flagged),
        (eight, eight),
        scratch=[pltpu.VMEM((SIDE, SIDE), F32)] * 2 + [pltpu.VMEM((pieces, 8, SIDE // 2), F32)],
        after=after,
        cost=cost,
        limit=8,
    )


def first_sums_kernel(keep, got, to_x, to_y):
    to_x[...] = total([keep[0:2], got[0:2]]).astype(BF16)
    to_y[...] = total([keep[2:4], got[2:4]]).astype(BF16)


def second_sums_kernel(start, keep, got, from_x, from_y, to_y, to_x):
    to_y[...] = total([keep[start], got[start], from_x[0]]).astype(BF16)
    to_x[...] = total([keep[start + 1], got[start + 1], from_y[0]]).astype(BF16)


def third_sums_kernel(start, place, keep, got, from_x, from_y, then_y, then_x, send, kept):
    half = SIDE // 2
    bit = place[0] & 1
    for out, share_bit in ((send, 1 - bit), (kept, bit)):
        for high in range(SHARES // 2):
            share = 2 * high + share_bit
            a = total([keep[start + 2, share], got[start + 2, share], from_x[1, share], then_y[share]])
            b = total([keep[start + 3, share], got[start + 3, share], from_y[1, share], then_x[share]])
            out[high, :, :half] = a.astype(out.dtype)
            out[high, :, half:] = b.astype(out.dtype)


def fourth_sums_kernel(place, kept, got, send):
    other = 1 - (place[0] >> 1)
    send[...] = total([kept[other], got[other]]).astype(BF16)


def last_sums_kernel(form, place, kept, got, last, *refs):
    count = (len(refs) - 2) // 2
    outs, token, staged, semaphores = refs[:count], refs[count], refs[count + 1 : -1], refs[-1]
    token[...] = jnp.zeros(token.shape, F32)
    mine = place[0] >> 1
    result = total([kept[mine], got[mine], last[...]])
    each = PIECE // 4
    rows = [result[i * each : (i + 1) * each] for i in range(result.shape[0] // each)]
    if form == "tall":
        staged[0][...] = result
    elif form == "wide":
        for i in range(4):
            staged[0][:, i * SIDE : (i + 1) * SIDE] = rows[i]
        staged[1][...] = rows[4]
    else:
        for i in range(3):
            staged[i][...] = rows[i]
        vectors = result[3 * each :]
        staged[3][...] = vectors[0:2, LANES : LANES + each]
        staged[4][...] = vectors[0, 2 * LANES : 2 * LANES + 4 * each]
        for i in range(8):
            row, lane = (i, 0) if i < 6 else (i - 4, LANES)
            staged[5 + i][...] = vectors[row, lane : lane + each]
    for copy in fetch(staged, outs, semaphores):
        copy.wait()


class Halving:
    def __init__(self, place, send, keep):
        self.place, self.keep = place, keep
        self.got = [swap_pairs(part, "batch", 1) for part in send]
        self.late = 0 if len(keep) > 1 else 4

    def step(self, kernel, name, scalars, arrays, outs, after, cost=0.5):
        results = call(kernel, name, scalars, arrays, outs, after=after, cost=cost)
        self.done = results[:1]
        return results

    def first(self, after=(), cost=0.5):
        half = low(2, *self.keep[0].shape[1:])
        arrays = (self.keep[0], self.got[0])
        to = self.step(first_sums_kernel, "first_sums", (), arrays, (half, half), after, cost)
        self.from_x, self.from_y = swap_pairs(to[0], "batch", 2), swap_pairs(to[1], "batch", 4)

    def second(self, after=(), cost=0.5):
        quarter = low(*self.keep[0].shape[1:])
        arrays = (self.keep[-1], self.got[-1], self.from_x, self.from_y)
        kernel = functools.partial(second_sums_kernel, self.late)
        to = self.step(kernel, "second_sums", (), arrays, (quarter, quarter), after, cost)
        self.then_y, self.then_x = swap_pairs(to[0], "batch", 4), swap_pairs(to[1], "batch", 2)

    def third(self, after=(), cost=0.5):
        shape = (SHARES // 2, self.keep[0].shape[2], SIDE)
        arrays = (self.keep[-1], self.got[-1], self.from_x, self.from_y, self.then_y, self.then_x)
        outs = (low(*shape), full(*shape))
        kernel = functools.partial(third_sums_kernel, self.late)
        to, self.kept = self.step(kernel, "third_sums", (self.place,), arrays, outs, after, cost)
        self.pair = swap_pairs(to, "seq", 1)

    def fourth(self, after=(), cost=0.5):
        arrays = (self.kept, self.pair)
        outs = (low(*self.kept.shape[1:]),)
        (to,) = self.step(fourth_sums_kernel, "fourth_sums", (self.place,), arrays, outs, after, cost)
        self.others = swap_pairs(to, "seq", 2)

    def last(self, form, after=()):
        each = PIECE // 4
        shapes = {
            "tall": [(PIECE, SIDE)],
            "wide": [(each, 4 * SIDE), (each, SIDE)],
            "square": [(each, SIDE)] * 3 + [(2, each), (4 * each,)] + [(each,)] * 8,
        }[form]
        *self.result, token = call(
            functools.partial(last_sums_kernel, form),
            "last_sums",
            (self.place,),
            (self.kept, self.pair, self.others),
            tuple(full(*shape) for shape in shapes),
            scratch=[pltpu.VMEM(shape, F32) for shape in shapes] + [pltpu.SemaphoreType.DMA((len(shapes),))],
            after=after,
            cost=0.5,
            out_far=True,
        )
        self.done = (token,)


def add_pieces(pieces):
    batch, seq = lax.axis_size("batch"), lax.axis_size("seq")
    parts = [pieces.reshape((2,) * ((batch * seq).bit_length() - 1) + pieces.shape[1:])]
    for axis in ("batch", "seq"):
        bits = lax.axis_size(axis).bit_length() - 1
        for bit in range(bits):
            parts = [total(halve(parts, bits - 1 - bit, axis, bit, F32))]
    return parts[0]


def per_device(
    hidden,
    groups,
    answer_flags,
    lengths,
    answer_embed,
    query_weight,
    query_bias,
    key_weight,
    value_weight,
    value_bias,
    output_weight,
    output_bias,
    first_gain,
    first_shift,
    inner_weight,
    inner_bias,
    outer_weight,
    outer_bias,
    second_gain,
    second_shift,
    cotangent,
):
    items, block_rows, width = hidden.shape
    batch, seq = lax.axis_size("batch"), lax.axis_size("seq")
    me, group = lax.axis_index("seq"), lax.axis_index("batch")
    place = jnp.stack([me, group & 1, (group >> 1) & 1, (group >> 2) & 1]).astype(jnp.int32)
    high = inner_weight.shape[1]
    even = (batch, seq, width, high) == (8, SHARES, SIDE, 4 * SIDE)

    arrays = (hidden, answer_flags, answer_embed)
    masks = order(items)
    far_blocks = entry_blocks(place, masks[1:-1], arrays)
    near_blocks = entry_blocks(place, (masks[0], masks[-1]), arrays, far_blocks[:1])
    got = exchange([near_blocks[0], *far_blocks, near_blocks[1]])
    output_near, inner_near, outer_near = load((output_weight, inner_weight, outer_weight), near_blocks[:1])
    upper = exchange(flagged_blocks(place, cotangent, answer_flags, (*got[1:-1], output_near)))
    acts, queries, keys, values, context, exponents, inverse_sums = attend(
        place,
        lengths,
        groups,
        got,
        (query_weight, query_bias, key_weight, value_weight, value_bias),
        (),
    )
    settled, hat, inverse, active, slope, hat_two, inverse_two, *output = feed(
        place,
        acts,
        context,
        (
            output_near,
            output_bias,
            first_gain,
            first_shift,
            inner_near,
            inner_bias,
            outer_near,
            outer_bias,
            second_gain,
            second_shift,
        ),
        items,
    )
    branch, sums = turn(place, hat_two, inverse_two, second_gain, upper)
    if even:
        send = tall_gradient(place, active, branch, False)
        keep = tall_gradient(place, active, branch, True, (send,))
        outer = Halving(place, (send,), (keep,))
        outer.first()
        after = outer.done
    else:
        outer_weight_gradient = scatter(dot(active, branch, CONTRACT_FIRST))
        after = ()
    output_own, output_far, output_near_block = output
    output_got = swap_pairs(output_far, "seq", 2)
    d_inner, mixed, d_context, sums = feed_back(
        (
            branch,
            outer_near,
            slope,
            inner_near,
            hat,
            inverse,
            first_gain,
            output_near,
            sums,
        ),
        after,
    )
    if even:
        send, keep = wide_gradient(place, (settled, d_inner, context, mixed))
        inner = Halving(place, (send,), (keep,))
        outer.second((send,))
        after = (*outer.done, output_got)
    else:
        inner_weight_gradient = scatter(dot(settled, d_inner, CONTRACT_FIRST))
    weights = (query_weight, key_weight, value_weight)
    d_queries, d_keys, d_values = attend_back(
        (exponents, queries, keys, values, context, inverse_sums, d_context),
        after,
    )
    if even:
        inner.first((d_queries,))
        outer.third(inner.done)
        after = outer.done
    input_gradient = entry_back(
        place, (mixed, d_queries, d_keys, d_values, *weights), items, after
    )
    back = exchange(input_gradient)
    if even:
        send, keep = square_gradients(
            place,
            (acts, mixed, d_queries, d_keys, d_values, *weights, sums),
            upper,
            batch * seq,
            input_gradient[:1],
        )
        narrow = Halving(place, (send,), (keep,))
        relayed = relay(output_near_block, output_got, (send,))
        near_got = swap_pairs(relayed, "seq", 1)
        outer.fourth((relayed, back[1]))
        inner.second(outer.done, cost=25.0)
        narrow.first((*inner.done, outer.others))
        output, token = join_pairs(place, output_own, output_got, near_got, narrow.done)
        inner.third((token,))
        outer.last("tall", inner.done)
        narrow.second((*outer.done, back[2]))
        inner.fourth(narrow.done)
        narrow.third((*inner.done, back[3]))
        narrow.fourth(narrow.done)
        inner.last("wide", narrow.done)
        input_gradient, token = join_blocks(place, back, inner.done)
        narrow.last("square", (token,))
        (outer_weight_gradient,), (inner_weight_gradient, output_weight_gradient) = outer.result, inner.result
        vectors = narrow.result[5:]
        *narrow, embed_gradient, inner_bias_gradient = narrow.result[:5]
    else:
        squares = jnp.concatenate(
            [
                dot(left, right, CONTRACT_FIRST).astype(BF16)
                for left, right in (
                    (context, mixed),
                    (acts, d_queries),
                    (acts, d_keys),
                    (acts, d_values),
                )
            ],
            1,
        )
        output_weight_gradient, *narrow = jnp.split(scatter(squares), 4, 1)
        pieces = add_pieces(
            vector_pieces(
                place, (mixed, d_queries, d_keys, d_values, *weights, sums), upper, batch * seq
            )
        )
        early, later = pieces[:, : width // (batch * seq)], pieces[:, LANES : LANES + width // (batch * seq)]
        embed_gradient, inner_bias_gradient = later[0:2], pieces[0, 2 * LANES : 2 * LANES + high // (batch * seq)]
        vectors = [early[i] for i in range(6)] + [later[2], later[3]]
        near_got = swap_pairs(relay(output_near_block, output_got, ()), "seq", 1)
        output, _ = join_pairs(place, output_own, output_got, near_got, ())
        input_gradient, _ = join_blocks(place, back)
    query_weight_gradient, key_weight_gradient, value_weight_gradient = narrow
    return (
        output,
        input_gradient,
        embed_gradient,
        query_weight_gradient,
        vectors[6],
        key_weight_gradient,
        value_weight_gradient,
        vectors[7],
        output_weight_gradient,
        vectors[0],
        vectors[1],
        vectors[2],
        inner_weight_gradient,
        inner_bias_gradient,
        outer_weight_gradient,
        vectors[3],
        vectors[4],
        vectors[5],
    )


def solution(mesh):
    both = ("batch", "seq")
    in_specs = (
        (P("batch", "seq", None), P("batch", None), P("batch", "seq"), P("batch"))
        + (P(),) * 16
        + (P("batch", "seq", None),)
    )
    matrix, vector = P(both, None), P(both)
    out_specs = (
        P("batch", "seq", None),
        P("batch", "seq", None),
        P(None, both),
        matrix,
        vector,
        matrix,
        matrix,
        vector,
        matrix,
        vector,
        vector,
        vector,
        matrix,
        vector,
        matrix,
        vector,
        vector,
        vector,
    )
    return jax.shard_map(
        per_device, mesh=mesh, in_specs=in_specs, out_specs=out_specs, check_vma=False
    )
```
